128 devices in a mesh: fsdp: 128 (over x, y, z, core).
Axes of the slice: x: 4, y: 4, z: 4, core: 2. Of those that a mesh axis runs over, the one named last changes fastest.
Arguments:
- hidden_in: bfloat16 [16384, 576], P('fsdp'), may hold values from -6 to 6
- segment_ids: int32 [16384], P('fsdp'), may hold values from 0 to 16383, as said below
- weights_flat: bfloat16 [2, 3540096], P(None, 'fsdp'), may hold values from -2 to 2, as said below
- cotangent: bfloat16 [16384, 576], P('fsdp'), may hold values from -6 to 6
Outputs:
- layer_out: bfloat16 [16384, 576], P('fsdp')
- grad_input: float32 [16384, 576], P('fsdp')
- grad_weights: float32 [2, 3540096], P(None, 'fsdp')
The draws below stay inside these ranges and needn't reach their ends.
Inputs may be any that keep to these rules, and one draw needn't show every extreme that they name: segment_ids[t] is the index of the first token of t's document; ids never fall; every document holds 1 to 1024 tokens and one holds exactly 1024. `weights_flat`: gain entries lie in 0.7 to 1.3.
All inputs are finite; a program needn't handle non-finite values.
Results may differ from the reference program's by a relative error of at most 0.025.
Values may be sent and summed in bfloat16 or wider, within the bound.
No kernel may reach another device: no remote copies, remote signals or barrier semaphores. Data moves between devices by JAX's collectives and lax.ppermute only.
A program may use at most 192 MiB of HBM per device.

```python
import math
import jax
import jax.numpy as jnp
from jax import lax

D = 576
FF = 1536
QH = 9
KVH = 3
HD = 64
LAYERS = 2
MAXLEN = 1024
TOK_DEV = 128
TOKENS = 16384
WINDOW = 8
PARAMS = 3540096


def draw_segment_ids(key, part):
    key = jax.random.fold_in(key, 7)
    key_ticks, key_place = jax.random.split(key)
    period = max(MAXLEN // 3, 2)
    ticks = jax.random.randint(key_ticks, (TOKENS,), 0, period)
    index = jnp.arange(TOKENS, dtype=jnp.int32)
    marks = jnp.where(ticks == 0, index, 0)
    starts = lax.cummax(marks, axis=0)
    starts = starts + (index - starts) // MAXLEN * MAXLEN
    device_count = TOKENS // TOK_DEV
    span = (MAXLEN + TOK_DEV - 1) // TOK_DEV + 1
    chosen = jax.random.randint(key_place, (), 0, device_count - span + 1)
    first = chosen * TOK_DEV + TOK_DEV - 1
    last = first + MAXLEN
    inside = (index >= first) & (index < last)
    after = index >= last
    starts = jnp.where(inside, first, jnp.where(after, jnp.maximum(starts, last), starts))
    return starts.astype(jnp.int32)


def draw_weights_flat(key, part):
    key = jax.random.fold_in(key, 11)
    key_normal, key_uniform = jax.random.split(key)
    qkv_width = (QH + 2 * KVH) * HD
    pieces = [(D, 0.0, 1.0), (D * qkv_width, 1.2 / math.sqrt(D), 0.0), (QH * HD * D, 3.0 / math.sqrt(QH * HD), 0.0), (D, 0.0, 1.0), (2 * D * FF, 1.0 / math.sqrt(D), 0.0), (FF * D, 2.0 / math.sqrt(FF), 0.0)]
    scale_row = jnp.concatenate([jnp.full((piece_size,), piece_scale, jnp.float32) for piece_size, piece_scale, piece_gain in pieces])
    marker = jnp.concatenate([jnp.full((piece_size,), piece_gain, jnp.float32) for piece_size, piece_scale, piece_gain in pieces])
    normal_part = jax.random.normal(key_normal, (LAYERS, PARAMS), jnp.float32)
    uniform_part = jax.random.uniform(key_uniform, (LAYERS, PARAMS), jnp.float32, -1.0, 1.0)
    return (normal_part * scale_row + marker * (1.0 + 0.3 * uniform_part)).astype(jnp.bfloat16)


def levels(rng, shape, cuts, least, high):
    level = 1.0
    for axis_at, shards_of in cuts:
        draws = jax.random.uniform(jax.random.fold_in(jax.random.fold_in(rng, 6), axis_at), (shards_of,), jnp.float32, least / len(cuts), high / len(cuts))
        level = level * jnp.repeat(jnp.exp(draws), shape[axis_at] // shards_of).reshape((-1,) + (1,) * (len(shape) - 1 - axis_at))
    return level


def gaussian(rng, dims, spread, most, cuts=(), held_as=jnp.bfloat16):
    level = levels(rng, dims, cuts, -0.22, 0.18) if cuts else 1.0
    values = jax.random.normal(rng, dims, jnp.float32) * spread * level
    return jnp.minimum(jnp.maximum(values, -most), most).astype(held_as)


def setup_inputs(seed: int = 0) -> dict:
    splits = jax.random.split(jax.random.key(seed), 5)
    return {
        "hidden_in": gaussian(splits[0], (TOKENS, D), 1.0, 6.0, ((0, 128),)),
        "segment_ids": draw_segment_ids(jax.random.fold_in(splits[4], 71), 0),
        "weights_flat": draw_weights_flat(jax.random.fold_in(splits[4], 71), 0),
        "cotangent": gaussian(splits[3], (TOKENS, D), 1.0, 6.0, ((0, 128),)),
    }


@jax.custom_vjp
def low(v):
    return lax.optimization_barrier(v.astype(jnp.bfloat16)).astype(jnp.float32)

@jax.custom_vjp
def low_back(v):
    return v

def low_keep(v):
    return (low(v), None)

def low_pass(kept, grad):
    return (grad,)

def back_keep(v):
    return (v, None)

def back_low(kept, grad):
    return (low(grad),)
low.defvjp(low_keep, low_pass)
low_back.defvjp(back_keep, back_low)
epsilon = 1e-05
rope_base = 10000.0
highest = lax.Precision.HIGHEST

def rotate_half(values):
    half_size = values.shape[-1] // 2
    return jnp.concatenate([-values[..., half_size:], values[..., :half_size]], axis=-1)

def rope_tables(positions, head_size):
    half_size = head_size // 2
    frequency = rope_base ** (-jnp.arange(half_size, dtype=jnp.float32) / half_size)
    angles = positions.astype(jnp.float32)[:, None] * frequency[None, :]
    angles = jnp.concatenate([angles, angles], axis=-1)
    return (jnp.cos(angles), jnp.sin(angles))

def apply_rope(values, cosine, sine):
    return values * cosine[:, None, :] + rotate_half(values) * sine[:, None, :]

def unpack(flat):
    qkv_width = (QH + 2 * KVH) * HD
    sizes_list = [D, D * qkv_width, QH * HD * D, D, 2 * D * FF, FF * D]
    shapes_list = [(D,), (D, qkv_width), (QH * HD, D), (D,), (D, 2 * FF), (FF, D)]
    pieces = []
    offset = 0
    for piece_size, piece_shape in zip(sizes_list, shapes_list):
        pieces.append(flat[offset:offset + piece_size].reshape(piece_shape))
        offset = offset + piece_size
    return pieces

def normalize(values, gain):
    inverse = lax.rsqrt(lax.optimization_barrier(jnp.mean(values * values, axis=-1, keepdims=True)) + epsilon)
    return values * inverse * gain

def attend_block(keys_pad, values_pad, block_index, query, segment):
    window_rows = (WINDOW + 1) * TOK_DEV
    start = (block_index * TOK_DEV).astype(jnp.int32)
    keys = lax.dynamic_slice_in_dim(keys_pad, start, window_rows, 0)
    values = lax.dynamic_slice_in_dim(values_pad, start, window_rows, 0)
    row_count = query.shape[0]
    grouped = query.reshape(row_count, KVH, QH // KVH, HD)
    scores = low_back(jnp.einsum('qkgd,tkd->kgqt', grouped, keys, precision=highest) * HD ** (-0.5))
    key_global = start - WINDOW * TOK_DEV + jnp.arange(window_rows, dtype=jnp.int32)
    query_global = start + jnp.arange(row_count, dtype=jnp.int32)
    allowed = (key_global[None, :] >= segment[:, None]) & (key_global[None, :] <= query_global[:, None])
    scores = jnp.where(allowed, scores, -1e+30)
    peak = lax.optimization_barrier(jnp.max(scores, axis=-1, keepdims=True))
    log_total = peak + jnp.log(lax.optimization_barrier(jnp.sum(jnp.exp(scores - peak), axis=-1, keepdims=True)))
    weights = low(jnp.exp(scores - log_total))
    mixed = jnp.einsum('kgqt,tkd->qkgd', weights, values, precision=highest)
    return mixed.reshape(row_count, QH * HD)

def layer(hidden, flat, segments, cosine, sine):
    gain_one, w_qkv, w_out, gain_two, w_in, w_down = unpack(flat)
    query_width = QH * HD
    kv_width = KVH * HD
    normed = low(normalize(hidden, gain_one))
    project = low_back(jnp.dot(normed, w_qkv, precision=highest))
    query = low(apply_rope(project[:, :query_width].reshape(-1, QH, HD), cosine, sine))
    keys = low(apply_rope(project[:, query_width:query_width + kv_width].reshape(-1, KVH, HD), cosine, sine))
    values = low(project[:, query_width + kv_width:].reshape(-1, KVH, HD))
    padding = jnp.zeros((WINDOW * TOK_DEV, KVH, HD), jnp.float32)
    keys_pad = jnp.concatenate([padding, keys], axis=0)
    values_pad = jnp.concatenate([padding, values], axis=0)
    blocks = TOKENS // TOK_DEV
    attend = jax.checkpoint(attend_block)
    mixed = lax.map(lambda items: attend(keys_pad, values_pad, items[0], items[1], items[2]), (jnp.arange(blocks, dtype=jnp.int32), query.reshape(blocks, TOK_DEV, QH, HD), segments.reshape(blocks, TOK_DEV)))
    mixed = low(low_back(mixed.reshape(TOKENS, query_width)))
    middle = hidden + low_back(jnp.dot(mixed, w_out, precision=highest))
    normed_two = low(normalize(middle, gain_two))
    gate_up = low_back(jnp.dot(normed_two, w_in, precision=highest))
    gate_part = gate_up[:, :FF]
    up_part = gate_up[:, FF:]
    hidden_units = low(gate_part * jax.nn.sigmoid(gate_part) * up_part)
    return middle + low_back(jnp.dot(hidden_units, w_down, precision=highest))

def reference(hidden_in, segment_ids, weights_flat, cotangent):
    hidden = hidden_in.astype(jnp.float32)
    flat_all = weights_flat.astype(jnp.float32)
    positions = jnp.arange(TOKENS, dtype=jnp.int32) - segment_ids
    cosine, sine = rope_tables(positions, HD)

    def forward(residual, params):
        for layer_index in range(LAYERS):
            residual = layer(residual, params[layer_index], segment_ids, cosine, sine)
        return residual
    result, pullback = jax.vjp(forward, hidden, flat_all)
    grad_hidden, grad_flat = pullback(cotangent.astype(jnp.float32))
    return (result.astype(jnp.bfloat16), grad_hidden, grad_flat)
```

```python
import functools

import jax
import jax.numpy as jnp
from jax import lax
from jax.experimental import pallas as pl
from jax.experimental.pallas import tpu as pltpu
from jax.sharding import PartitionSpec as P

D = 576
FF = 1536
QH = 9
KVH = 3
HD = 64
MAXLEN = 1024
QW = QH * HD
KW = KVH * HD
PW = QW + 2 * KW
GROUP = QH // KVH
DEVICES = 128
ROWS = 128
PARAMS = 3540096
SHARD = PARAMS // DEVICES
CHUNK = 224
FLAT_ROWS = 27904
SAME_CORE = 4
WIN_S = (SAME_CORE + 1) * ROWS
WIN_T = SAME_CORE * ROWS
WIN = WIN_S + WIN_T

bf16 = jnp.bfloat16
f32 = jnp.float32
epsilon = 1e-05
rope_base = 10000.0
FACTOR = HD ** (-0.5)
VMEM_LIMIT = 60 * 1024 * 1024

HALF_GAIN_ONE = 0
HALF_QKV = D // 64
HALF_OUT = HALF_QKV + D * PW // 64
HALF_GAIN_TWO = HALF_OUT + QW * D // 64
HALF_IN = HALF_GAIN_TWO + D // 64
HALF_DOWN = HALF_IN + D * 2 * FF // 64


def mm(a, b):
    return lax.dot_general(a, b, (((1,), (0,)), ((), ())), preferred_element_type=f32)


def mm_t(a, b):
    return lax.dot_general(a, b, (((1,), (1,)), ((), ())), preferred_element_type=f32)


def t_mm(a, b):
    return lax.dot_general(a, b, (((0,), (0,)), ((), ())), preferred_element_type=f32)


def call(kernel, out_shape, args, scratch=(), smem=0, flops=0, nbytes=0):
    in_specs = [
        pl.BlockSpec(memory_space=pltpu.SMEM if at < smem else pltpu.VMEM)
        for at in range(len(args))
    ]
    return pl.pallas_call(
        kernel,
        out_shape=[jax.ShapeDtypeStruct(s, d) for s, d in out_shape],
        in_specs=in_specs,
        out_specs=[pl.BlockSpec(memory_space=pltpu.VMEM) for _ in out_shape],
        scratch_shapes=list(scratch),
        compiler_params=pltpu.CompilerParams(vmem_limit_bytes=VMEM_LIMIT),
        cost_estimate=pl.CostEstimate(flops=flops, bytes_accessed=nbytes, transcendentals=0),
    )(*args)


def low_half(shape):
    return lax.broadcasted_iota(jnp.int32, shape, 1) < 64


def take_rows(flat, start_half, pairs, width_half, store):
    tiles = (width_half + 1) // 2
    if start_half % 2 == 0:
        for t in range(tiles):
            store(t, flat[pl.ds(start_half // 2 + t, pairs, stride=width_half), :])
    else:
        before = None
        for t in range(tiles + 1):
            if t == tiles and width_half % 2 == 1:
                store(t - 1, before)
                break
            now = pltpu.roll(flat[pl.ds(start_half // 2 + t, pairs, stride=width_half), :], 64, 1)
            if before is not None:
                store(t - 1, jnp.where(low_half(now.shape), before, now))
            before = now


def put_rows(flat, start_half, pairs, width_half, load):
    tiles = (width_half + 1) // 2
    if start_half % 2 == 0:
        for t in range(tiles):
            place = pl.ds(start_half // 2 + t, pairs, stride=width_half)
            value = load(t)
            if 2 * t + 1 == width_half:
                value = jnp.where(low_half(value.shape), value, flat[place, :])
            flat[place, :] = value
    else:
        before = None
        for t in range(tiles + 1):
            if t == tiles and width_half % 2 == 1:
                break
            place = pl.ds(start_half // 2 + t, pairs, stride=width_half)
            now = pltpu.roll(load(t), 64, 1) if t < tiles else None
            if before is None:
                value = jnp.where(low_half(now.shape), flat[place, :], now)
            else:
                value = jnp.where(low_half(before.shape), before, now)
            flat[place, :] = value
            before = now


def unpack_kernel(gathered, w_qkv, w_out, w_in, w_down, gains, flat, tile):
    flat[0:8, :] = jnp.zeros((8, 128), f32)
    lane = lax.broadcasted_iota(jnp.int32, (CHUNK, 128), 1)
    first_two = lax.broadcasted_iota(jnp.int32, (8, 128), 0) < 2

    def one_shard(d, carry):
        shift = lax.rem(d * 9, 128)
        base = d * 216 + lax.div(d * 9, 128)
        rows = gathered[pl.ds(pl.multiple_of(d * CHUNK, CHUNK), CHUNK), :].astype(f32)
        turned = pltpu.roll(rows, shift, 1)
        behind = pltpu.roll(turned, 1, 0)
        value = jnp.where(lane >= shift, turned, behind)
        shared = jnp.where(first_two, flat[pl.ds(base, 8), :], 0.0)
        flat[pl.ds(base, 8), :] = shared + value[0:8, :]
        flat[pl.ds(base + 8, CHUNK - 8), :] = value[8:, :]
        return carry

    lax.fori_loop(0, DEVICES, one_shard, 0)

    def matrix(out, start_half, width_half):
        rows, columns = out.shape

        def store(parity, at, value):
            tile[at, pl.ds(parity, rows // 2, stride=2), :] = value

        for parity in range(2):
            take_rows(
                flat, start_half + parity * width_half, rows // 2, width_half,
                functools.partial(store, parity),
            )
        for t in range((width_half + 1) // 2):
            wide = min(128, columns - 128 * t)
            out[:, 128 * t : 128 * t + wide] = tile[t, 0:rows, 0:wide].astype(bf16)

    matrix(w_qkv, HALF_QKV, PW // 64)
    matrix(w_out, HALF_OUT, D // 64)
    matrix(w_down, HALF_DOWN, D // 64)

    def in_tile(c, carry):
        w_in[:, pl.ds(pl.multiple_of(c * 128, 128), 128)] = flat[
            pl.ds(HALF_IN // 2 + c, D, stride=24), :
        ].astype(bf16)
        return carry

    lax.fori_loop(0, 24, in_tile, 0)

    for at, start in ((0, HALF_GAIN_ONE), (1, HALF_GAIN_TWO)):
        first = start // 2
        for t in range(5):
            if start % 2 == 0:
                value = flat[first + t : first + t + 1, :]
            else:
                here = pltpu.roll(flat[first + t : first + t + 1, :], 64, 1)
                after = pltpu.roll(flat[first + t + 1 : first + t + 2, :], 64, 1)
                value = jnp.where(low_half((1, 128)), here, after)
            gains[at : at + 1, 128 * t : 128 * t + 128] = value


def unpack(gathered):
    return call(
        unpack_kernel,
        [((D, PW), bf16), ((QW, D), bf16), ((D, 2 * FF), bf16), ((FF, D), bf16), ((8, 640), f32)],
        [gathered],
        scratch=[pltpu.VMEM((FLAT_ROWS, 128), f32), pltpu.VMEM((8, FF, 128), f32)],
        flops=200_000_000, nbytes=30_000_000,
    )


def turn(value, cosine, sine):
    lane = lax.broadcasted_iota(jnp.int32, (value.shape[0], 128), 1)
    first = lax.rem(lane, 64) < 32
    pieces = []
    for t in range(value.shape[1] // 128):
        part = value[:, 128 * t : 128 * t + 128]
        swapped = jnp.where(first, -pltpu.roll(part, 96, 1), pltpu.roll(part, 32, 1))
        pieces.append(part * cosine + swapped * sine)
    return jnp.concatenate(pieces, axis=1)


def inverse_norm(values):
    return lax.rsqrt(jnp.mean(values * values, axis=-1, keepdims=True) + epsilon)


def heads_zero_kernel(window, cosine, sine, gains, w_qkv, q_out, kv_s, kv_t, normed_out):
    gain = gains[0:1, 0:D]
    for begin, rows in ((0, 384), (384, 384), (768, 384)):
        x = window[begin : begin + rows, :].astype(f32)
        normed = (x * inverse_norm(x) * gain).astype(bf16)
        project = mm(normed, w_qkv[:, 512:PW])
        both = turn(project[:, 0:256], cosine[begin : begin + rows, :], sine[begin : begin + rows, :])
        kv = jnp.concatenate([both[:, 64:256], project[:, 256:448]], axis=1).astype(bf16)
        for r in range(0, rows, 128):
            at = begin + r
            if at < WIN_S:
                kv_s[at : at + 128, :] = kv[r : r + 128, :]
            else:
                kv_t[at - WIN_S : at - WIN_S + 128, :] = kv[r : r + 128, :]
    own = SAME_CORE * ROWS
    x = window[own : own + ROWS, :].astype(f32)
    normed = (x * inverse_norm(x) * gain).astype(bf16)
    normed_out[...] = normed
    project = mm(normed, w_qkv[:, 0:640])
    q_out[...] = turn(project, cosine[own : own + ROWS, :], sine[own : own + ROWS, :])[
        :, 0:QW
    ].astype(bf16)


def heads_kernel(x_in, cosine, sine, gains, w_qkv, q_out, kv_out, normed_out):
    x = x_in[...]
    normed = (x * inverse_norm(x) * gains[0:1, 0:D]).astype(bf16)
    normed_out[...] = normed
    project = mm(normed, w_qkv[...])
    both = turn(project[:, 0:768], cosine[...], sine[...])
    q_out[...] = both[:, 0:QW].astype(bf16)
    kv_out[...] = jnp.concatenate([both[:, QW:768], project[:, 768:PW]], axis=1).astype(bf16)


def allowed_of(segment, key_row, first_row):
    query = first_row + lax.broadcasted_iota(jnp.int32, (ROWS, 1), 0)
    return (key_row >= segment) & (key_row <= query)


def group_rows(value, group):
    return jnp.concatenate(
        [value[:, (GROUP * group + n) * HD : (GROUP * group + n + 1) * HD] for n in range(GROUP)],
        axis=0,
    )


def window_rows(kv_s, kv_t, begin):
    return jnp.concatenate(
        [kv_s[:, begin : begin + HD], kv_t[:, begin : begin + HD]], axis=0
    )


def attend_kernel(
    first, x_in, q_in, kv_s, kv_t, segment, key_row, gains, w_out, w_in, w_down,
    x_out, mixed_out, lse_out, middle_out, normed_out, gate_up_out, hidden_out,
):
    allowed = allowed_of(segment[...], key_row[...], first[0])
    bias = jnp.where(allowed, 0.0, -1e30).astype(f32)
    bias = jnp.concatenate([bias] * GROUP, axis=0)
    q = q_in[...]
    pieces = []
    for group in range(KVH):
        keys = window_rows(kv_s, kv_t, group * HD)
        values = window_rows(kv_s, kv_t, KW + group * HD)
        scores = mm_t(group_rows(q, group), keys) * FACTOR + bias
        peak = jnp.max(scores, axis=-1, keepdims=True)
        powers = jnp.exp(scores - peak)
        total = jnp.sum(powers, axis=-1, keepdims=True)
        lse_out[:, group : group + 1] = peak + jnp.log(total)
        weights = (powers * (1.0 / total)).astype(bf16)
        mixed = mm(weights, values)
        for n in range(GROUP):
            pieces.append(mixed[n * ROWS : (n + 1) * ROWS, :])
    mixed = jnp.concatenate(pieces, axis=1).astype(bf16)
    mixed_out[...] = mixed
    middle = x_in[...].astype(f32) + mm(mixed, w_out[...])
    middle_out[...] = middle
    normed = (middle * inverse_norm(middle) * gains[1:2, 0:D]).astype(bf16)
    normed_out[...] = normed
    gate_up = mm(normed, w_in[...])
    gate_up_out[...] = gate_up
    gate = gate_up[:, 0:FF]
    hidden = (gate * jax.nn.sigmoid(gate) * gate_up[:, FF:]).astype(bf16)
    hidden_out[...] = hidden
    x_out[...] = middle + mm(hidden, w_down[...])


def norm_back(values, inverse, gain, grad):
    weighted = grad * gain
    return inverse * weighted - values * inverse**3 * jnp.mean(
        weighted * values, axis=-1, keepdims=True
    )


def back_kernel(
    first, g_in, q_in, kv_s, kv_t, segment, key_row, cosine, sine, gains, w_out, w_in, w_down,
    lse, middle_in, gate_up,
    branch_out, grad_gu_out, attn_out, middle_grad_out, dq_out, dkv_s, dkv_t, gain_out,
):
    g = g_in[...].astype(f32)
    branch = g.astype(bf16)
    branch_out[...] = branch
    grad_hidden = mm_t(branch, w_down[...])
    gate = gate_up[:, 0:FF]
    up = gate_up[:, FF:]
    sigma = jax.nn.sigmoid(gate)
    grad_gu_out[:, 0:FF] = (
        grad_hidden * up * sigma * (1.0 + gate * (1.0 - sigma))
    ).astype(bf16)
    grad_gu_out[:, FF:] = (grad_hidden * gate * sigma).astype(bf16)
    grad_two = mm_t(grad_gu_out[...], w_in[...])
    middle = middle_in[...]
    inverse = inverse_norm(middle)
    gain_out[...] = jnp.sum(grad_two * middle * inverse, axis=0, keepdims=True)
    grad_middle = g + norm_back(middle, inverse, gains[1:2, 0:D], grad_two)
    middle_grad_out[...] = grad_middle
    attn = grad_middle.astype(bf16)
    attn_out[...] = attn
    grad_mixed = mm_t(attn, w_out[...]).astype(bf16)

    allowed = allowed_of(segment[...], key_row[...], first[0])
    bias = jnp.where(allowed, 0.0, -1e30).astype(f32)
    bias = jnp.concatenate([bias] * GROUP, axis=0)
    q = q_in[...]
    dq, dk, dv = [], [], []
    for group in range(KVH):
        keys = window_rows(kv_s, kv_t, group * HD)
        values = window_rows(kv_s, kv_t, KW + group * HD)
        query = group_rows(q, group)
        grad = group_rows(grad_mixed, group)
        scores = mm_t(query, keys) * FACTOR + bias
        probs = jnp.exp(scores - lse[:, group : group + 1])
        grad_w = mm_t(grad, values)
        delta = jnp.sum(probs * grad_w, axis=-1, keepdims=True)
        grad_scores = (probs * (grad_w - delta)).astype(bf16)
        part = mm(grad_scores, keys) * FACTOR
        for n in range(GROUP):
            dq.append(part[n * ROWS : (n + 1) * ROWS, :])
        dk.append(t_mm(grad_scores, query) * FACTOR)
        dv.append(t_mm(probs.astype(bf16), grad))
    dkv = jnp.concatenate(dk + dv, axis=1)
    dkv_s[...] = dkv[0:WIN_S, :]
    dkv_t[...] = dkv[WIN_S:, :].astype(bf16)
    wide = jnp.concatenate(dq + [jnp.zeros((ROWS, HD), f32)], axis=1)
    dq_out[...] = turn(wide, cosine[...], -sine[...])[:, 0:QW].astype(bf16)


def back_heads_kernel(
    x_in, dq, own, r8, r6, r4, r2, cosine, sine, gains, w_qkv, middle_grad,
    g_out, project_out, gain_out,
):
    total = own[...]
    for piece in (r8, r6, r4, r2):
        total = total + piece[...].astype(f32)
    keys = jnp.concatenate([total[:, 0:KW], jnp.zeros((ROWS, HD), f32)], axis=1)
    keys = turn(keys, cosine[...], -sine[...])[:, 0:KW]
    project = jnp.concatenate(
        [dq[...].astype(f32), keys, total[:, KW:]], axis=1
    ).astype(bf16)
    project_out[...] = project
    grad = mm_t(project, w_qkv[...])
    x = x_in[...].astype(f32)
    inverse = inverse_norm(x)
    gain_out[...] = jnp.sum(grad * x * inverse, axis=0, keepdims=True)
    g_out[...] = middle_grad[...] + norm_back(x, inverse, gains[0:1, 0:D], grad)


def pack_kernel(
    core, normed, project, mixed, attn, normed_two, grad_gu, hidden, branch, gain_one, gain_two,
    keep, send, flat, tile,
):
    for at, start, gain in ((0, HALF_GAIN_ONE, gain_one), (1, HALF_GAIN_TWO, gain_two)):
        row = jnp.concatenate([gain[...], jnp.zeros((1, 64), f32)], axis=1)
        first = start // 2
        before = None
        for t in range(5):
            part = row[:, 128 * t : 128 * t + 128]
            place = slice(first + t, first + t + 1)
            if start % 2 == 0:
                flat[place, :] = part
            else:
                now = pltpu.roll(part, 64, 1)
                if before is None:
                    flat[place, :] = now
                else:
                    flat[place, :] = jnp.where(low_half((1, 128)), before, now)
                before = now

    def matrix(left, right, start_half, width_half):
        rows, columns = left.shape[1], right.shape[1]
        for t in range((width_half + 1) // 2):
            wide = min(128, columns - 128 * t)
            tile[t, 0:rows, 0:wide] = t_mm(left[...], right[:, 128 * t : 128 * t + wide])
        for parity in range(2):
            put_rows(
                flat, start_half + parity * width_half, rows // 2, width_half,
                lambda t, parity=parity: tile[t, pl.ds(parity, rows // 2, stride=2), :],
            )

    matrix(normed, project, HALF_QKV, PW // 64)
    matrix(mixed, attn, HALF_OUT, D // 64)
    matrix(hidden, branch, HALF_DOWN, D // 64)

    def in_tile(c, carry):
        flat[pl.ds(HALF_IN // 2 + c, D, stride=24), :] = t_mm(
            normed_two[...], grad_gu[:, pl.ds(pl.multiple_of(c * 128, 128), 128)]
        )
        return carry

    lax.fori_loop(0, 24, in_tile, 0)

    lane = lax.broadcasted_iota(jnp.int32, (CHUNK, 128), 1)
    for out, flip in ((keep, 0), (send, 1)):
        def one_shard(k, carry):
            d = 2 * k + lax.rem(core[0] + flip, 2)
            shift = lax.rem(d * 9, 128)
            base = d * 216 + lax.div(d * 9, 128)
            turned = pltpu.roll(flat[pl.ds(base, CHUNK), :], lax.rem(128 - shift, 128), 1)
            ahead = pltpu.roll(turned, CHUNK - 1, 0)
            value = jnp.where(lane < 128 - shift, turned, ahead)
            out[pl.ds(pl.multiple_of(k * CHUNK, CHUNK), CHUNK), :] = value.astype(bf16)
            return carry

        lax.fori_loop(0, DEVICES // 2, one_shard, 0)


def hop(value, by):
    pairs = [(i, i + by) for i in range(DEVICES) if 0 <= i + by < DEVICES]
    return lax.ppermute(value, "fsdp", pairs)


def swap(value):
    return lax.ppermute(value, "fsdp", [(i, i ^ 1) for i in range(DEVICES)])


def window_of(value, core):
    blocks = [hop(value, by) for by in (8, 6, 4, 2)] + [value]
    same = jnp.concatenate(blocks, axis=0)
    rows = value.shape[0]
    gift = lax.dynamic_slice_in_dim(same, (1 - core) * rows, SAME_CORE * rows, 0)
    return same, swap(gift)


def give_back(dkv_s, dkv_t, core):
    got = swap(dkv_t).astype(f32)
    blank = jnp.zeros((ROWS, 2 * KW), f32)
    early = jnp.concatenate([got, blank], axis=0)
    late = jnp.concatenate([blank, got], axis=0)
    total = dkv_s + jnp.where(core == 0, late, early)
    pieces = [
        hop(total[at * ROWS : (at + 1) * ROWS].astype(bf16), -by)
        for at, by in enumerate((8, 6, 4, 2))
    ]
    return total[SAME_CORE * ROWS :], pieces


def reduce_packed(keep, send):
    got = swap(send)
    total = (keep.astype(f32) + got.astype(f32)).astype(bf16)
    total = total.reshape(DEVICES // 2, CHUNK, 128)
    groups = [list(range(0, DEVICES, 2)), list(range(1, DEVICES, 2))]
    pieces = lax.all_to_all(
        total, "fsdp", split_axis=0, concat_axis=0, tiled=True, axis_index_groups=groups
    )
    own = jnp.sum(pieces.astype(f32), axis=0)
    return own.reshape(-1)[:SHARD]


def tables(positions):
    half = HD // 2
    frequency = rope_base ** (-jnp.arange(half, dtype=f32) / half)
    angles = positions.astype(f32)[:, None] * frequency[None, :]
    return (
        jnp.concatenate([jnp.cos(angles)] * 4, axis=-1),
        jnp.concatenate([jnp.sin(angles)] * 4, axis=-1),
    )


def body(hidden_in, segment_ids, weights_flat, cotangent):
    device = lax.axis_index("fsdp")
    core = lax.rem(device, 2)
    first_row = device * ROWS
    layers = weights_flat.shape[0]
    gathered = []
    for layer in range(layers):
        padded = jnp.pad(weights_flat[layer], (0, CHUNK * 128 - SHARD))
        gathered.append(lax.all_gather(padded, "fsdp", axis=0, tiled=True))

    x_same, x_sibling = window_of(hidden_in, core)
    window = jnp.concatenate([x_same, x_sibling], axis=0)
    s_same, s_sibling = window_of(segment_ids, core)
    segments = jnp.concatenate([s_same, s_sibling], axis=0)
    order = jnp.arange(ROWS, dtype=jnp.int32)
    same_first = first_row - ROWS * jnp.array([8, 6, 4, 2, 0], jnp.int32)
    sibling_first = first_row - ROWS * jnp.array([7, 5, 3, 1], jnp.int32)
    key_row = jnp.concatenate([same_first, sibling_first])[:, None] + order[None, :]
    key_row = key_row.reshape(-1)
    cosine_all, sine_all = tables(key_row - segments)
    own = SAME_CORE * ROWS
    cosine, sine = cosine_all[own : own + ROWS], sine_all[own : own + ROWS]
    key_row = key_row[None, :]
    segment = segment_ids[:, None]
    first = first_row[None]
    core_in = core[None]

    x = hidden_in
    held = []
    for layer in range(layers):
        w_qkv, w_out, w_in, w_down, gains = unpack(gathered[layer].reshape(DEVICES * CHUNK, 128))
        if layer == 0:
            q, kv_s, kv_t, normed = call(
                heads_zero_kernel,
                [((ROWS, QW), bf16), ((WIN_S, 2 * KW), bf16), ((WIN_T, 2 * KW), bf16),
                 ((ROWS, D), bf16)],
                [window, cosine_all, sine_all, gains, w_qkv],
                flops=800_000_000, nbytes=6_000_000,
            )
        else:
            q, kv, normed = call(
                heads_kernel,
                [((ROWS, QW), bf16), ((ROWS, 2 * KW), bf16), ((ROWS, D), bf16)],
                [x, cosine, sine, gains, w_qkv],
                flops=150_000_000, nbytes=3_000_000,
            )
            kv_s, kv_t = window_of(kv, core)
        x_next, mixed, lse, middle, normed_two, gate_up, hidden = call(
            attend_kernel,
            [((ROWS, D), f32), ((ROWS, QW), bf16), ((GROUP * ROWS, KVH), f32), ((ROWS, D), f32),
             ((ROWS, D), bf16), ((ROWS, 2 * FF), f32), ((ROWS, FF), bf16)],
            [first, x, q, kv_s, kv_t, segment, key_row, gains, w_out, w_in, w_down],
            smem=1, flops=2_000_000_000, nbytes=12_000_000,
        )
        held.append((x, q, kv_s, kv_t, normed, mixed, lse, middle, normed_two, gate_up, hidden,
                     w_qkv, w_out, w_in, w_down, gains))
        x = x_next
    layer_out = x.astype(bf16)

    g = cotangent
    grads = [None] * layers
    for layer in reversed(range(layers)):
        (x, q, kv_s, kv_t, normed, mixed, lse, middle, normed_two, gate_up, hidden,
         w_qkv, w_out, w_in, w_down, gains) = held[layer]
        branch, grad_gu, attn, middle_grad, dq, dkv_s, dkv_t, gain_two = call(
            back_kernel,
            [((ROWS, D), bf16), ((ROWS, 2 * FF), bf16), ((ROWS, D), bf16), ((ROWS, D), f32),
             ((ROWS, QW), bf16), ((WIN_S, 2 * KW), f32), ((WIN_T, 2 * KW), bf16), ((1, D), f32)],
            [first, g, q, kv_s, kv_t, segment, key_row, cosine, sine, gains, w_out, w_in, w_down,
             lse, middle, gate_up],
            smem=1, flops=3_000_000_000, nbytes=15_000_000,
        )
        own_kv, pieces = give_back(dkv_s, dkv_t, core)
        g, project, gain_one = call(
            back_heads_kernel,
            [((ROWS, D), f32), ((ROWS, PW), bf16), ((1, D), f32)],
            [x, dq, own_kv, *pieces, cosine, sine, gains, w_qkv, middle_grad],
            flops=150_000_000, nbytes=3_000_000,
        )
        keep, send = call(
            pack_kernel,
            [((DEVICES // 2 * CHUNK, 128), bf16), ((DEVICES // 2 * CHUNK, 128), bf16)],
            [core_in, normed, project, mixed, attn, normed_two, grad_gu, hidden, branch,
             gain_one, gain_two],
            scratch=[pltpu.VMEM((FLAT_ROWS, 128), f32), pltpu.VMEM((8, FF, 128), f32)],
            smem=1, flops=1_200_000_000, nbytes=30_000_000,
        )
        grads[layer] = reduce_packed(keep, send)
    return (layer_out, g, jnp.stack(grads))


def solution(mesh):
    in_specs = (P("fsdp", None), P("fsdp"), P(None, "fsdp"), P("fsdp", None))
    out_specs = (P("fsdp", None), P("fsdp", None), P(None, "fsdp"))
    return jax.shard_map(body, mesh=mesh, in_specs=in_specs, out_specs=out_specs, check_vma=False)
```

```python
import functools

import jax
import jax.numpy as jnp
from jax import lax
from jax.experimental import pallas as pl
from jax.experimental.pallas import tpu as pltpu
from jax.sharding import PartitionSpec as P

D = 576
FF = 1536
QH = 9
KVH = 3
HD = 64
MAXLEN = 1024
QW = QH * HD
KW = KVH * HD
PW = QW + 2 * KW
GROUP = QH // KVH
DEVICES = 128
ROWS = 128
PARAMS = 3540096
SHARD = PARAMS // DEVICES
CHUNK = 224
SECTION = 240
SPLIT = 20
LOW_PLANES = 11
EDGE = 456
SAME_CORE = 4
WIN_S = (SAME_CORE + 1) * ROWS
WIN_T = SAME_CORE * ROWS
WIN = WIN_S + WIN_T

bf16 = jnp.bfloat16
f32 = jnp.float32
epsilon = 1e-05
rope_base = 10000.0
FACTOR = HD ** (-0.5)
VMEM_LIMIT = 60 * 1024 * 1024

HALF_GAIN_ONE = 0
HALF_QKV = D // 64
HALF_OUT = HALF_QKV + D * PW // 64
HALF_GAIN_TWO = HALF_OUT + QW * D // 64
HALF_IN = HALF_GAIN_TWO + D // 64
HALF_DOWN = HALF_IN + D * 2 * FF // 64


def mm(a, b):
    return lax.dot_general(a, b, (((1,), (0,)), ((), ())), preferred_element_type=f32)


def mm_t(a, b):
    return lax.dot_general(a, b, (((1,), (1,)), ((), ())), preferred_element_type=f32)


def t_mm(a, b):
    return lax.dot_general(a, b, (((0,), (0,)), ((), ())), preferred_element_type=f32)


def call(kernel, out_shape, args, scratch=(), smem=0, flops=0, nbytes=0):
    in_specs = [
        pl.BlockSpec(memory_space=pltpu.SMEM if at < smem else pltpu.VMEM)
        for at in range(len(args))
    ]
    return pl.pallas_call(
        kernel,
        out_shape=[jax.ShapeDtypeStruct(s, d) for s, d in out_shape],
        in_specs=in_specs,
        out_specs=[pl.BlockSpec(memory_space=pltpu.VMEM) for _ in out_shape],
        scratch_shapes=list(scratch),
        compiler_params=pltpu.CompilerParams(vmem_limit_bytes=VMEM_LIMIT),
        cost_estimate=pl.CostEstimate(flops=flops, bytes_accessed=nbytes, transcendentals=0),
    )(*args)


def low_half(shape):
    return lax.broadcasted_iota(jnp.int32, shape, 1) < 64


def take_rows(flat, start_half, pairs, width_half, store):
    tiles = (width_half + 1) // 2
    if start_half % 2 == 0:
        for t in range(tiles):
            store(t, flat[pl.ds(start_half // 2 + t, pairs, stride=width_half), :])
    else:
        before = None
        for t in range(tiles + 1):
            if t == tiles and width_half % 2 == 1:
                store(t - 1, before)
                break
            now = pltpu.roll(flat[pl.ds(start_half // 2 + t, pairs, stride=width_half), :], 64, 1)
            if before is not None:
                store(t - 1, jnp.where(low_half(now.shape), before, now))
            before = now


def put_rows(flat, start_half, pairs, width_half, load):
    tiles = (width_half + 1) // 2
    if start_half % 2 == 0:
        for t in range(tiles):
            place = pl.ds(start_half // 2 + t, pairs, stride=width_half)
            value = load(t)
            if 2 * t + 1 == width_half:
                value = jnp.where(low_half(value.shape), value, flat[place, :])
            flat[place, :] = value
    else:
        before = None
        for t in range(tiles + 1):
            if t == tiles and width_half % 2 == 1:
                break
            place = pl.ds(start_half // 2 + t, pairs, stride=width_half)
            now = pltpu.roll(load(t), 64, 1) if t < tiles else None
            if before is None:
                value = jnp.where(low_half(now.shape), flat[place, :], now)
            else:
                value = jnp.where(low_half(before.shape), before, now)
            flat[place, :] = value
            before = now


def gather_flat(gathered, layer, first, count, groups, flat, landing, sems):
    size = count // groups
    copies = []
    for n in range(groups):
        copies.append(
            pltpu.make_async_copy(
                gathered.at[pl.ds(first + n * size, size), layer],
                landing.at[pl.ds(n * size, size)],
                sems.at[n],
            )
        )
        copies[-1].start()
    tail = jnp.zeros((SECTION - 216, 128), f32)
    for n in range(groups):
        copies[n].wait()

        def one_shard(d, tail):
            rows = landing[d].astype(f32)
            base = pl.multiple_of(d * 216, 8)
            flat[pl.ds(base, 24), :] = tail + rows[0:24, :]
            flat[pl.ds(base + 24, 192), :] = rows[24:216, :]
            return rows[216:SECTION, :]

        tail = lax.fori_loop(n * size, (n + 1) * size, one_shard, tail)
    flat[count * 216 : count * 216 + 24, :] = tail


def take_matrix(flat, tile, out, start_half, width_half):
    rows, columns = out.shape

    def store(parity, at, value):
        tile[at, pl.ds(parity, rows // 2, stride=2), :] = value

    for parity in range(2):
        take_rows(
            flat, start_half + parity * width_half, rows // 2, width_half,
            functools.partial(store, parity),
        )
    for t in range((width_half + 1) // 2):
        wide = min(128, columns - 128 * t)
        out[:, 128 * t : 128 * t + wide] = tile[t, 0:rows, 0:wide].astype(bf16)


def take_gain(flat, gain, start):
    first = start // 2
    for t in range(5):
        if start % 2 == 0:
            value = flat[first + t : first + t + 1, :]
        else:
            here = pltpu.roll(flat[first + t : first + t + 1, :], 64, 1)
            after = pltpu.roll(flat[first + t + 1 : first + t + 2, :], 64, 1)
            value = jnp.where(low_half((1, 128)), here, after)
        gain[0:1, 128 * t : 128 * t + 128] = value


def unpack_first_kernel(layer, gathered, w_qkv, gain, landing, flat, tile, sems):
    gather_flat(gathered, layer, 0, SPLIT + 1, 3, flat, landing, sems)
    take_gain(flat, gain, HALF_GAIN_ONE)
    take_matrix(flat, tile, w_qkv, HALF_QKV, PW // 64)


def unpack_rest_kernel(layer, gathered, w_out, w_in, w_down, gain, landing, flat, tile, sems):
    gather_flat(gathered, layer, SPLIT, DEVICES - SPLIT, 4, flat, landing, sems)
    skip = 2 * 216 * SPLIT
    take_matrix(flat, tile, w_out, HALF_OUT - skip, D // 64)
    take_gain(flat, gain, HALF_GAIN_TWO - skip)
    take_matrix(flat, tile, w_down, HALF_DOWN - skip, D // 64)

    def in_tile(c, carry):
        w_in[:, pl.ds(pl.multiple_of(c * 128, 128), 128)] = flat[
            pl.ds((HALF_IN - skip) // 2 + c, D, stride=24), :
        ].astype(bf16)
        return carry

    lax.fori_loop(0, 24, in_tile, 0)


def unpack_call(kernel, layer, out_shape, gathered, count, groups, tiles, nbytes):
    return pl.pallas_call(
        functools.partial(kernel, layer),
        out_shape=[jax.ShapeDtypeStruct(s, d) for s, d in out_shape],
        in_specs=[pl.BlockSpec(memory_space=pl.ANY)],
        out_specs=[pl.BlockSpec(memory_space=pltpu.VMEM) for _ in out_shape],
        scratch_shapes=[
            pltpu.VMEM((count, SECTION, 128), bf16),
            pltpu.VMEM((count * 216 + 32, 128), f32),
            pltpu.VMEM(tiles, f32),
            pltpu.SemaphoreType.DMA((groups,)),
        ],
        compiler_params=pltpu.CompilerParams(vmem_limit_bytes=VMEM_LIMIT),
        cost_estimate=pl.CostEstimate(flops=0, bytes_accessed=nbytes, transcendentals=0),
    )(gathered)


def unpack_first(gathered, layer):
    return unpack_call(
        unpack_first_kernel, layer, [((D, PW), bf16), ((1, 640), f32)], gathered,
        SPLIT + 1, 3, (8, D, 128), 9_000_000,
    )


def unpack_rest(gathered, layer):
    return unpack_call(
        unpack_rest_kernel, layer,
        [((QW, D), bf16), ((D, 2 * FF), bf16), ((FF, D), bf16), ((1, 640), f32)], gathered,
        DEVICES - SPLIT, 4, (5, FF, 128), 30_000_000,
    )


def turn(value, cosine, sine):
    lane = lax.broadcasted_iota(jnp.int32, (value.shape[0], 128), 1)
    first = lax.rem(lane, 64) < 32
    pieces = []
    for t in range(value.shape[1] // 128):
        part = value[:, 128 * t : 128 * t + 128]
        swapped = jnp.where(first, -pltpu.roll(part, 96, 1), pltpu.roll(part, 32, 1))
        pieces.append(part * cosine + swapped * sine)
    return jnp.concatenate(pieces, axis=1)


def inverse_norm(values):
    return lax.rsqrt(jnp.mean(values * values, axis=-1, keepdims=True) + epsilon)


def heads_zero_kernel(window, cosine, sine, gain_row, w_qkv, q_out, kv_s, kv_t, normed_out):
    gain = gain_row[:, 0:D]
    for begin, rows in ((0, 384), (384, 384), (768, 384)):
        x = window[begin : begin + rows, :].astype(f32)
        normed = (x * inverse_norm(x) * gain).astype(bf16)
        project = mm(normed, w_qkv[:, 512:PW])
        both = turn(project[:, 0:256], cosine[begin : begin + rows, :], sine[begin : begin + rows, :])
        kv = jnp.concatenate([both[:, 64:256], project[:, 256:448]], axis=1).astype(bf16)
        for r in range(0, rows, 128):
            at = begin + r
            if at < WIN_S:
                kv_s[at : at + 128, :] = kv[r : r + 128, :]
            else:
                kv_t[at - WIN_S : at - WIN_S + 128, :] = kv[r : r + 128, :]
    own = SAME_CORE * ROWS
    x = window[own : own + ROWS, :].astype(f32)
    normed = (x * inverse_norm(x) * gain).astype(bf16)
    normed_out[...] = normed
    project = mm(normed, w_qkv[:, 0:640])
    q_out[...] = turn(project, cosine[own : own + ROWS, :], sine[own : own + ROWS, :])[
        :, 0:QW
    ].astype(bf16)


def heads_kernel(x_in, cosine, sine, gain_row, w_qkv, q_out, kv_out, normed_out):
    x = x_in[...]
    normed = (x * inverse_norm(x) * gain_row[:, 0:D]).astype(bf16)
    normed_out[...] = normed
    project = mm(normed, w_qkv[...])
    both = turn(project[:, 0:768], cosine[...], sine[...])
    q_out[...] = both[:, 0:QW].astype(bf16)
    kv_out[...] = jnp.concatenate([both[:, QW:768], project[:, 768:PW]], axis=1).astype(bf16)


def allowed_of(segment, key_row, first_row):
    query = first_row + lax.broadcasted_iota(jnp.int32, (ROWS, 1), 0)
    return (key_row >= segment) & (key_row <= query)


def group_rows(value, group):
    return jnp.concatenate(
        [value[:, (GROUP * group + n) * HD : (GROUP * group + n + 1) * HD] for n in range(GROUP)],
        axis=0,
    )


def window_rows(kv_s, kv_t, begin):
    return jnp.concatenate(
        [kv_s[:, begin : begin + HD], kv_t[:, begin : begin + HD]], axis=0
    )


def attend_kernel(
    first, x_in, q_in, kv_s, kv_t, segment, key_row, gain_row, w_out, w_in, w_down,
    x_out, mixed_out, lse_out, middle_out, normed_out, gate_up_out, hidden_out,
):
    allowed = allowed_of(segment[...], key_row[...], first[0])
    bias = jnp.where(allowed, 0.0, -1e30).astype(f32)
    bias = jnp.concatenate([bias] * GROUP, axis=0)
    q = q_in[...]
    pieces = []
    for group in range(KVH):
        keys = window_rows(kv_s, kv_t, group * HD)
        values = window_rows(kv_s, kv_t, KW + group * HD)
        scores = mm_t(group_rows(q, group), keys) * FACTOR + bias
        peak = jnp.max(scores, axis=-1, keepdims=True)
        powers = jnp.exp(scores - peak)
        total = jnp.sum(powers, axis=-1, keepdims=True)
        lse_out[:, group : group + 1] = peak + jnp.log(total)
        weights = (powers * (1.0 / total)).astype(bf16)
        mixed = mm(weights, values)
        for n in range(GROUP):
            pieces.append(mixed[n * ROWS : (n + 1) * ROWS, :])
    mixed = jnp.concatenate(pieces, axis=1).astype(bf16)
    mixed_out[...] = mixed
    middle = x_in[...].astype(f32) + mm(mixed, w_out[...])
    middle_out[...] = middle
    normed = (middle * inverse_norm(middle) * gain_row[:, 0:D]).astype(bf16)
    normed_out[...] = normed
    gate_up = mm(normed, w_in[...])
    gate_up_out[...] = gate_up
    gate = gate_up[:, 0:FF]
    hidden = (gate * jax.nn.sigmoid(gate) * gate_up[:, FF:]).astype(bf16)
    hidden_out[...] = hidden
    x_out[...] = middle + mm(hidden, w_down[...])


def norm_back(values, inverse, gain, grad):
    weighted = grad * gain
    return inverse * weighted - values * inverse**3 * jnp.mean(
        weighted * values, axis=-1, keepdims=True
    )


def back_kernel(
    first, g_in, q_in, kv_s, kv_t, segment, key_row, cosine, sine, gain_row, w_out, w_in, w_down,
    lse, middle_in, gate_up,
    branch_out, grad_gu_out, attn_out, middle_grad_out, dq_out, dkv_s, dkv_t, gain_out,
):
    g = g_in[...].astype(f32)
    branch = g.astype(bf16)
    branch_out[...] = branch
    grad_hidden = mm_t(branch, w_down[...])
    gate = gate_up[:, 0:FF]
    up = gate_up[:, FF:]
    sigma = jax.nn.sigmoid(gate)
    grad_gu_out[:, 0:FF] = (
        grad_hidden * up * sigma * (1.0 + gate * (1.0 - sigma))
    ).astype(bf16)
    grad_gu_out[:, FF:] = (grad_hidden * gate * sigma).astype(bf16)
    grad_two = mm_t(grad_gu_out[...], w_in[...])
    middle = middle_in[...]
    inverse = inverse_norm(middle)
    gain_out[...] = jnp.sum(grad_two * middle * inverse, axis=0, keepdims=True)
    grad_middle = g + norm_back(middle, inverse, gain_row[:, 0:D], grad_two)
    middle_grad_out[...] = grad_middle
    attn = grad_middle.astype(bf16)
    attn_out[...] = attn
    grad_mixed = mm_t(attn, w_out[...]).astype(bf16)

    allowed = allowed_of(segment[...], key_row[...], first[0])
    bias = jnp.where(allowed, 0.0, -1e30).astype(f32)
    bias = jnp.concatenate([bias] * GROUP, axis=0)
    q = q_in[...]
    dq, dk, dv = [], [], []
    for group in range(KVH):
        keys = window_rows(kv_s, kv_t, group * HD)
        values = window_rows(kv_s, kv_t, KW + group * HD)
        query = group_rows(q, group)
        grad = group_rows(grad_mixed, group)
        scores = mm_t(query, keys) * FACTOR + bias
        probs = jnp.exp(scores - lse[:, group : group + 1])
        grad_w = mm_t(grad, values)
        delta = jnp.sum(probs * grad_w, axis=-1, keepdims=True)
        grad_scores = (probs * (grad_w - delta)).astype(bf16)
        part = mm(grad_scores, keys) * FACTOR
        for n in range(GROUP):
            dq.append(part[n * ROWS : (n + 1) * ROWS, :])
        dk.append(t_mm(grad_scores, query) * FACTOR)
        dv.append(t_mm(probs.astype(bf16), grad))
    dkv = jnp.concatenate(dk + dv, axis=1)
    dkv_s[...] = dkv[0:WIN_S, :]
    dkv_t[...] = dkv[WIN_S:, :].astype(bf16)
    wide = jnp.concatenate(dq + [jnp.zeros((ROWS, HD), f32)], axis=1)
    dq_out[...] = turn(wide, cosine[...], -sine[...])[:, 0:QW].astype(bf16)


def back_heads_kernel(
    x_in, dq, own, r8, r6, r4, r2, cosine, sine, gain_row, w_qkv, middle_grad,
    g_out, project_out, gain_out,
):
    total = own[...]
    for piece in (r8, r6, r4, r2):
        total = total + piece[...].astype(f32)
    keys = jnp.concatenate([total[:, 0:KW], jnp.zeros((ROWS, HD), f32)], axis=1)
    keys = turn(keys, cosine[...], -sine[...])[:, 0:KW]
    project = jnp.concatenate(
        [dq[...].astype(f32), keys, total[:, KW:]], axis=1
    ).astype(bf16)
    project_out[...] = project
    grad = mm_t(project, w_qkv[...])
    x = x_in[...].astype(f32)
    inverse = inverse_norm(x)
    gain_out[...] = jnp.sum(grad * x * inverse, axis=0, keepdims=True)
    g_out[...] = middle_grad[...] + norm_back(x, inverse, gain_row[:, 0:D], grad)


def put_gain(flat, gain, start):
    row = jnp.concatenate([gain[...], jnp.zeros((1, 64), f32)], axis=1)
    first = start // 2
    before = None
    for t in range(5):
        part = row[:, 128 * t : 128 * t + 128]
        place = slice(first + t, first + t + 1)
        if start % 2 == 0:
            flat[place, :] = part
        else:
            now = pltpu.roll(part, 64, 1)
            if before is None:
                flat[place, :] = now
            else:
                flat[place, :] = jnp.where(low_half((1, 128)), before, now)
            before = now


def put_matrix(flat, tile, left, right, start_half, width_half):
    rows, columns = left.shape[1], right.shape[1]
    for t in range((width_half + 1) // 2):
        wide = min(128, columns - 128 * t)
        tile[t, 0:rows, 0:wide] = t_mm(left[...], right[:, 128 * t : 128 * t + wide])
    for parity in range(2):
        put_rows(
            flat, start_half + parity * width_half, rows // 2, width_half,
            lambda t, parity=parity: tile[t, pl.ds(parity, rows // 2, stride=2), :],
        )


def cut(flat, core, first_plane, planes, skip, keep, send):
    last = lax.broadcasted_iota(jnp.int32, (CHUNK, 128), 0) == CHUNK - 1
    for out, flip in ((keep, 0), (send, 1)):
        def one_owner(k, carry, out=out, flip=flip):
            d = 2 * (first_plane + k) + lax.rem(core[0] + flip, 2)
            base = pl.multiple_of(d * 216 - skip + 8, 8)
            odd = jnp.where(d < DEVICES // 2, base - 1, base + CHUNK - 1)
            value = jnp.where(last, flat[pl.ds(odd, 1), :], flat[pl.ds(base, CHUNK), :])
            out[pl.ds(pl.multiple_of(k * CHUNK, CHUNK), CHUNK), :] = value.astype(bf16)
            return carry

        lax.fori_loop(0, planes, one_owner, 0)


def pack_rest_kernel(
    core, mixed, attn, normed_two, grad_gu, hidden, branch, gain_two, keep, send, edge, flat, tile
):
    skip = 216 * SPLIT
    half = 2 * (7 - skip)
    put_gain(flat, gain_two, HALF_GAIN_TWO + half)
    put_matrix(flat, tile, mixed, attn, HALF_OUT + half, D // 64)
    put_matrix(flat, tile, hidden, branch, HALF_DOWN + half, D // 64)

    def in_tile(c, carry):
        flat[pl.ds((HALF_IN + half) // 2 + c, D, stride=24), :] = t_mm(
            normed_two[...], grad_gu[:, pl.ds(pl.multiple_of(c * 128, 128), 128)]
        )
        return carry

    lax.fori_loop(0, 24, in_tile, 0)
    cut(flat, core, LOW_PLANES, DEVICES // 2 - LOW_PLANES, skip, keep, send)
    edge[...] = flat[0:EDGE, :]


def pack_first_kernel(core, normed, project, gain_one, edge, keep, send, flat, tile):
    skip = 216 * SPLIT
    flat[skip : skip + EDGE, :] = edge[...]
    put_gain(flat, gain_one, HALF_GAIN_ONE + 14)
    put_matrix(flat, tile, normed, project, HALF_QKV + 14, PW // 64)
    cut(flat, core, 0, LOW_PLANES, 0, keep, send)


def hop(value, by):
    pairs = [(i, i + by) for i in range(DEVICES) if 0 <= i + by < DEVICES]
    return lax.ppermute(value, "fsdp", pairs)


def swap(value):
    return lax.ppermute(value, "fsdp", [(i, i ^ 1) for i in range(DEVICES)])


def window_of(value, core):
    blocks = [hop(value, by) for by in (8, 6, 4, 2)] + [value]
    same = jnp.concatenate(blocks, axis=0)
    rows = value.shape[0]
    gift = lax.dynamic_slice_in_dim(same, (1 - core) * rows, SAME_CORE * rows, 0)
    return same, swap(gift)


def give_back(dkv_s, dkv_t, core):
    got = swap(dkv_t).astype(f32)
    blank = jnp.zeros((ROWS, 2 * KW), f32)
    early = jnp.concatenate([got, blank], axis=0)
    late = jnp.concatenate([blank, got], axis=0)
    total = dkv_s + jnp.where(core == 0, late, early)
    pieces = [
        hop(total[at * ROWS : (at + 1) * ROWS].astype(bf16), -by)
        for at, by in enumerate((8, 6, 4, 2))
    ]
    return total[SAME_CORE * ROWS :], pieces


def both_cores(keep, send):
    return (keep.astype(f32) + swap(send).astype(f32)).astype(bf16)


def to_owners(first, rest, device):
    total = jnp.concatenate([first, rest], axis=0).reshape(DEVICES // 2, CHUNK, 128)
    groups = [list(range(0, DEVICES, 2)), list(range(1, DEVICES, 2))]
    pieces = lax.all_to_all(
        total, "fsdp", split_axis=0, concat_axis=0, tiled=True, axis_index_groups=groups
    )
    own = jnp.sum(pieces.astype(f32), axis=0)
    rows = jnp.concatenate([own[CHUNK - 1 :], own], axis=0)
    return lax.dynamic_slice_in_dim(rows.reshape(-1), 9 * device, SHARD, 0)


def tables(positions):
    half = HD // 2
    frequency = rope_base ** (-jnp.arange(half, dtype=f32) / half)
    angles = positions.astype(f32)[:, None] * frequency[None, :]
    return (
        jnp.concatenate([jnp.cos(angles)] * 4, axis=-1),
        jnp.concatenate([jnp.sin(angles)] * 4, axis=-1),
    )


def body(hidden_in, segment_ids, weights_flat, cotangent):
    device = lax.axis_index("fsdp")
    core = lax.rem(device, 2)
    first_row = device * ROWS
    layers = weights_flat.shape[0]
    sections = []
    for layer in range(layers):
        blank = jnp.zeros((SECTION * 128,), bf16)
        sections.append(lax.dynamic_update_slice(blank, weights_flat[layer], (9 * device,)))
    gathered = lax.all_gather(jnp.concatenate(sections), "fsdp", axis=0, tiled=True)
    gathered = gathered.reshape(DEVICES, layers, SECTION, 128)

    x_same, x_sibling = window_of(hidden_in, core)
    window = jnp.concatenate([x_same, x_sibling], axis=0)
    s_same, s_sibling = window_of(segment_ids, core)
    segments = jnp.concatenate([s_same, s_sibling], axis=0)
    order = jnp.arange(ROWS, dtype=jnp.int32)
    same_first = first_row - ROWS * jnp.array([8, 6, 4, 2, 0], jnp.int32)
    sibling_first = first_row - ROWS * jnp.array([7, 5, 3, 1], jnp.int32)
    key_row = jnp.concatenate([same_first, sibling_first])[:, None] + order[None, :]
    key_row = key_row.reshape(-1)
    cosine_all, sine_all = tables(key_row - segments)
    own = SAME_CORE * ROWS
    cosine, sine = cosine_all[own : own + ROWS], sine_all[own : own + ROWS]
    key_row = key_row[None, :]
    segment = segment_ids[:, None]
    first = first_row[None]
    core_in = core[None]

    x = hidden_in
    held = []
    for layer in range(layers):
        w_qkv, gain_one = unpack_first(gathered, layer)
        w_out, w_in, w_down, gain_two = unpack_rest(gathered, layer)
        if layer == 0:
            q, kv_s, kv_t, normed = call(
                heads_zero_kernel,
                [((ROWS, QW), bf16), ((WIN_S, 2 * KW), bf16), ((WIN_T, 2 * KW), bf16),
                 ((ROWS, D), bf16)],
                [window, cosine_all, sine_all, gain_one, w_qkv],
                flops=800_000_000, nbytes=6_000_000,
            )
        else:
            q, kv, normed = call(
                heads_kernel,
                [((ROWS, QW), bf16), ((ROWS, 2 * KW), bf16), ((ROWS, D), bf16)],
                [x, cosine, sine, gain_one, w_qkv],
                flops=150_000_000, nbytes=3_000_000,
            )
            kv_s, kv_t = window_of(kv, core)
        x_next, mixed, lse, middle, normed_two, gate_up, hidden = call(
            attend_kernel,
            [((ROWS, D), f32), ((ROWS, QW), bf16), ((GROUP * ROWS, KVH), f32), ((ROWS, D), f32),
             ((ROWS, D), bf16), ((ROWS, 2 * FF), f32), ((ROWS, FF), bf16)],
            [first, x, q, kv_s, kv_t, segment, key_row, gain_two, w_out, w_in, w_down],
            smem=1, flops=2_000_000_000, nbytes=12_000_000,
        )
        held.append((x, q, kv_s, kv_t, normed, mixed, lse, middle, normed_two, gate_up, hidden,
                     w_qkv, w_out, w_in, w_down, gain_one, gain_two))
        x = x_next
    layer_out = x.astype(bf16)

    g = cotangent
    grads = [None] * layers
    for layer in reversed(range(layers)):
        (x, q, kv_s, kv_t, normed, mixed, lse, middle, normed_two, gate_up, hidden,
         w_qkv, w_out, w_in, w_down, gain_one, gain_two) = held[layer]
        branch, grad_gu, attn, middle_grad, dq, dkv_s, dkv_t, grad_two = call(
            back_kernel,
            [((ROWS, D), bf16), ((ROWS, 2 * FF), bf16), ((ROWS, D), bf16), ((ROWS, D), f32),
             ((ROWS, QW), bf16), ((WIN_S, 2 * KW), f32), ((WIN_T, 2 * KW), bf16), ((1, D), f32)],
            [first, g, q, kv_s, kv_t, segment, key_row, cosine, sine, gain_two, w_out, w_in, w_down,
             lse, middle, gate_up],
            smem=1, flops=3_000_000_000, nbytes=15_000_000,
        )
        rest_shape = (((DEVICES // 2 - LOW_PLANES) * CHUNK, 128), bf16)
        keep, send, edge = call(
            pack_rest_kernel,
            [rest_shape, rest_shape, ((EDGE, 128), f32)],
            [core_in, mixed, attn, normed_two, grad_gu, hidden, branch, grad_two],
            scratch=[
                pltpu.VMEM((216 * (DEVICES - SPLIT) + 40, 128), f32), pltpu.VMEM((5, FF, 128), f32)
            ],
            smem=1, flops=1_000_000_000, nbytes=25_000_000,
        )
        own_kv, pieces = give_back(dkv_s, dkv_t, core)
        send, pieces = lax.optimization_barrier((send, pieces))
        rest_part = both_cores(keep, send)
        g, project, grad_one = call(
            back_heads_kernel,
            [((ROWS, D), f32), ((ROWS, PW), bf16), ((1, D), f32)],
            [x, dq, own_kv, *pieces, cosine, sine, gain_one, w_qkv, middle_grad],
            flops=150_000_000, nbytes=3_000_000,
        )
        if layer + 1 < layers:
            project, grads[layer + 1] = lax.optimization_barrier((project, grads[layer + 1]))
        low_shape = ((LOW_PLANES * CHUNK, 128), bf16)
        keep, send = call(
            pack_first_kernel,
            [low_shape, low_shape],
            [core_in, normed, project, grad_one, edge],
            scratch=[pltpu.VMEM((216 * SPLIT + 480, 128), f32), pltpu.VMEM((8, D, 128), f32)],
            smem=1, flops=200_000_000, nbytes=8_000_000,
        )
        first_part = both_cores(keep, send)
        if layer > 0:
            g, first_part, rest_part = lax.optimization_barrier((g, first_part, rest_part))
        grads[layer] = to_owners(first_part, rest_part, device)
    return (layer_out, g, jnp.stack(grads))


def solution(mesh):
    in_specs = (P("fsdp", None), P("fsdp"), P(None, "fsdp"), P("fsdp", None))
    out_specs = (P("fsdp", None), P("fsdp", None), P(None, "fsdp"))
    return jax.shard_map(body, mesh=mesh, in_specs=in_specs, out_specs=out_specs, check_vma=False)
```

```python
import functools

import jax
import jax.numpy as jnp
from jax import lax
from jax.experimental import pallas as pl
from jax.experimental.pallas import tpu as pltpu
from jax.sharding import PartitionSpec as P

D = 576
FF = 1536
QH = 9
KVH = 3
HD = 64
MAXLEN = 1024
QW = QH * HD
KW = KVH * HD
PW = QW + 2 * KW
GROUP = QH // KVH
DEVICES = 128
ROWS = 128
PARAMS = 3540096
SHARD = PARAMS // DEVICES
CHUNK = 224
SECTION = 240
SPLIT = 20
LOW_PLANES = 16
JOIN = 8
EDGE = 2616
SAME_CORE = 4
WIN_S = (SAME_CORE + 1) * ROWS
WIN_T = SAME_CORE * ROWS
WIN = WIN_S + WIN_T

bf16 = jnp.bfloat16
f32 = jnp.float32
epsilon = 1e-05
rope_base = 10000.0
FACTOR = HD ** (-0.5)
VMEM_LIMIT = 60 * 1024 * 1024

HALF_GAIN_ONE = 0
HALF_QKV = D // 64
HALF_OUT = HALF_QKV + D * PW // 64
HALF_GAIN_TWO = HALF_OUT + QW * D // 64
HALF_IN = HALF_GAIN_TWO + D // 64
HALF_DOWN = HALF_IN + D * 2 * FF // 64


def mm(a, b):
    return lax.dot_general(a, b, (((1,), (0,)), ((), ())), preferred_element_type=f32)


def mm_t(a, b):
    return lax.dot_general(a, b, (((1,), (1,)), ((), ())), preferred_element_type=f32)


def t_mm(a, b):
    return lax.dot_general(a, b, (((0,), (0,)), ((), ())), preferred_element_type=f32)


def call(kernel, out_shape, args, scratch=(), smem=0, apart=0, flops=0, nbytes=0):
    in_specs = [
        pl.BlockSpec(
            memory_space=pltpu.SMEM if at < smem
            else pl.ANY if at >= len(args) - apart else pltpu.VMEM
        )
        for at in range(len(args))
    ]
    return pl.pallas_call(
        kernel,
        out_shape=[jax.ShapeDtypeStruct(s, d) for s, d in out_shape],
        in_specs=in_specs,
        out_specs=[pl.BlockSpec(memory_space=pltpu.VMEM) for _ in out_shape],
        scratch_shapes=list(scratch),
        compiler_params=pltpu.CompilerParams(vmem_limit_bytes=VMEM_LIMIT),
        cost_estimate=pl.CostEstimate(flops=flops, bytes_accessed=nbytes, transcendentals=0),
    )(*args)


def low_half(shape):
    return lax.broadcasted_iota(jnp.int32, shape, 1) < 64


def take_rows(flat, start_half, pairs, width_half, store):
    tiles = (width_half + 1) // 2
    if start_half % 2 == 0:
        for t in range(tiles):
            store(t, flat[pl.ds(start_half // 2 + t, pairs, stride=width_half), :])
    else:
        before = None
        for t in range(tiles + 1):
            if t == tiles and width_half % 2 == 1:
                store(t - 1, before)
                break
            now = pltpu.roll(flat[pl.ds(start_half // 2 + t, pairs, stride=width_half), :], 64, 1)
            if before is not None:
                store(t - 1, jnp.where(low_half(now.shape), before, now))
            before = now


def put_rows(flat, start_half, pairs, width_half, load):
    tiles = (width_half + 1) // 2
    if start_half % 2 == 0:
        for t in range(tiles):
            place = pl.ds(start_half // 2 + t, pairs, stride=width_half)
            value = load(t)
            if 2 * t + 1 == width_half:
                value = jnp.where(low_half(value.shape), value, flat[place, :])
            flat[place, :] = value
    else:
        before = None
        for t in range(tiles + 1):
            if t == tiles and width_half % 2 == 1:
                break
            place = pl.ds(start_half // 2 + t, pairs, stride=width_half)
            now = pltpu.roll(load(t), 64, 1) if t < tiles else None
            if before is None:
                value = jnp.where(low_half(now.shape), flat[place, :], now)
            else:
                value = jnp.where(low_half(before.shape), before, now)
            flat[place, :] = value
            before = now


WEIGHT_SCRATCH = (
    pltpu.VMEM((QW, D), bf16),
    pltpu.VMEM((D, 2 * FF), bf16),
    pltpu.VMEM((FF, D), bf16),
    pltpu.SemaphoreType.DMA((3,)),
)


def fetch(sources, places, sems):
    copies = [
        pltpu.make_async_copy(source, place, sems.at[n])
        for n, (source, place) in enumerate(zip(sources, places))
    ]
    return copies


def gather_flat(gathered, layer, first, count, groups, flat, landing, sems):
    size = count // groups
    copies = []
    for n in range(groups):
        copies.append(
            pltpu.make_async_copy(
                gathered.at[pl.ds(first + n * size, size), layer],
                landing.at[pl.ds(n * size, size)],
                sems.at[n],
            )
        )
        copies[-1].start()
    tail = jnp.zeros((SECTION - 216, 128), f32)
    for n in range(groups):
        copies[n].wait()

        def one_shard(d, tail):
            rows = landing[d].astype(f32)
            base = pl.multiple_of(d * 216, 8)
            flat[pl.ds(base, 24), :] = tail + rows[0:24, :]
            flat[pl.ds(base + 24, 192), :] = rows[24:216, :]
            return rows[216:SECTION, :]

        tail = lax.fori_loop(n * size, (n + 1) * size, one_shard, tail)
    flat[count * 216 : count * 216 + 24, :] = tail


def take_matrix(flat, tile, out, start_half, width_half):
    rows, columns = out.shape

    def store(parity, at, value):
        tile[at, pl.ds(parity, rows // 2, stride=2), :] = value

    for parity in range(2):
        take_rows(
            flat, start_half + parity * width_half, rows // 2, width_half,
            functools.partial(store, parity),
        )
    for t in range((width_half + 1) // 2):
        wide = min(128, columns - 128 * t)
        out[:, 128 * t : 128 * t + wide] = tile[t, 0:rows, 0:wide].astype(bf16)


def take_gain(flat, gain, start):
    first = start // 2
    for t in range(5):
        if start % 2 == 0:
            value = flat[first + t : first + t + 1, :]
        else:
            here = pltpu.roll(flat[first + t : first + t + 1, :], 64, 1)
            after = pltpu.roll(flat[first + t + 1 : first + t + 2, :], 64, 1)
            value = jnp.where(low_half((1, 128)), here, after)
        gain[0:1, 128 * t : 128 * t + 128] = value


def unpack_first_kernel(layer, gathered, w_qkv, gain, landing, flat, tile, sems):
    gather_flat(gathered, layer, 0, SPLIT + 1, 3, flat, landing, sems)
    take_gain(flat, gain, HALF_GAIN_ONE)
    take_matrix(flat, tile, w_qkv, HALF_QKV, PW // 64)


def unpack_rest_kernel(
    layer, gathered, w_out_at, w_in_at, w_down_at, gain, landing, flat, tile, sems,
    w_out, w_in, w_down, out_sems,
):
    gather_flat(gathered, layer, SPLIT, DEVICES - SPLIT, 4, flat, landing, sems)
    skip = 2 * 216 * SPLIT

    def in_tile(c, carry):
        w_in[:, pl.ds(pl.multiple_of(c * 128, 128), 128)] = flat[
            pl.ds((HALF_IN - skip) // 2 + c, D, stride=24), :
        ].astype(bf16)
        return carry

    lax.fori_loop(0, 24, in_tile, 0)
    copies = fetch((w_out, w_in, w_down), (w_out_at, w_in_at, w_down_at), out_sems)
    copies[1].start()
    take_matrix(flat, tile, w_down, HALF_DOWN - skip, D // 64)
    copies[2].start()
    take_matrix(flat, tile, w_out, HALF_OUT - skip, D // 64)
    copies[0].start()
    take_gain(flat, gain, HALF_GAIN_TWO - skip)
    for copy in copies:
        copy.wait()


def unpack_call(
    kernel, layer, out_shape, gathered, count, groups, tiles, nbytes, apart=0, scratch=()
):
    return pl.pallas_call(
        functools.partial(kernel, layer),
        out_shape=[jax.ShapeDtypeStruct(s, d) for s, d in out_shape],
        in_specs=[pl.BlockSpec(memory_space=pl.ANY)],
        out_specs=[
            pl.BlockSpec(memory_space=pl.ANY if at < apart else pltpu.VMEM)
            for at in range(len(out_shape))
        ],
        scratch_shapes=[
            pltpu.VMEM((count, SECTION, 128), bf16),
            pltpu.VMEM((count * 216 + 32, 128), f32),
            pltpu.VMEM(tiles, f32),
            pltpu.SemaphoreType.DMA((groups,)),
            *scratch,
        ],
        compiler_params=pltpu.CompilerParams(vmem_limit_bytes=VMEM_LIMIT),
        cost_estimate=pl.CostEstimate(flops=2_000_000_000, bytes_accessed=nbytes, transcendentals=0),
    )(gathered)


def unpack_first(gathered, layer):
    return unpack_call(
        unpack_first_kernel, layer, [((D, PW), bf16), ((1, 640), f32)], gathered,
        SPLIT + 1, 3, (8, D, 128), 9_000_000,
    )


def unpack_rest(gathered, layer):
    return unpack_call(
        unpack_rest_kernel, layer,
        [((QW, D), bf16), ((D, 2 * FF), bf16), ((FF, D), bf16), ((1, 640), f32)], gathered,
        DEVICES - SPLIT, 4, (5, FF, 128), 30_000_000, apart=3, scratch=WEIGHT_SCRATCH,
    )


def turn(value, cosine, sine):
    lane = lax.broadcasted_iota(jnp.int32, (value.shape[0], 128), 1)
    first = lax.rem(lane, 64) < 32
    pieces = []
    for t in range(value.shape[1] // 128):
        part = value[:, 128 * t : 128 * t + 128]
        swapped = jnp.where(first, -pltpu.roll(part, 96, 1), pltpu.roll(part, 32, 1))
        pieces.append(part * cosine + swapped * sine)
    return jnp.concatenate(pieces, axis=1)


def inverse_norm(values):
    return lax.rsqrt(jnp.mean(values * values, axis=-1, keepdims=True) + epsilon)


def heads_zero_kernel(window, cosine, sine, gain_row, w_qkv, q_out, kv_s, kv_t, normed_out):
    gain = gain_row[:, 0:D]
    for begin, rows in ((0, 384), (384, 384), (768, 384)):
        x = window[begin : begin + rows, :].astype(f32)
        normed = (x * inverse_norm(x) * gain).astype(bf16)
        project = mm(normed, w_qkv[:, 512:PW])
        both = turn(project[:, 0:256], cosine[begin : begin + rows, :], sine[begin : begin + rows, :])
        kv = jnp.concatenate([both[:, 64:256], project[:, 256:448]], axis=1).astype(bf16)
        for r in range(0, rows, 128):
            at = begin + r
            if at < WIN_S:
                kv_s[at : at + 128, :] = kv[r : r + 128, :]
            else:
                kv_t[at - WIN_S : at - WIN_S + 128, :] = kv[r : r + 128, :]
    own = SAME_CORE * ROWS
    x = window[own : own + ROWS, :].astype(f32)
    normed = (x * inverse_norm(x) * gain).astype(bf16)
    normed_out[...] = normed
    project = mm(normed, w_qkv[:, 0:640])
    q_out[...] = turn(project, cosine[own : own + ROWS, :], sine[own : own + ROWS, :])[
        :, 0:QW
    ].astype(bf16)


def heads_kernel(x_in, cosine, sine, gain_row, w_qkv, q_out, kv_out, normed_out):
    x = x_in[...]
    normed = (x * inverse_norm(x) * gain_row[:, 0:D]).astype(bf16)
    normed_out[...] = normed
    project = mm(normed, w_qkv[...])
    both = turn(project[:, 0:768], cosine[...], sine[...])
    q_out[...] = both[:, 0:QW].astype(bf16)
    kv_out[...] = jnp.concatenate([both[:, QW:768], project[:, 768:PW]], axis=1).astype(bf16)


def allowed_of(segment, key_row, first_row):
    query = first_row + lax.broadcasted_iota(jnp.int32, (ROWS, 1), 0)
    return (key_row >= segment) & (key_row <= query)


def group_rows(value, group):
    return jnp.concatenate(
        [value[:, (GROUP * group + n) * HD : (GROUP * group + n + 1) * HD] for n in range(GROUP)],
        axis=0,
    )


def window_rows(kv_s, kv_t, begin):
    return jnp.concatenate(
        [kv_s[:, begin : begin + HD], kv_t[:, begin : begin + HD]], axis=0
    )


def attend_kernel(
    first, x_in, q_in, kv_s, kv_t, segment, key_row, gain_row, w_out_at, w_in_at, w_down_at,
    x_out, mixed_out, lse_out, middle_out, normed_out, gate_up_out, hidden_out,
    w_out, w_in, w_down, sems,
):
    copies = fetch((w_out_at, w_in_at, w_down_at), (w_out, w_in, w_down), sems)
    for copy in copies:
        copy.start()
    allowed = allowed_of(segment[...], key_row[...], first[0])
    bias = jnp.where(allowed, 0.0, -1e30).astype(f32)
    bias = jnp.concatenate([bias] * GROUP, axis=0)
    q = q_in[...]
    pieces = []
    for group in range(KVH):
        keys = window_rows(kv_s, kv_t, group * HD)
        values = window_rows(kv_s, kv_t, KW + group * HD)
        scores = mm_t(group_rows(q, group), keys) * FACTOR + bias
        peak = jnp.max(scores, axis=-1, keepdims=True)
        powers = jnp.exp(scores - peak)
        total = jnp.sum(powers, axis=-1, keepdims=True)
        lse_out[:, group : group + 1] = peak + jnp.log(total)
        weights = (powers * (1.0 / total)).astype(bf16)
        mixed = mm(weights, values)
        for n in range(GROUP):
            pieces.append(mixed[n * ROWS : (n + 1) * ROWS, :])
    mixed = jnp.concatenate(pieces, axis=1).astype(bf16)
    mixed_out[...] = mixed
    copies[0].wait()
    middle = x_in[...].astype(f32) + mm(mixed, w_out[...])
    middle_out[...] = middle
    normed = (middle * inverse_norm(middle) * gain_row[:, 0:D]).astype(bf16)
    normed_out[...] = normed
    copies[1].wait()
    gate_up = mm(normed, w_in[...])
    gate_up_out[...] = gate_up
    gate = gate_up[:, 0:FF]
    hidden = (gate * jax.nn.sigmoid(gate) * gate_up[:, FF:]).astype(bf16)
    hidden_out[...] = hidden
    copies[2].wait()
    x_out[...] = middle + mm(hidden, w_down[...])


def norm_back(values, inverse, gain, grad):
    weighted = grad * gain
    return inverse * weighted - values * inverse**3 * jnp.mean(
        weighted * values, axis=-1, keepdims=True
    )


def back_kernel(
    first, g_in, q_in, kv_s, kv_t, segment, key_row, cosine, sine, gain_row, lse, middle_in,
    gate_up_at, w_out_at, w_in_at, w_down_at,
    branch_out, grad_gu_out, attn_out, middle_grad_out, dq_out, dkv_s, dkv_t, gain_out,
    w_out, w_in, w_down, sems, gate_up, gate_sem,
):
    copies = fetch((w_out_at, w_in_at, w_down_at), (w_out, w_in, w_down), sems)
    gate_copy = pltpu.make_async_copy(gate_up_at, gate_up, gate_sem)
    copies[2].start()
    gate_copy.start()
    copies[1].start()
    copies[0].start()
    allowed = allowed_of(segment[...], key_row[...], first[0])
    bias = jnp.where(allowed, 0.0, -1e30).astype(f32)
    bias = jnp.concatenate([bias] * GROUP, axis=0)
    q = q_in[...]
    held = []
    for group in range(KVH):
        keys = window_rows(kv_s, kv_t, group * HD)
        scores = mm_t(group_rows(q, group), keys) * FACTOR + bias
        held.append(jnp.exp(scores - lse[:, group : group + 1]))
    g = g_in[...].astype(f32)
    branch = g.astype(bf16)
    branch_out[...] = branch
    copies[2].wait()
    grad_hidden = mm_t(branch, w_down[...])
    gate_copy.wait()
    gate = gate_up[:, 0:FF]
    up = gate_up[:, FF:]
    sigma = jax.nn.sigmoid(gate)
    grad_gu_out[:, 0:FF] = (
        grad_hidden * up * sigma * (1.0 + gate * (1.0 - sigma))
    ).astype(bf16)
    grad_gu_out[:, FF:] = (grad_hidden * gate * sigma).astype(bf16)
    copies[1].wait()
    grad_two = mm_t(grad_gu_out[...], w_in[...])
    middle = middle_in[...]
    inverse = inverse_norm(middle)
    gain_out[...] = jnp.sum(grad_two * middle * inverse, axis=0, keepdims=True)
    grad_middle = g + norm_back(middle, inverse, gain_row[:, 0:D], grad_two)
    middle_grad_out[...] = grad_middle
    attn = grad_middle.astype(bf16)
    attn_out[...] = attn
    copies[0].wait()
    grad_mixed = mm_t(attn, w_out[...]).astype(bf16)

    dq, dk, dv = [], [], []
    for group in range(KVH):
        keys = window_rows(kv_s, kv_t, group * HD)
        values = window_rows(kv_s, kv_t, KW + group * HD)
        query = group_rows(q, group)
        grad = group_rows(grad_mixed, group)
        probs = held[group]
        grad_w = mm_t(grad, values)
        delta = jnp.sum(probs * grad_w, axis=-1, keepdims=True)
        grad_scores = (probs * (grad_w - delta)).astype(bf16)
        part = mm(grad_scores, keys) * FACTOR
        for n in range(GROUP):
            dq.append(part[n * ROWS : (n + 1) * ROWS, :])
        dk.append(mm(query.T, grad_scores) * FACTOR)
        dv.append(mm(grad.T, probs.astype(bf16)))
    dkv = jnp.concatenate(dk + dv, axis=0).T
    dkv_s[...] = dkv[0:WIN_S, :]
    dkv_t[...] = dkv[WIN_S:, :].astype(bf16)
    wide = jnp.concatenate(dq + [jnp.zeros((ROWS, HD), f32)], axis=1)
    dq_out[...] = turn(wide, cosine[...], -sine[...])[:, 0:QW].astype(bf16)


def back_heads_kernel(
    x_in, dq, own, r8, r6, r4, r2, cosine, sine, gain_row, w_qkv, middle_grad,
    g_out, project_out, gain_out,
):
    total = own[...]
    for piece in (r8, r6, r4, r2):
        total = total + piece[...].astype(f32)
    keys = jnp.concatenate([total[:, 0:KW], jnp.zeros((ROWS, HD), f32)], axis=1)
    keys = turn(keys, cosine[...], -sine[...])[:, 0:KW]
    project = jnp.concatenate(
        [dq[...].astype(f32), keys, total[:, KW:]], axis=1
    ).astype(bf16)
    project_out[...] = project
    grad = mm_t(project, w_qkv[...])
    x = x_in[...].astype(f32)
    inverse = inverse_norm(x)
    gain_out[...] = jnp.sum(grad * x * inverse, axis=0, keepdims=True)
    g_out[...] = middle_grad[...] + norm_back(x, inverse, gain_row[:, 0:D], grad)


def put_gain(flat, gain, start):
    row = jnp.concatenate([gain[...], jnp.zeros((1, 64), f32)], axis=1)
    first = start // 2
    before = None
    for t in range(5):
        part = row[:, 128 * t : 128 * t + 128]
        place = slice(first + t, first + t + 1)
        if start % 2 == 0:
            flat[place, :] = part
        else:
            now = pltpu.roll(part, 64, 1)
            if before is None:
                flat[place, :] = now
            else:
                flat[place, :] = jnp.where(low_half((1, 128)), before, now)
            before = now


def put_matrix(flat, tile, left, right, start_half, width_half):
    rows, columns = left.shape[1], right.shape[1]
    turned = left[...].T
    for t in range((width_half + 1) // 2):
        wide = min(128, columns - 128 * t)
        tile[t, 0:rows, 0:wide] = mm(turned, right[:, 128 * t : 128 * t + wide])
    for parity in range(2):
        put_rows(
            flat, start_half + parity * width_half, rows // 2, width_half,
            lambda t, parity=parity: tile[t, pl.ds(parity, rows // 2, stride=2), :],
        )


def cut(flat, core, first_plane, planes, skip, keep, send):
    last = lax.broadcasted_iota(jnp.int32, (CHUNK, 128), 0) == CHUNK - 1
    for out, flip in ((keep, 0), (send, 1)):
        def one_owner(k, carry, out=out, flip=flip):
            d = 2 * (first_plane + k) + lax.rem(core[0] + flip, 2)
            base = pl.multiple_of(d * 216 - skip + 8, 8)
            odd = jnp.where(d < DEVICES // 2, base - 1, base + CHUNK - 1)
            value = jnp.where(last, flat[pl.ds(odd, 1), :], flat[pl.ds(base, CHUNK), :])
            out[pl.ds(pl.multiple_of(k * CHUNK, CHUNK), CHUNK), :] = value.astype(bf16)
            return carry

        lax.fori_loop(0, planes, one_owner, 0)


def pack_rest_kernel(
    core, mixed, attn, normed_two, grad_gu, hidden, branch, gain_two, keep, send, edge, flat, tile
):
    skip = 216 * SPLIT
    half = 2 * (7 - skip)
    put_gain(flat, gain_two, HALF_GAIN_TWO + half)
    put_matrix(flat, tile, mixed, attn, HALF_OUT + half, D // 64)
    put_matrix(flat, tile, hidden, branch, HALF_DOWN + half, D // 64)

    turned = normed_two[...].T

    def in_tile(c, carry):
        flat[pl.ds((HALF_IN + half) // 2 + c, D, stride=24), :] = mm(
            turned, grad_gu[:, pl.ds(pl.multiple_of(c * 128, 128), 128)]
        )
        return carry

    lax.fori_loop(0, 24, in_tile, 0)
    cut(flat, core, LOW_PLANES, DEVICES // 2 - LOW_PLANES, skip, keep, send)
    edge[...] = flat[0:EDGE, :]


def pack_first_kernel(core, normed, project, gain_one, edge, keep, send, flat, tile):
    skip = 216 * SPLIT
    flat[skip : skip + EDGE, :] = edge[...]
    put_gain(flat, gain_one, HALF_GAIN_ONE + 14)
    put_matrix(flat, tile, normed, project, HALF_QKV + 14, PW // 64)
    cut(flat, core, 0, LOW_PLANES, 0, keep, send)


def hop(value, by):
    pairs = [(i, i + by) for i in range(DEVICES) if 0 <= i + by < DEVICES]
    return lax.ppermute(value, "fsdp", pairs)


def swap(value):
    return lax.ppermute(value, "fsdp", [(i, i ^ 1) for i in range(DEVICES)])


def window_of(value, core, beside=()):
    blocks = [hop(value, by) for by in (8, 6, 4, 2)] + [value]
    same = jnp.concatenate(blocks, axis=0)
    rows = value.shape[0]
    gift = lax.dynamic_slice_in_dim(same, (1 - core) * rows, SAME_CORE * rows, 0)
    if beside:
        gift, _ = lax.optimization_barrier((gift, beside))
    return same, swap(gift)


def give_back(dkv_s, dkv_t, core):
    got = swap(dkv_t).astype(f32)
    blank = jnp.zeros((ROWS, 2 * KW), f32)
    early = jnp.concatenate([got, blank], axis=0)
    late = jnp.concatenate([blank, got], axis=0)
    total = dkv_s + jnp.where(core == 0, late, early)
    pieces = [
        hop(total[at * ROWS : (at + 1) * ROWS].astype(bf16), -by)
        for at, by in enumerate((8, 6, 4, 2))
    ]
    return total[SAME_CORE * ROWS :], pieces


def join_kernel(keep_first, got_first, keep_rest, got_rest, out):
    low = LOW_PLANES // JOIN

    @pl.when(pl.program_id(0) < low)
    def _():
        out[...] = (keep_first[...].astype(f32) + got_first[...].astype(f32)).astype(bf16)

    @pl.when(pl.program_id(0) >= low)
    def _():
        out[...] = (keep_rest[...].astype(f32) + got_rest[...].astype(f32)).astype(bf16)


def join(keep_first, got_first, keep_rest, got_rest):
    low = LOW_PLANES // JOIN
    block = (JOIN * CHUNK, 128)
    first = pl.BlockSpec(block, lambda i: (jnp.minimum(i, low - 1), 0))
    rest = pl.BlockSpec(block, lambda i: (jnp.maximum(i - low, 0), 0))
    return pl.pallas_call(
        join_kernel,
        grid=(DEVICES // 2 // JOIN,),
        out_shape=jax.ShapeDtypeStruct((DEVICES // 2 * CHUNK, 128), bf16),
        in_specs=[first, first, rest, rest],
        out_specs=pl.BlockSpec(block, lambda i: (i, 0)),
        compiler_params=pltpu.CompilerParams(vmem_limit_bytes=16 * 1024 * 1024),
        cost_estimate=pl.CostEstimate(flops=0, bytes_accessed=11_000_000, transcendentals=0),
    )(keep_first, got_first, keep_rest, got_rest)


def to_owners(total, device):
    total = total.reshape(DEVICES // 2, CHUNK, 128)
    groups = [list(range(0, DEVICES, 2)), list(range(1, DEVICES, 2))]
    pieces = lax.all_to_all(
        total, "fsdp", split_axis=0, concat_axis=0, tiled=True, axis_index_groups=groups
    )
    own = jnp.sum(pieces.astype(f32), axis=0)
    rows = jnp.concatenate([own[CHUNK - 1 :], own], axis=0)
    return lax.dynamic_slice_in_dim(rows.reshape(-1), 9 * device, SHARD, 0)


def tables(positions):
    half = HD // 2
    frequency = rope_base ** (-jnp.arange(half, dtype=f32) / half)
    angles = positions.astype(f32)[:, None] * frequency[None, :]
    return (
        jnp.concatenate([jnp.cos(angles)] * 4, axis=-1),
        jnp.concatenate([jnp.sin(angles)] * 4, axis=-1),
    )


def body(hidden_in, segment_ids, weights_flat, cotangent):
    device = lax.axis_index("fsdp")
    core = lax.rem(device, 2)
    first_row = device * ROWS
    layers = weights_flat.shape[0]
    sections = []
    for layer in range(layers):
        blank = jnp.zeros((SECTION * 128,), bf16)
        sections.append(lax.dynamic_update_slice(blank, weights_flat[layer], (9 * device,)))
    gathered = lax.all_gather(jnp.concatenate(sections), "fsdp", axis=0, tiled=True)
    gathered = gathered.reshape(DEVICES, layers, SECTION, 128)

    x_same, x_sibling = window_of(hidden_in, core)
    window = jnp.concatenate([x_same, x_sibling], axis=0)
    s_same, s_sibling = window_of(segment_ids, core)
    segments = jnp.concatenate([s_same, s_sibling], axis=0)
    order = jnp.arange(ROWS, dtype=jnp.int32)
    same_first = first_row - ROWS * jnp.array([8, 6, 4, 2, 0], jnp.int32)
    sibling_first = first_row - ROWS * jnp.array([7, 5, 3, 1], jnp.int32)
    key_row = jnp.concatenate([same_first, sibling_first])[:, None] + order[None, :]
    key_row = key_row.reshape(-1)
    cosine_all, sine_all = tables(key_row - segments)
    own = SAME_CORE * ROWS
    cosine, sine = cosine_all[own : own + ROWS], sine_all[own : own + ROWS]
    key_row = key_row[None, :]
    segment = segment_ids[:, None]
    first = first_row[None]
    core_in = core[None]

    x = hidden_in
    held = []
    for layer in range(layers):
        w_qkv, gain_one = unpack_first(gathered, layer)
        w_out, w_in, w_down, gain_two = unpack_rest(gathered, layer)
        if layer == 0:
            q, kv_s, kv_t, normed = call(
                heads_zero_kernel,
                [((ROWS, QW), bf16), ((WIN_S, 2 * KW), bf16), ((WIN_T, 2 * KW), bf16),
                 ((ROWS, D), bf16)],
                [window, cosine_all, sine_all, gain_one, w_qkv],
                flops=800_000_000, nbytes=6_000_000,
            )
        else:
            q, kv, normed = call(
                heads_kernel,
                [((ROWS, QW), bf16), ((ROWS, 2 * KW), bf16), ((ROWS, D), bf16)],
                [x, cosine, sine, gain_one, w_qkv],
                flops=150_000_000, nbytes=3_000_000,
            )
            kv_s, kv_t = window_of(kv, core, (w_out,))
        x_next, mixed, lse, middle, normed_two, gate_up, hidden = call(
            attend_kernel,
            [((ROWS, D), f32), ((ROWS, QW), bf16), ((GROUP * ROWS, KVH), f32), ((ROWS, D), f32),
             ((ROWS, D), bf16), ((ROWS, 2 * FF), f32), ((ROWS, FF), bf16)],
            [first, x, q, kv_s, kv_t, segment, key_row, gain_two, w_out, w_in, w_down],
            scratch=WEIGHT_SCRATCH, smem=1, apart=3, flops=2_000_000_000, nbytes=12_000_000,
        )
        held.append((x, q, kv_s, kv_t, normed, mixed, lse, middle, normed_two, gate_up, hidden,
                     w_qkv, w_out, w_in, w_down, gain_one, gain_two))
        x = x_next
    layer_out = x.astype(bf16)

    g = cotangent
    grads = [None] * layers
    for layer in reversed(range(layers)):
        (x, q, kv_s, kv_t, normed, mixed, lse, middle, normed_two, gate_up, hidden,
         w_qkv, w_out, w_in, w_down, gain_one, gain_two) = held[layer]
        branch, grad_gu, attn, middle_grad, dq, dkv_s, dkv_t, grad_two = call(
            back_kernel,
            [((ROWS, D), bf16), ((ROWS, 2 * FF), bf16), ((ROWS, D), bf16), ((ROWS, D), f32),
             ((ROWS, QW), bf16), ((WIN_S, 2 * KW), f32), ((WIN_T, 2 * KW), bf16), ((1, D), f32)],
            [first, g, q, kv_s, kv_t, segment, key_row, cosine, sine, gain_two, lse, middle,
             gate_up, w_out, w_in, w_down],
            scratch=WEIGHT_SCRATCH
            + (pltpu.VMEM((ROWS, 2 * FF), f32), pltpu.SemaphoreType.DMA),
            smem=1, apart=4, flops=3_000_000_000, nbytes=15_000_000,
        )
        rest_shape = (((DEVICES // 2 - LOW_PLANES) * CHUNK, 128), bf16)
        keep, send, edge = call(
            pack_rest_kernel,
            [rest_shape, rest_shape, ((EDGE, 128), f32)],
            [core_in, mixed, attn, normed_two, grad_gu, hidden, branch, grad_two],
            scratch=[
                pltpu.VMEM((216 * (DEVICES - SPLIT) + 40, 128), f32), pltpu.VMEM((5, FF, 128), f32)
            ],
            smem=1, flops=1_000_000_000, nbytes=25_000_000,
        )
        own_kv, pieces = give_back(dkv_s, dkv_t, core)
        send, pieces = lax.optimization_barrier((send, pieces))
        keep_rest, got_rest = keep, swap(send)
        g, project, grad_one = call(
            back_heads_kernel,
            [((ROWS, D), f32), ((ROWS, PW), bf16), ((1, D), f32)],
            [x, dq, own_kv, *pieces, cosine, sine, gain_one, w_qkv, middle_grad],
            flops=150_000_000, nbytes=3_000_000,
        )
        if layer + 1 < layers:
            project, grads[layer + 1] = lax.optimization_barrier((project, grads[layer + 1]))
        low_shape = ((LOW_PLANES * CHUNK, 128), bf16)
        keep, send = call(
            pack_first_kernel,
            [low_shape, low_shape],
            [core_in, normed, project, grad_one, edge],
            scratch=[
                pltpu.VMEM((216 * SPLIT + EDGE + 8, 128), f32), pltpu.VMEM((8, D, 128), f32)
            ],
            smem=1, flops=200_000_000, nbytes=8_000_000,
        )
        total = join(keep, swap(send), keep_rest, got_rest)
        if layer > 0:
            g, total = lax.optimization_barrier((g, total))
        grads[layer] = to_owners(total, device)
    return (layer_out, g, jnp.stack(grads))


def solution(mesh):
    in_specs = (P("fsdp", None), P("fsdp"), P(None, "fsdp"), P("fsdp", None))
    out_specs = (P("fsdp", None), P("fsdp", None), P(None, "fsdp"))
    return jax.shard_map(body, mesh=mesh, in_specs=in_specs, out_specs=out_specs, check_vma=False)
```

```python
import functools

import jax
import jax.numpy as jnp
from jax import lax
from jax.experimental import pallas as pl
from jax.experimental.pallas import tpu as pltpu
from jax.sharding import PartitionSpec as P

D = 576
FF = 1536
QH = 9
KVH = 3
HD = 64
MAXLEN = 1024
QW = QH * HD
KW = KVH * HD
PW = QW + 2 * KW
GROUP = QH // KVH
DEVICES = 128
ROWS = 128
PARAMS = 3540096
SHARD = PARAMS // DEVICES
CHUNK = 224
SECTION = 240
SPLIT = 20
FIRST = 22
LOW_PLANES = 16
JOIN = 8
EDGE = 2616
SAME_CORE = 4
WIN_S = (SAME_CORE + 1) * ROWS
WIN_T = SAME_CORE * ROWS
WIN = WIN_S + WIN_T

bf16 = jnp.bfloat16
f32 = jnp.float32
epsilon = 1e-05
rope_base = 10000.0
FACTOR = HD ** (-0.5)
VMEM_LIMIT = 60 * 1024 * 1024

HALF_GAIN_ONE = 0
HALF_QKV = D // 64
HALF_OUT = HALF_QKV + D * PW // 64
HALF_GAIN_TWO = HALF_OUT + QW * D // 64
HALF_IN = HALF_GAIN_TWO + D // 64
HALF_DOWN = HALF_IN + D * 2 * FF // 64


def mm(a, b):
    return lax.dot_general(a, b, (((1,), (0,)), ((), ())), preferred_element_type=f32)


def mm_t(a, b):
    return lax.dot_general(a, b, (((1,), (1,)), ((), ())), preferred_element_type=f32)


def t_mm(a, b):
    return lax.dot_general(a, b, (((0,), (0,)), ((), ())), preferred_element_type=f32)


def call(kernel, out_shape, args, scratch=(), smem=0, apart=0, flops=0, nbytes=0):
    in_specs = [
        pl.BlockSpec(
            memory_space=pltpu.SMEM if at < smem
            else pl.ANY if at >= len(args) - apart else pltpu.VMEM
        )
        for at in range(len(args))
    ]
    return pl.pallas_call(
        kernel,
        out_shape=[jax.ShapeDtypeStruct(s, d) for s, d in out_shape],
        in_specs=in_specs,
        out_specs=[pl.BlockSpec(memory_space=pltpu.VMEM) for _ in out_shape],
        scratch_shapes=list(scratch),
        compiler_params=pltpu.CompilerParams(vmem_limit_bytes=VMEM_LIMIT),
        cost_estimate=pl.CostEstimate(flops=flops, bytes_accessed=nbytes, transcendentals=0),
    )(*args)


def low_half(shape):
    return lax.broadcasted_iota(jnp.int32, shape, 1) < 64


def take_rows(flat, start_half, pairs, width_half, store):
    tiles = (width_half + 1) // 2
    if start_half % 2 == 0:
        for t in range(tiles):
            store(t, flat[pl.ds(start_half // 2 + t, pairs, stride=width_half), :])
    else:
        before = None
        for t in range(tiles + 1):
            if t == tiles and width_half % 2 == 1:
                store(t - 1, before)
                break
            now = pltpu.roll(flat[pl.ds(start_half // 2 + t, pairs, stride=width_half), :], 64, 1)
            if before is not None:
                store(t - 1, jnp.where(low_half(now.shape), before, now))
            before = now


def put_rows(flat, start_half, pairs, width_half, load):
    tiles = (width_half + 1) // 2
    if start_half % 2 == 0:
        for t in range(tiles):
            place = pl.ds(start_half // 2 + t, pairs, stride=width_half)
            value = load(t)
            if 2 * t + 1 == width_half:
                value = jnp.where(low_half(value.shape), value, flat[place, :])
            flat[place, :] = value
    else:
        before = None
        for t in range(tiles + 1):
            if t == tiles and width_half % 2 == 1:
                break
            place = pl.ds(start_half // 2 + t, pairs, stride=width_half)
            now = pltpu.roll(load(t), 64, 1) if t < tiles else None
            if before is None:
                value = jnp.where(low_half(now.shape), flat[place, :], now)
            else:
                value = jnp.where(low_half(before.shape), before, now)
            flat[place, :] = value
            before = now


WEIGHT_SCRATCH = (
    pltpu.VMEM((QW, D), bf16),
    pltpu.VMEM((D, 2 * FF), bf16),
    pltpu.VMEM((FF, D), bf16),
    pltpu.SemaphoreType.DMA((3,)),
)


def fetch(sources, places, sems):
    copies = [
        pltpu.make_async_copy(source, place, sems.at[n])
        for n, (source, place) in enumerate(zip(sources, places))
    ]
    return copies


def gather_flat(core, sources, first, count, groups, flat, landing, sems):
    size = count // 2 // groups
    copies = []
    for n in range(groups):
        rows = pl.ds(first // 2 + n * size, size)
        places = pl.ds(n * size, size)
        if len(sources) == 1:
            group = [pltpu.make_async_copy(sources[0].at[rows], landing.at[places], sems.at[n, 0])]
        else:
            group = [
                pltpu.make_async_copy(
                    source.at[rows], landing.at[places, lax.rem(core[0] + at, 2)], sems.at[n, at]
                )
                for at, source in enumerate(sources)
            ]
        for copy in group:
            copy.start()
        copies.append(group)
    tail = jnp.zeros((SECTION - 216, 128), f32)
    for n in range(groups):
        for copy in copies[n]:
            copy.wait()

        def one_pair(k, tail):
            for side in range(2):
                rows = landing[k, side].astype(f32)
                base = pl.multiple_of(k * 432 + side * 216, 8)
                flat[pl.ds(base, 24), :] = tail + rows[0:24, :]
                flat[pl.ds(base + 24, 192), :] = rows[24:216, :]
                tail = rows[216:SECTION, :]
            return tail

        tail = lax.fori_loop(n * size, (n + 1) * size, one_pair, tail)
    flat[count * 216 : count * 216 + 24, :] = tail


def take_matrix(flat, tile, out, start_half, width_half):
    rows, columns = out.shape

    def store(parity, at, value):
        tile[at, pl.ds(parity, rows // 2, stride=2), :] = value

    for parity in range(2):
        take_rows(
            flat, start_half + parity * width_half, rows // 2, width_half,
            functools.partial(store, parity),
        )
    for t in range((width_half + 1) // 2):
        wide = min(128, columns - 128 * t)
        out[:, 128 * t : 128 * t + wide] = tile[t, 0:rows, 0:wide].astype(bf16)


def take_gain(flat, gain, start):
    first = start // 2
    for t in range(5):
        if start % 2 == 0:
            value = flat[first + t : first + t + 1, :]
        else:
            here = pltpu.roll(flat[first + t : first + t + 1, :], 64, 1)
            after = pltpu.roll(flat[first + t + 1 : first + t + 2, :], 64, 1)
            value = jnp.where(low_half((1, 128)), here, after)
        gain[0:1, 128 * t : 128 * t + 128] = value


def unpack_first_kernel(parts, core, *refs):
    sources, (w_qkv, gain, landing, flat, tile, sems) = refs[:parts], refs[parts:]
    gather_flat(core, sources, 0, FIRST, 1, flat, landing, sems)
    take_gain(flat, gain, HALF_GAIN_ONE)
    take_matrix(flat, tile, w_qkv, HALF_QKV, PW // 64)


def unpack_rest_kernel(parts, core, *refs):
    sources = refs[:parts]
    (w_out_at, w_in_at, w_down_at, gain, landing, flat, tile, sems,
     w_out, w_in, w_down, out_sems) = refs[parts:]
    gather_flat(core, sources, SPLIT, DEVICES - SPLIT, 3, flat, landing, sems)
    skip = 2 * 216 * SPLIT

    def in_tile(c, carry):
        w_in[:, pl.ds(pl.multiple_of(c * 128, 128), 128)] = flat[
            pl.ds((HALF_IN - skip) // 2 + c, D, stride=24), :
        ].astype(bf16)
        return carry

    lax.fori_loop(0, 24, in_tile, 0)
    copies = fetch((w_out, w_in, w_down), (w_out_at, w_in_at, w_down_at), out_sems)
    copies[1].start()
    take_matrix(flat, tile, w_down, HALF_DOWN - skip, D // 64)
    copies[2].start()
    take_matrix(flat, tile, w_out, HALF_OUT - skip, D // 64)
    copies[0].start()
    take_gain(flat, gain, HALF_GAIN_TWO - skip)
    for copy in copies:
        copy.wait()


def unpack_call(kernel, out_shape, core, sources, count, groups, tiles, nbytes, apart=0, scratch=()):
    return pl.pallas_call(
        functools.partial(kernel, len(sources)),
        out_shape=[jax.ShapeDtypeStruct(s, d) for s, d in out_shape],
        in_specs=[pl.BlockSpec(memory_space=pltpu.SMEM)]
        + [pl.BlockSpec(memory_space=pl.ANY) for _ in sources],
        out_specs=[
            pl.BlockSpec(memory_space=pl.ANY if at < apart else pltpu.VMEM)
            for at in range(len(out_shape))
        ],
        scratch_shapes=[
            pltpu.VMEM((count // 2, 2, SECTION, 128), bf16),
            pltpu.VMEM((count * 216 + 32, 128), f32),
            pltpu.VMEM(tiles, f32),
            pltpu.SemaphoreType.DMA((groups, 2)),
            *scratch,
        ],
        compiler_params=pltpu.CompilerParams(vmem_limit_bytes=VMEM_LIMIT),
        cost_estimate=pl.CostEstimate(
            flops=2_000_000_000, bytes_accessed=nbytes, transcendentals=0
        ),
    )(core, *sources)


def unpack_first(core, sources):
    return unpack_call(
        unpack_first_kernel, [((D, PW), bf16), ((1, 640), f32)], core, sources,
        FIRST, 1, (8, D, 128), 9_000_000,
    )


def unpack_rest(core, sources):
    return unpack_call(
        unpack_rest_kernel,
        [((QW, D), bf16), ((D, 2 * FF), bf16), ((FF, D), bf16), ((1, 640), f32)], core, sources,
        DEVICES - SPLIT, 3, (5, FF, 128), 30_000_000, apart=3, scratch=WEIGHT_SCRATCH,
    )


def turn(value, cosine, sine):
    lane = lax.broadcasted_iota(jnp.int32, (value.shape[0], 128), 1)
    first = lax.rem(lane, 64) < 32
    pieces = []
    for t in range(value.shape[1] // 128):
        part = value[:, 128 * t : 128 * t + 128]
        swapped = jnp.where(first, -pltpu.roll(part, 96, 1), pltpu.roll(part, 32, 1))
        pieces.append(part * cosine + swapped * sine)
    return jnp.concatenate(pieces, axis=1)


def inverse_norm(values):
    return lax.rsqrt(jnp.mean(values * values, axis=-1, keepdims=True) + epsilon)


def heads_zero_kernel(window, cosine, sine, gain_row, w_qkv, q_out, kv_s, kv_t, normed_out):
    gain = gain_row[:, 0:D]
    for begin, rows in ((0, 384), (384, 384), (768, 384)):
        x = window[begin : begin + rows, :].astype(f32)
        normed = (x * inverse_norm(x) * gain).astype(bf16)
        project = mm(normed, w_qkv[:, 512:PW])
        both = turn(project[:, 0:256], cosine[begin : begin + rows, :], sine[begin : begin + rows, :])
        kv = jnp.concatenate([both[:, 64:256], project[:, 256:448]], axis=1).astype(bf16)
        for r in range(0, rows, 128):
            at = begin + r
            if at < WIN_S:
                kv_s[at : at + 128, :] = kv[r : r + 128, :]
            else:
                kv_t[at - WIN_S : at - WIN_S + 128, :] = kv[r : r + 128, :]
    own = SAME_CORE * ROWS
    x = window[own : own + ROWS, :].astype(f32)
    normed = (x * inverse_norm(x) * gain).astype(bf16)
    normed_out[...] = normed
    project = mm(normed, w_qkv[:, 0:640])
    q_out[...] = turn(project, cosine[own : own + ROWS, :], sine[own : own + ROWS, :])[
        :, 0:QW
    ].astype(bf16)


def heads_kernel(x_in, cosine, sine, gain_row, w_qkv, q_out, kv_out, normed_out):
    x = x_in[...]
    normed = (x * inverse_norm(x) * gain_row[:, 0:D]).astype(bf16)
    normed_out[...] = normed
    project = mm(normed, w_qkv[...])
    both = turn(project[:, 0:768], cosine[...], sine[...])
    q_out[...] = both[:, 0:QW].astype(bf16)
    kv_out[...] = jnp.concatenate([both[:, QW:768], project[:, 768:PW]], axis=1).astype(bf16)


def allowed_of(segment, key_row, first_row):
    query = first_row + lax.broadcasted_iota(jnp.int32, (ROWS, 1), 0)
    return (key_row >= segment) & (key_row <= query)


def group_rows(value, group):
    return jnp.concatenate(
        [value[:, (GROUP * group + n) * HD : (GROUP * group + n + 1) * HD] for n in range(GROUP)],
        axis=0,
    )


def window_rows(kv_s, kv_t, begin):
    return jnp.concatenate(
        [kv_s[:, begin : begin + HD], kv_t[:, begin : begin + HD]], axis=0
    )


def attend_kernel(
    first, x_in, q_in, kv_s, kv_t, segment, key_row, gain_row, w_out_at, w_in_at, w_down_at,
    x_out, mixed_out, lse_out, middle_out, normed_out, gate_up_out, hidden_out,
    w_out, w_in, w_down, sems,
):
    copies = fetch((w_out_at, w_in_at, w_down_at), (w_out, w_in, w_down), sems)
    for copy in copies:
        copy.start()
    allowed = allowed_of(segment[...], key_row[...], first[0])
    bias = jnp.where(allowed, 0.0, -1e30).astype(f32)
    bias = jnp.concatenate([bias] * GROUP, axis=0)
    q = q_in[...]
    pieces = []
    for group in range(KVH):
        keys = window_rows(kv_s, kv_t, group * HD)
        values = window_rows(kv_s, kv_t, KW + group * HD)
        scores = mm_t(group_rows(q, group), keys) * FACTOR + bias
        peak = jnp.max(scores, axis=-1, keepdims=True)
        powers = jnp.exp(scores - peak)
        total = jnp.sum(powers, axis=-1, keepdims=True)
        lse_out[:, group : group + 1] = peak + jnp.log(total)
        weights = (powers * (1.0 / total)).astype(bf16)
        mixed = mm(weights, values)
        for n in range(GROUP):
            pieces.append(mixed[n * ROWS : (n + 1) * ROWS, :])
    mixed = jnp.concatenate(pieces, axis=1).astype(bf16)
    mixed_out[...] = mixed
    copies[0].wait()
    middle = x_in[...].astype(f32) + mm(mixed, w_out[...])
    middle_out[...] = middle
    normed = (middle * inverse_norm(middle) * gain_row[:, 0:D]).astype(bf16)
    normed_out[...] = normed
    copies[1].wait()
    gate_up = mm(normed, w_in[...])
    gate_up_out[...] = gate_up
    gate = gate_up[:, 0:FF]
    hidden = (gate * jax.nn.sigmoid(gate) * gate_up[:, FF:]).astype(bf16)
    hidden_out[...] = hidden
    copies[2].wait()
    x_out[...] = middle + mm(hidden, w_down[...])


def norm_back(values, inverse, gain, grad):
    weighted = grad * gain
    return inverse * weighted - values * inverse**3 * jnp.mean(
        weighted * values, axis=-1, keepdims=True
    )


def back_kernel(
    first, g_in, q_in, kv_s, kv_t, segment, key_row, cosine, sine, gain_row, lse, middle_in,
    gate_up_at, w_out_at, w_in_at, w_down_at,
    branch_out, grad_gu_out, attn_out, middle_grad_out, dq_out, dkv_s, dkv_t, gain_out,
    w_out, w_in, w_down, sems, gate_up, gate_sem,
):
    copies = fetch((w_out_at, w_in_at, w_down_at), (w_out, w_in, w_down), sems)
    gate_copy = pltpu.make_async_copy(gate_up_at, gate_up, gate_sem)
    copies[2].start()
    gate_copy.start()
    copies[1].start()
    copies[0].start()
    allowed = allowed_of(segment[...], key_row[...], first[0])
    bias = jnp.where(allowed, 0.0, -1e30).astype(f32)
    bias = jnp.concatenate([bias] * GROUP, axis=0)
    q = q_in[...]
    held = []
    for group in range(KVH):
        keys = window_rows(kv_s, kv_t, group * HD)
        scores = mm_t(group_rows(q, group), keys) * FACTOR + bias
        held.append(jnp.exp(scores - lse[:, group : group + 1]))
    g = g_in[...].astype(f32)
    branch = g.astype(bf16)
    branch_out[...] = branch
    copies[2].wait()
    grad_hidden = mm_t(branch, w_down[...])
    gate_copy.wait()
    gate = gate_up[:, 0:FF]
    up = gate_up[:, FF:]
    sigma = jax.nn.sigmoid(gate)
    grad_gu_out[:, 0:FF] = (
        grad_hidden * up * sigma * (1.0 + gate * (1.0 - sigma))
    ).astype(bf16)
    grad_gu_out[:, FF:] = (grad_hidden * gate * sigma).astype(bf16)
    copies[1].wait()
    grad_two = mm_t(grad_gu_out[...], w_in[...])
    middle = middle_in[...]
    inverse = inverse_norm(middle)
    gain_out[...] = jnp.sum(grad_two * middle * inverse, axis=0, keepdims=True)
    grad_middle = g + norm_back(middle, inverse, gain_row[:, 0:D], grad_two)
    middle_grad_out[...] = grad_middle
    attn = grad_middle.astype(bf16)
    attn_out[...] = attn
    copies[0].wait()
    grad_mixed = mm_t(attn, w_out[...]).astype(bf16)

    dq, dk, dv = [], [], []
    for group in range(KVH):
        keys = window_rows(kv_s, kv_t, group * HD)
        values = window_rows(kv_s, kv_t, KW + group * HD)
        query = group_rows(q, group)
        grad = group_rows(grad_mixed, group)
        probs = held[group]
        grad_w = mm_t(grad, values)
        delta = jnp.sum(probs * grad_w, axis=-1, keepdims=True)
        grad_scores = (probs * (grad_w - delta)).astype(bf16)
        part = mm(grad_scores, keys) * FACTOR
        for n in range(GROUP):
            dq.append(part[n * ROWS : (n + 1) * ROWS, :])
        dk.append(mm(query.T, grad_scores) * FACTOR)
        dv.append(mm(grad.T, probs.astype(bf16)))
    dkv = jnp.concatenate(dk + dv, axis=0).T
    dkv_s[...] = dkv[0:WIN_S, :]
    dkv_t[...] = dkv[WIN_S:, :].astype(bf16)
    wide = jnp.concatenate(dq + [jnp.zeros((ROWS, HD), f32)], axis=1)
    dq_out[...] = turn(wide, cosine[...], -sine[...])[:, 0:QW].astype(bf16)


def back_heads_kernel(
    x_in, dq, own, r8, r6, r4, r2, cosine, sine, gain_row, w_qkv, middle_grad,
    g_out, project_out, gain_out,
):
    total = own[...]
    for piece in (r8, r6, r4, r2):
        total = total + piece[...].astype(f32)
    keys = jnp.concatenate([total[:, 0:KW], jnp.zeros((ROWS, HD), f32)], axis=1)
    keys = turn(keys, cosine[...], -sine[...])[:, 0:KW]
    project = jnp.concatenate(
        [dq[...].astype(f32), keys, total[:, KW:]], axis=1
    ).astype(bf16)
    project_out[...] = project
    grad = mm_t(project, w_qkv[...])
    x = x_in[...].astype(f32)
    inverse = inverse_norm(x)
    gain_out[...] = jnp.sum(grad * x * inverse, axis=0, keepdims=True)
    g_out[...] = middle_grad[...] + norm_back(x, inverse, gain_row[:, 0:D], grad)


def put_gain(flat, gain, start):
    row = jnp.concatenate([gain[...], jnp.zeros((1, 64), f32)], axis=1)
    first = start // 2
    before = None
    for t in range(5):
        part = row[:, 128 * t : 128 * t + 128]
        place = slice(first + t, first + t + 1)
        if start % 2 == 0:
            flat[place, :] = part
        else:
            now = pltpu.roll(part, 64, 1)
            if before is None:
                flat[place, :] = now
            else:
                flat[place, :] = jnp.where(low_half((1, 128)), before, now)
            before = now


def put_matrix(flat, tile, left, right, start_half, width_half):
    rows, columns = left.shape[1], right.shape[1]
    turned = left[...].T
    for t in range((width_half + 1) // 2):
        wide = min(128, columns - 128 * t)
        tile[t, 0:rows, 0:wide] = mm(turned, right[:, 128 * t : 128 * t + wide])
    for parity in range(2):
        put_rows(
            flat, start_half + parity * width_half, rows // 2, width_half,
            lambda t, parity=parity: tile[t, pl.ds(parity, rows // 2, stride=2), :],
        )


def cut(flat, core, first_plane, planes, skip, keep, send):
    last = lax.broadcasted_iota(jnp.int32, (CHUNK, 128), 0) == CHUNK - 1
    for out, flip in ((keep, 0), (send, 1)):
        def one_owner(k, carry, out=out, flip=flip):
            d = 2 * (first_plane + k) + lax.rem(core[0] + flip, 2)
            base = pl.multiple_of(d * 216 - skip + 8, 8)
            odd = jnp.where(d < DEVICES // 2, base - 1, base + CHUNK - 1)
            value = jnp.where(last, flat[pl.ds(odd, 1), :], flat[pl.ds(base, CHUNK), :])
            out[pl.ds(pl.multiple_of(k * CHUNK, CHUNK), CHUNK), :] = value.astype(bf16)
            return carry

        lax.fori_loop(0, planes, one_owner, 0)


def pack_rest_kernel(
    core, mixed, attn, normed_two, grad_gu, hidden, branch, gain_two, keep, send, edge, flat, tile
):
    skip = 216 * SPLIT
    half = 2 * (7 - skip)
    put_gain(flat, gain_two, HALF_GAIN_TWO + half)
    put_matrix(flat, tile, mixed, attn, HALF_OUT + half, D // 64)
    put_matrix(flat, tile, hidden, branch, HALF_DOWN + half, D // 64)

    turned = normed_two[...].T

    def in_tile(c, carry):
        flat[pl.ds((HALF_IN + half) // 2 + c, D, stride=24), :] = mm(
            turned, grad_gu[:, pl.ds(pl.multiple_of(c * 128, 128), 128)]
        )
        return carry

    lax.fori_loop(0, 24, in_tile, 0)
    cut(flat, core, LOW_PLANES, DEVICES // 2 - LOW_PLANES, skip, keep, send)
    edge[...] = flat[0:EDGE, :]


def pack_first_kernel(core, normed, project, gain_one, edge, keep, send, flat, tile):
    skip = 216 * SPLIT
    flat[skip : skip + EDGE, :] = edge[...]
    put_gain(flat, gain_one, HALF_GAIN_ONE + 14)
    put_matrix(flat, tile, normed, project, HALF_QKV + 14, PW // 64)
    cut(flat, core, 0, LOW_PLANES, 0, keep, send)


def hop(value, by):
    pairs = [(i, i + by) for i in range(DEVICES) if 0 <= i + by < DEVICES]
    return lax.ppermute(value, "fsdp", pairs)


def swap(value):
    return lax.ppermute(value, "fsdp", [(i, i ^ 1) for i in range(DEVICES)])


def window_of(value, core, beside=()):
    blocks = [hop(value, by) for by in (8, 6, 4, 2)] + [value]
    same = jnp.concatenate(blocks, axis=0)
    rows = value.shape[0]
    gift = lax.dynamic_slice_in_dim(same, (1 - core) * rows, SAME_CORE * rows, 0)
    if beside:
        gift, _ = lax.optimization_barrier((gift, beside))
    return same, swap(gift)


def give_back(dkv_s, dkv_t, core):
    got = swap(dkv_t).astype(f32)
    blank = jnp.zeros((ROWS, 2 * KW), f32)
    early = jnp.concatenate([got, blank], axis=0)
    late = jnp.concatenate([blank, got], axis=0)
    total = dkv_s + jnp.where(core == 0, late, early)
    pieces = [
        hop(total[at * ROWS : (at + 1) * ROWS].astype(bf16), -by)
        for at, by in enumerate((8, 6, 4, 2))
    ]
    return total[SAME_CORE * ROWS :], pieces


def spread(blocks):
    groups = [list(range(0, DEVICES, 2)), list(range(1, DEVICES, 2))]
    return lax.all_to_all(
        blocks, "fsdp", split_axis=0, concat_axis=0, tiled=True, axis_index_groups=groups
    )


def join_kernel(keep_first, got_first, keep_rest, got_rest, out):
    low = LOW_PLANES // JOIN

    @pl.when(pl.program_id(0) < low)
    def _():
        out[...] = (keep_first[...].astype(f32) + got_first[...].astype(f32)).astype(bf16)

    @pl.when(pl.program_id(0) >= low)
    def _():
        out[...] = (keep_rest[...].astype(f32) + got_rest[...].astype(f32)).astype(bf16)


def join(keep_first, got_first, keep_rest, got_rest):
    low = LOW_PLANES // JOIN
    block = (JOIN * CHUNK, 128)
    first = pl.BlockSpec(block, lambda i: (jnp.minimum(i, low - 1), 0))
    rest = pl.BlockSpec(block, lambda i: (jnp.maximum(i - low, 0), 0))
    return pl.pallas_call(
        join_kernel,
        grid=(DEVICES // 2 // JOIN,),
        out_shape=jax.ShapeDtypeStruct((DEVICES // 2 * CHUNK, 128), bf16),
        in_specs=[first, first, rest, rest],
        out_specs=pl.BlockSpec(block, lambda i: (i, 0)),
        compiler_params=pltpu.CompilerParams(vmem_limit_bytes=VMEM_LIMIT),
        cost_estimate=pl.CostEstimate(flops=0, bytes_accessed=11_000_000, transcendentals=0),
    )(keep_first, got_first, keep_rest, got_rest)


def to_owners(total):
    return spread(total.reshape(DEVICES // 2, CHUNK, 128))


def own_part(pieces, device):
    own = jnp.sum(pieces.astype(f32), axis=0)
    rows = jnp.concatenate([own[CHUNK - 1 :], own], axis=0)
    return lax.dynamic_slice_in_dim(rows.reshape(-1), 9 * device, SHARD, 0)


def tables(positions):
    half = HD // 2
    frequency = rope_base ** (-jnp.arange(half, dtype=f32) / half)
    angles = positions.astype(f32)[:, None] * frequency[None, :]
    return (
        jnp.concatenate([jnp.cos(angles)] * 4, axis=-1),
        jnp.concatenate([jnp.sin(angles)] * 4, axis=-1),
    )


def body(hidden_in, segment_ids, weights_flat, cotangent):
    device = lax.axis_index("fsdp")
    core = lax.rem(device, 2)
    first_row = device * ROWS
    layers = weights_flat.shape[0]
    sections = []
    for layer in range(layers):
        blank = jnp.zeros((SECTION * 128,), bf16)
        sections.append(lax.dynamic_update_slice(blank, weights_flat[layer], (9 * device,)))
    sources = [None] * layers
    for layer in range(1, layers):
        gathered = lax.all_gather(sections[layer], "fsdp", axis=0, tiled=True)
        sources[layer] = (gathered.reshape(DEVICES // 2, 2, SECTION, 128),)
    copies = jnp.broadcast_to(
        sections[0].reshape(1, SECTION, 128), (DEVICES // 2, SECTION, 128)
    )
    same_core = spread(copies)

    x_same, x_sibling = window_of(hidden_in, core)
    window = jnp.concatenate([x_same, x_sibling], axis=0)
    s_same, s_sibling = window_of(segment_ids, core)
    segments = jnp.concatenate([s_same, s_sibling], axis=0)
    order = jnp.arange(ROWS, dtype=jnp.int32)
    same_first = first_row - ROWS * jnp.array([8, 6, 4, 2, 0], jnp.int32)
    sibling_first = first_row - ROWS * jnp.array([7, 5, 3, 1], jnp.int32)
    key_row = jnp.concatenate([same_first, sibling_first])[:, None] + order[None, :]
    key_row = key_row.reshape(-1)
    cosine_all, sine_all = tables(key_row - segments)
    same_core, window, cosine_all, sine_all = lax.optimization_barrier(
        (same_core, window, cosine_all, sine_all)
    )
    sources[0] = (same_core, swap(same_core))
    own = SAME_CORE * ROWS
    cosine, sine = cosine_all[own : own + ROWS], sine_all[own : own + ROWS]
    key_row = key_row[None, :]
    segment = segment_ids[:, None]
    first = first_row[None]
    core_in = core[None]

    x = hidden_in
    held = []
    for layer in range(layers):
        if layer > 0:
            x, sources[layer] = lax.optimization_barrier((x, sources[layer]))
        w_qkv, gain_one = unpack_first(core_in, sources[layer])
        w_out, w_in, w_down, gain_two = unpack_rest(core_in, sources[layer])
        if layer == 0:
            q, kv_s, kv_t, normed = call(
                heads_zero_kernel,
                [((ROWS, QW), bf16), ((WIN_S, 2 * KW), bf16), ((WIN_T, 2 * KW), bf16),
                 ((ROWS, D), bf16)],
                [window, cosine_all, sine_all, gain_one, w_qkv],
                flops=800_000_000, nbytes=6_000_000,
            )
        else:
            q, kv, normed = call(
                heads_kernel,
                [((ROWS, QW), bf16), ((ROWS, 2 * KW), bf16), ((ROWS, D), bf16)],
                [x, cosine, sine, gain_one, w_qkv],
                flops=150_000_000, nbytes=3_000_000,
            )
            kv_s, kv_t = window_of(kv, core, (w_out,))
        x_next, mixed, lse, middle, normed_two, gate_up, hidden = call(
            attend_kernel,
            [((ROWS, D), f32), ((ROWS, QW), bf16), ((GROUP * ROWS, KVH), f32), ((ROWS, D), f32),
             ((ROWS, D), bf16), ((ROWS, 2 * FF), f32), ((ROWS, FF), bf16)],
            [first, x, q, kv_s, kv_t, segment, key_row, gain_two, w_out, w_in, w_down],
            scratch=WEIGHT_SCRATCH, smem=1, apart=3, flops=2_000_000_000, nbytes=12_000_000,
        )
        held.append((x, q, kv_s, kv_t, normed, mixed, lse, middle, normed_two, gate_up, hidden,
                     w_qkv, w_out, w_in, w_down, gain_one, gain_two))
        x = x_next
    layer_out = x.astype(bf16)

    g = cotangent
    grads = [None] * layers
    for layer in reversed(range(layers)):
        (x, q, kv_s, kv_t, normed, mixed, lse, middle, normed_two, gate_up, hidden,
         w_qkv, w_out, w_in, w_down, gain_one, gain_two) = held[layer]
        branch, grad_gu, attn, middle_grad, dq, dkv_s, dkv_t, grad_two = call(
            back_kernel,
            [((ROWS, D), bf16), ((ROWS, 2 * FF), bf16), ((ROWS, D), bf16), ((ROWS, D), f32),
             ((ROWS, QW), bf16), ((WIN_S, 2 * KW), f32), ((WIN_T, 2 * KW), bf16), ((1, D), f32)],
            [first, g, q, kv_s, kv_t, segment, key_row, cosine, sine, gain_two, lse, middle,
             gate_up, w_out, w_in, w_down],
            scratch=WEIGHT_SCRATCH
            + (pltpu.VMEM((ROWS, 2 * FF), f32), pltpu.SemaphoreType.DMA),
            smem=1, apart=4, flops=3_000_000_000, nbytes=15_000_000,
        )
        rest_shape = (((DEVICES // 2 - LOW_PLANES) * CHUNK, 128), bf16)
        keep, send, edge = call(
            pack_rest_kernel,
            [rest_shape, rest_shape, ((EDGE, 128), f32)],
            [core_in, mixed, attn, normed_two, grad_gu, hidden, branch, grad_two],
            scratch=[
                pltpu.VMEM((216 * (DEVICES - SPLIT) + 40, 128), f32), pltpu.VMEM((5, FF, 128), f32)
            ],
            smem=1, flops=1_000_000_000, nbytes=25_000_000,
        )
        own_kv, pieces = give_back(dkv_s, dkv_t, core)
        send, pieces = lax.optimization_barrier((send, pieces))
        keep_rest, got_rest = keep, swap(send)
        g, project, grad_one = call(
            back_heads_kernel,
            [((ROWS, D), f32), ((ROWS, PW), bf16), ((1, D), f32)],
            [x, dq, own_kv, *pieces, cosine, sine, gain_one, w_qkv, middle_grad],
            flops=150_000_000, nbytes=3_000_000,
        )
        if layer + 1 < layers:
            project, grads[layer + 1] = lax.optimization_barrier((project, grads[layer + 1]))
        low_shape = ((LOW_PLANES * CHUNK, 128), bf16)
        keep, send = call(
            pack_first_kernel,
            [low_shape, low_shape],
            [core_in, normed, project, grad_one, edge],
            scratch=[
                pltpu.VMEM((216 * SPLIT + EDGE + 8, 128), f32), pltpu.VMEM((8, D, 128), f32)
            ],
            smem=1, flops=200_000_000, nbytes=8_000_000,
        )
        total = join(keep, swap(send), keep_rest, got_rest)
        if layer > 0:
            g, total = lax.optimization_barrier((g, total))
        grads[layer] = to_owners(total)
    return (layer_out, g, jnp.stack([own_part(pieces, device) for pieces in grads]))


def solution(mesh):
    in_specs = (P("fsdp", None), P("fsdp"), P(None, "fsdp"), P("fsdp", None))
    out_specs = (P("fsdp", None), P("fsdp", None), P(None, "fsdp"))
    return jax.shard_map(body, mesh=mesh, in_specs=in_specs, out_specs=out_specs, check_vma=False)
```

```python
import functools

import jax
import jax.numpy as jnp
from jax import lax
from jax.experimental import pallas as pl
from jax.experimental.pallas import tpu as pltpu
from jax.sharding import PartitionSpec as P

D = 576
FF = 1536
QH = 9
KVH = 3
HD = 64
MAXLEN = 1024
QW = QH * HD
KW = KVH * HD
PW = QW + 2 * KW
GROUP = QH // KVH
DEVICES = 128
ROWS = 128
PARAMS = 3540096
SHARD = PARAMS // DEVICES
CHUNK = 224
SECTION = 240
SPLIT = 20
LOW_PLANES = 16
JOIN = 8
EDGE = 2616
SAME_CORE = 4
WIN_S = (SAME_CORE + 1) * ROWS
WIN_T = SAME_CORE * ROWS
WIN = WIN_S + WIN_T

bf16 = jnp.bfloat16
f32 = jnp.float32
epsilon = 1e-05
rope_base = 10000.0
FACTOR = HD ** (-0.5)
VMEM_LIMIT = 60 * 1024 * 1024

HALF_GAIN_ONE = 0
HALF_QKV = D // 64
HALF_OUT = HALF_QKV + D * PW // 64
HALF_GAIN_TWO = HALF_OUT + QW * D // 64
HALF_IN = HALF_GAIN_TWO + D // 64
HALF_DOWN = HALF_IN + D * 2 * FF // 64


def mm(a, b):
    return lax.dot_general(a, b, (((1,), (0,)), ((), ())), preferred_element_type=f32)


def mm_t(a, b):
    return lax.dot_general(a, b, (((1,), (1,)), ((), ())), preferred_element_type=f32)


def t_mm(a, b):
    return lax.dot_general(a, b, (((0,), (0,)), ((), ())), preferred_element_type=f32)


def call(kernel, out_shape, args, scratch=(), smem=0, apart=0, flops=0, nbytes=0):
    in_specs = [
        pl.BlockSpec(
            memory_space=pltpu.SMEM if at < smem
            else pl.ANY if at >= len(args) - apart else pltpu.VMEM
        )
        for at in range(len(args))
    ]
    return pl.pallas_call(
        kernel,
        out_shape=[jax.ShapeDtypeStruct(s, d) for s, d in out_shape],
        in_specs=in_specs,
        out_specs=[pl.BlockSpec(memory_space=pltpu.VMEM) for _ in out_shape],
        scratch_shapes=list(scratch),
        compiler_params=pltpu.CompilerParams(vmem_limit_bytes=VMEM_LIMIT),
        cost_estimate=pl.CostEstimate(flops=flops, bytes_accessed=nbytes, transcendentals=0),
    )(*args)


def low_half(shape):
    return lax.broadcasted_iota(jnp.int32, shape, 1) < 64


def take_rows(flat, start_half, pairs, width_half, store):
    tiles = (width_half + 1) // 2
    if start_half % 2 == 0:
        for t in range(tiles):
            store(t, flat[pl.ds(start_half // 2 + t, pairs, stride=width_half), :])
    else:
        before = None
        for t in range(tiles + 1):
            if t == tiles and width_half % 2 == 1:
                store(t - 1, before)
                break
            now = pltpu.roll(flat[pl.ds(start_half // 2 + t, pairs, stride=width_half), :], 64, 1)
            if before is not None:
                store(t - 1, jnp.where(low_half(now.shape), before, now))
            before = now


def put_rows(flat, start_half, pairs, width_half, load):
    tiles = (width_half + 1) // 2
    if start_half % 2 == 0:
        for t in range(tiles):
            place = pl.ds(start_half // 2 + t, pairs, stride=width_half)
            value = load(t)
            if 2 * t + 1 == width_half:
                value = jnp.where(low_half(value.shape), value, flat[place, :])
            flat[place, :] = value
    else:
        before = None
        for t in range(tiles + 1):
            if t == tiles and width_half % 2 == 1:
                break
            place = pl.ds(start_half // 2 + t, pairs, stride=width_half)
            now = pltpu.roll(load(t), 64, 1) if t < tiles else None
            if before is None:
                value = jnp.where(low_half(now.shape), flat[place, :], now)
            else:
                value = jnp.where(low_half(before.shape), before, now)
            flat[place, :] = value
            before = now


WEIGHT_SCRATCH = (
    pltpu.VMEM((QW, D), bf16),
    pltpu.VMEM((D, 2 * FF), bf16),
    pltpu.VMEM((FF, D), bf16),
    pltpu.SemaphoreType.DMA((3,)),
)


def fetch(sources, places, sems):
    copies = [
        pltpu.make_async_copy(source, place, sems.at[n])
        for n, (source, place) in enumerate(zip(sources, places))
    ]
    return copies


def gather_flat(gathered, layer, first, count, groups, flat, landing, sems):
    size = count // groups
    copies = []
    for n in range(groups):
        copies.append(
            pltpu.make_async_copy(
                gathered.at[pl.ds(first + n * size, size), layer],
                landing.at[pl.ds(n * size, size)],
                sems.at[n],
            )
        )
        copies[-1].start()
    tail = jnp.zeros((SECTION - 216, 128), f32)
    for n in range(groups):
        copies[n].wait()

        def one_shard(d, tail):
            rows = landing[d].astype(f32)
            base = pl.multiple_of(d * 216, 8)
            flat[pl.ds(base, 24), :] = tail + rows[0:24, :]
            flat[pl.ds(base + 24, 192), :] = rows[24:216, :]
            return rows[216:SECTION, :]

        tail = lax.fori_loop(n * size, (n + 1) * size, one_shard, tail)
    flat[count * 216 : count * 216 + 24, :] = tail


def take_matrix(flat, tile, out, start_half, width_half):
    rows, columns = out.shape

    def store(parity, at, value):
        tile[at, pl.ds(parity, rows // 2, stride=2), :] = value

    for parity in range(2):
        take_rows(
            flat, start_half + parity * width_half, rows // 2, width_half,
            functools.partial(store, parity),
        )
    for t in range((width_half + 1) // 2):
        wide = min(128, columns - 128 * t)
        out[:, 128 * t : 128 * t + wide] = tile[t, 0:rows, 0:wide].astype(bf16)


def take_gain(flat, gain, start):
    first = start // 2
    for t in range(5):
        if start % 2 == 0:
            value = flat[first + t : first + t + 1, :]
        else:
            here = pltpu.roll(flat[first + t : first + t + 1, :], 64, 1)
            after = pltpu.roll(flat[first + t + 1 : first + t + 2, :], 64, 1)
            value = jnp.where(low_half((1, 128)), here, after)
        gain[0:1, 128 * t : 128 * t + 128] = value


def unpack_first_kernel(layer, gathered, w_qkv, gain, landing, flat, tile, sems):
    gather_flat(gathered, layer, 0, SPLIT + 1, 3, flat, landing, sems)
    take_gain(flat, gain, HALF_GAIN_ONE)
    take_matrix(flat, tile, w_qkv, HALF_QKV, PW // 64)


def unpack_rest_kernel(
    layer, gathered, w_out_at, w_in_at, w_down_at, gain, landing, flat, tile, sems,
    w_out, w_in, w_down, out_sems,
):
    gather_flat(gathered, layer, SPLIT, DEVICES - SPLIT, 4, flat, landing, sems)
    skip = 2 * 216 * SPLIT

    def in_tile(c, carry):
        w_in[:, pl.ds(pl.multiple_of(c * 128, 128), 128)] = flat[
            pl.ds((HALF_IN - skip) // 2 + c, D, stride=24), :
        ].astype(bf16)
        return carry

    lax.fori_loop(0, 24, in_tile, 0)
    copies = fetch((w_out, w_in, w_down), (w_out_at, w_in_at, w_down_at), out_sems)
    copies[1].start()
    take_matrix(flat, tile, w_down, HALF_DOWN - skip, D // 64)
    copies[2].start()
    take_matrix(flat, tile, w_out, HALF_OUT - skip, D // 64)
    copies[0].start()
    take_gain(flat, gain, HALF_GAIN_TWO - skip)
    for copy in copies:
        copy.wait()


def unpack_call(
    kernel, layer, out_shape, gathered, count, groups, tiles, nbytes, apart=0, scratch=()
):
    return pl.pallas_call(
        functools.partial(kernel, layer),
        out_shape=[jax.ShapeDtypeStruct(s, d) for s, d in out_shape],
        in_specs=[pl.BlockSpec(memory_space=pl.ANY)],
        out_specs=[
            pl.BlockSpec(memory_space=pl.ANY if at < apart else pltpu.VMEM)
            for at in range(len(out_shape))
        ],
        scratch_shapes=[
            pltpu.VMEM((count, SECTION, 128), bf16),
            pltpu.VMEM((count * 216 + 32, 128), f32),
            pltpu.VMEM(tiles, f32),
            pltpu.SemaphoreType.DMA((groups,)),
            *scratch,
        ],
        compiler_params=pltpu.CompilerParams(vmem_limit_bytes=VMEM_LIMIT),
        cost_estimate=pl.CostEstimate(flops=2_000_000_000, bytes_accessed=nbytes, transcendentals=0),
    )(gathered)


def unpack_first(gathered, layer):
    return unpack_call(
        unpack_first_kernel, layer, [((D, PW), bf16), ((1, 640), f32)], gathered,
        SPLIT + 1, 3, (8, D, 128), 9_000_000,
    )


def unpack_rest(gathered, layer):
    return unpack_call(
        unpack_rest_kernel, layer,
        [((QW, D), bf16), ((D, 2 * FF), bf16), ((FF, D), bf16), ((1, 640), f32)], gathered,
        DEVICES - SPLIT, 4, (5, FF, 128), 30_000_000, apart=3, scratch=WEIGHT_SCRATCH,
    )


def turn(value, cosine, sine):
    lane = lax.broadcasted_iota(jnp.int32, (value.shape[0], 128), 1)
    first = lax.rem(lane, 64) < 32
    pieces = []
    for t in range(value.shape[1] // 128):
        part = value[:, 128 * t : 128 * t + 128]
        swapped = jnp.where(first, -pltpu.roll(part, 96, 1), pltpu.roll(part, 32, 1))
        pieces.append(part * cosine + swapped * sine)
    return jnp.concatenate(pieces, axis=1)


def inverse_norm(values):
    return lax.rsqrt(jnp.mean(values * values, axis=-1, keepdims=True) + epsilon)


def heads_zero_kernel(window, cosine, sine, gain_row, w_qkv, q_out, kv_s, kv_t, normed_out):
    gain = gain_row[:, 0:D]
    for begin, rows in ((0, 384), (384, 384), (768, 384)):
        x = window[begin : begin + rows, :].astype(f32)
        normed = (x * inverse_norm(x) * gain).astype(bf16)
        project = mm(normed, w_qkv[:, 512:PW])
        both = turn(project[:, 0:256], cosine[begin : begin + rows, :], sine[begin : begin + rows, :])
        kv = jnp.concatenate([both[:, 64:256], project[:, 256:448]], axis=1).astype(bf16)
        for r in range(0, rows, 128):
            at = begin + r
            if at < WIN_S:
                kv_s[at : at + 128, :] = kv[r : r + 128, :]
            else:
                kv_t[at - WIN_S : at - WIN_S + 128, :] = kv[r : r + 128, :]
    own = SAME_CORE * ROWS
    x = window[own : own + ROWS, :].astype(f32)
    normed = (x * inverse_norm(x) * gain).astype(bf16)
    normed_out[...] = normed
    project = mm(normed, w_qkv[:, 0:640])
    q_out[...] = turn(project, cosine[own : own + ROWS, :], sine[own : own + ROWS, :])[
        :, 0:QW
    ].astype(bf16)


def heads_kernel(x_in, cosine, sine, gain_row, w_qkv, q_out, kv_out, normed_out):
    x = x_in[...]
    normed = (x * inverse_norm(x) * gain_row[:, 0:D]).astype(bf16)
    normed_out[...] = normed
    project = mm(normed, w_qkv[...])
    both = turn(project[:, 0:768], cosine[...], sine[...])
    q_out[...] = both[:, 0:QW].astype(bf16)
    kv_out[...] = jnp.concatenate([both[:, QW:768], project[:, 768:PW]], axis=1).astype(bf16)


def allowed_of(segment, key_row, first_row):
    query = first_row + lax.broadcasted_iota(jnp.int32, (ROWS, 1), 0)
    return (key_row >= segment) & (key_row <= query)


def group_rows(value, group):
    return jnp.concatenate(
        [value[:, (GROUP * group + n) * HD : (GROUP * group + n + 1) * HD] for n in range(GROUP)],
        axis=0,
    )


def window_rows(kv_s, kv_t, begin):
    return jnp.concatenate(
        [kv_s[:, begin : begin + HD], kv_t[:, begin : begin + HD]], axis=0
    )


def attend_kernel(
    first, x_in, q_in, kv_s, kv_t, segment, key_row, gain_row, w_out_at, w_in_at, w_down_at,
    x_out, mixed_out, lse_out, middle_out, normed_out, gate_up_out, hidden_out,
    w_out, w_in, w_down, sems,
):
    copies = fetch((w_out_at, w_in_at, w_down_at), (w_out, w_in, w_down), sems)
    for copy in copies:
        copy.start()
    allowed = allowed_of(segment[...], key_row[...], first[0])
    bias = jnp.where(allowed, 0.0, -1e30).astype(f32)
    bias = jnp.concatenate([bias] * GROUP, axis=0)
    q = q_in[...]
    pieces = []
    for group in range(KVH):
        keys = window_rows(kv_s, kv_t, group * HD)
        values = window_rows(kv_s, kv_t, KW + group * HD)
        scores = mm_t(group_rows(q, group), keys) * FACTOR + bias
        peak = jnp.max(scores, axis=-1, keepdims=True)
        powers = jnp.exp(scores - peak)
        total = jnp.sum(powers, axis=-1, keepdims=True)
        lse_out[:, group : group + 1] = peak + jnp.log(total)
        weights = (powers * (1.0 / total)).astype(bf16)
        mixed = mm(weights, values)
        for n in range(GROUP):
            pieces.append(mixed[n * ROWS : (n + 1) * ROWS, :])
    mixed = jnp.concatenate(pieces, axis=1).astype(bf16)
    mixed_out[...] = mixed
    copies[0].wait()
    middle = x_in[...].astype(f32) + mm(mixed, w_out[...])
    middle_out[...] = middle
    normed = (middle * inverse_norm(middle) * gain_row[:, 0:D]).astype(bf16)
    normed_out[...] = normed
    copies[1].wait()
    gate_up = mm(normed, w_in[...])
    gate_up_out[...] = gate_up
    gate = gate_up[:, 0:FF]
    hidden = (gate * jax.nn.sigmoid(gate) * gate_up[:, FF:]).astype(bf16)
    hidden_out[...] = hidden
    copies[2].wait()
    x_out[...] = middle + mm(hidden, w_down[...])


def norm_back(values, inverse, gain, grad):
    weighted = grad * gain
    return inverse * weighted - values * inverse**3 * jnp.mean(
        weighted * values, axis=-1, keepdims=True
    )


def back_kernel(
    first, g_in, q_in, kv_s, kv_t, segment, key_row, cosine, sine, gain_row, lse, middle_in,
    gate_up_at, w_out_at, w_in_at, w_down_at,
    branch_out, grad_gu_out, attn_out, middle_grad_out, dq_out, dkv_s, dkv_t, gain_out,
    w_out, w_in, w_down, sems, gate_up, gate_sem,
):
    copies = fetch((w_out_at, w_in_at, w_down_at), (w_out, w_in, w_down), sems)
    gate_copy = pltpu.make_async_copy(gate_up_at, gate_up, gate_sem)
    copies[2].start()
    gate_copy.start()
    copies[1].start()
    copies[0].start()
    allowed = allowed_of(segment[...], key_row[...], first[0])
    bias = jnp.where(allowed, 0.0, -1e30).astype(f32)
    bias = jnp.concatenate([bias] * GROUP, axis=0)
    q = q_in[...]
    held = []
    for group in range(KVH):
        keys = window_rows(kv_s, kv_t, group * HD)
        scores = mm_t(group_rows(q, group), keys) * FACTOR + bias
        held.append(jnp.exp(scores - lse[:, group : group + 1]))
    g = g_in[...].astype(f32)
    branch = g.astype(bf16)
    branch_out[...] = branch
    copies[2].wait()
    grad_hidden = mm_t(branch, w_down[...])
    gate_copy.wait()
    gate = gate_up[:, 0:FF]
    up = gate_up[:, FF:]
    sigma = jax.nn.sigmoid(gate)
    grad_gu_out[:, 0:FF] = (
        grad_hidden * up * sigma * (1.0 + gate * (1.0 - sigma))
    ).astype(bf16)
    grad_gu_out[:, FF:] = (grad_hidden * gate * sigma).astype(bf16)
    copies[1].wait()
    grad_two = mm_t(grad_gu_out[...], w_in[...])
    middle = middle_in[...]
    inverse = inverse_norm(middle)
    gain_out[...] = jnp.sum(grad_two * middle * inverse, axis=0, keepdims=True)
    grad_middle = g + norm_back(middle, inverse, gain_row[:, 0:D], grad_two)
    middle_grad_out[...] = grad_middle
    attn = grad_middle.astype(bf16)
    attn_out[...] = attn
    copies[0].wait()
    grad_mixed = mm_t(attn, w_out[...]).astype(bf16)

    dq, dk, dv = [], [], []
    for group in range(KVH):
        keys = window_rows(kv_s, kv_t, group * HD)
        values = window_rows(kv_s, kv_t, KW + group * HD)
        query = group_rows(q, group)
        grad = group_rows(grad_mixed, group)
        probs = held[group]
        grad_w = mm_t(grad, values)
        delta = jnp.sum(probs * grad_w, axis=-1, keepdims=True)
        grad_scores = (probs * (grad_w - delta)).astype(bf16)
        part = mm(grad_scores, keys) * FACTOR
        for n in range(GROUP):
            dq.append(part[n * ROWS : (n + 1) * ROWS, :])
        dk.append(mm(query.T, grad_scores) * FACTOR)
        dv.append(mm(grad.T, probs.astype(bf16)))
    dkv = jnp.concatenate(dk + dv, axis=0).T
    dkv_s[...] = dkv[0:WIN_S, :]
    dkv_t[...] = dkv[WIN_S:, :].astype(bf16)
    wide = jnp.concatenate(dq + [jnp.zeros((ROWS, HD), f32)], axis=1)
    dq_out[...] = turn(wide, cosine[...], -sine[...])[:, 0:QW].astype(bf16)


def back_heads_kernel(
    core, x_in, dq, own, r8, r6, r4, r2, cosine, sine, gain_row, w_qkv, middle_grad, normed, edge,
    g_out, keep, send, flat, tile, project_out, gain_out,
):
    total = own[...]
    for piece in (r8, r6, r4, r2):
        total = total + piece[...].astype(f32)
    keys = jnp.concatenate([total[:, 0:KW], jnp.zeros((ROWS, HD), f32)], axis=1)
    keys = turn(keys, cosine[...], -sine[...])[:, 0:KW]
    project = jnp.concatenate(
        [dq[...].astype(f32), keys, total[:, KW:]], axis=1
    ).astype(bf16)
    project_out[...] = project
    grad = mm_t(project, w_qkv[...])
    x = x_in[...].astype(f32)
    inverse = inverse_norm(x)
    gain_out[...] = jnp.sum(grad * x * inverse, axis=0, keepdims=True)
    g_out[...] = middle_grad[...] + norm_back(x, inverse, gain_row[:, 0:D], grad)
    pack_first(core, normed, project_out, gain_out, edge, keep, send, flat, tile)


def put_gain(flat, gain, start):
    row = jnp.concatenate([gain[...], jnp.zeros((1, 64), f32)], axis=1)
    first = start // 2
    before = None
    for t in range(5):
        part = row[:, 128 * t : 128 * t + 128]
        place = slice(first + t, first + t + 1)
        if start % 2 == 0:
            flat[place, :] = part
        else:
            now = pltpu.roll(part, 64, 1)
            if before is None:
                flat[place, :] = now
            else:
                flat[place, :] = jnp.where(low_half((1, 128)), before, now)
            before = now


def put_matrix(flat, tile, left, right, start_half, width_half):
    rows, columns = left.shape[1], right.shape[1]
    turned = left[...].T
    for t in range((width_half + 1) // 2):
        wide = min(128, columns - 128 * t)
        tile[t, 0:rows, 0:wide] = mm(turned, right[:, 128 * t : 128 * t + wide])
    for parity in range(2):
        put_rows(
            flat, start_half + parity * width_half, rows // 2, width_half,
            lambda t, parity=parity: tile[t, pl.ds(parity, rows // 2, stride=2), :],
        )


def cut(flat, core, first_plane, planes, skip, keep, send):
    last = lax.broadcasted_iota(jnp.int32, (CHUNK, 128), 0) == CHUNK - 1
    for out, flip in ((keep, 0), (send, 1)):
        def one_owner(k, carry, out=out, flip=flip):
            d = 2 * (first_plane + k) + lax.rem(core[0] + flip, 2)
            base = pl.multiple_of(d * 216 - skip + 8, 8)
            odd = jnp.where(d < DEVICES // 2, base - 1, base + CHUNK - 1)
            value = jnp.where(last, flat[pl.ds(odd, 1), :], flat[pl.ds(base, CHUNK), :])
            out[pl.ds(pl.multiple_of(k * CHUNK, CHUNK), CHUNK), :] = value.astype(bf16)
            return carry

        lax.fori_loop(0, planes, one_owner, 0)


def pack_rest_kernel(
    core, mixed, attn, normed_two, grad_gu, hidden, branch, gain_two, keep, send, edge, flat, tile
):
    skip = 216 * SPLIT
    half = 2 * (7 - skip)
    put_gain(flat, gain_two, HALF_GAIN_TWO + half)
    put_matrix(flat, tile, mixed, attn, HALF_OUT + half, D // 64)
    put_matrix(flat, tile, hidden, branch, HALF_DOWN + half, D // 64)

    turned = normed_two[...].T

    def in_tile(c, carry):
        flat[pl.ds((HALF_IN + half) // 2 + c, D, stride=24), :] = mm(
            turned, grad_gu[:, pl.ds(pl.multiple_of(c * 128, 128), 128)]
        )
        return carry

    lax.fori_loop(0, 24, in_tile, 0)
    cut(flat, core, LOW_PLANES, DEVICES // 2 - LOW_PLANES, skip, keep, send)
    edge[...] = flat[0:EDGE, :]


def pack_first(core, normed, project, gain_one, edge, keep, send, flat, tile):
    skip = 216 * SPLIT
    flat[skip : skip + EDGE, :] = edge[...]
    put_gain(flat, gain_one, HALF_GAIN_ONE + 14)
    put_matrix(flat, tile, normed, project, HALF_QKV + 14, PW // 64)
    cut(flat, core, 0, LOW_PLANES, 0, keep, send)


def hop(value, by):
    pairs = [(i, i + by) for i in range(DEVICES) if 0 <= i + by < DEVICES]
    return lax.ppermute(value, "fsdp", pairs)


def swap(value):
    return lax.ppermute(value, "fsdp", [(i, i ^ 1) for i in range(DEVICES)])


def window_of(value, core, beside=()):
    blocks = [hop(value, by) for by in (8, 6, 4, 2)] + [value]
    same = jnp.concatenate(blocks, axis=0)
    rows = value.shape[0]
    gift = lax.dynamic_slice_in_dim(same, (1 - core) * rows, SAME_CORE * rows, 0)
    if beside:
        gift, _ = lax.optimization_barrier((gift, beside))
    return same, swap(gift)


def give_back(dkv_s, dkv_t, core):
    got = swap(dkv_t).astype(f32)
    blank = jnp.zeros((ROWS, 2 * KW), f32)
    early = jnp.concatenate([got, blank], axis=0)
    late = jnp.concatenate([blank, got], axis=0)
    total = dkv_s + jnp.where(core == 0, late, early)
    pieces = [
        hop(total[at * ROWS : (at + 1) * ROWS].astype(bf16), -by)
        for at, by in enumerate((8, 6, 4, 2))
    ]
    return total[SAME_CORE * ROWS :], pieces


def join_kernel(keep_first, got_first, keep_rest, got_rest, out):
    low = LOW_PLANES // JOIN

    @pl.when(pl.program_id(0) < low)
    def _():
        out[...] = (keep_first[...].astype(f32) + got_first[...].astype(f32)).astype(bf16)

    @pl.when(pl.program_id(0) >= low)
    def _():
        out[...] = (keep_rest[...].astype(f32) + got_rest[...].astype(f32)).astype(bf16)


def join(keep_first, got_first, keep_rest, got_rest):
    low = LOW_PLANES // JOIN
    block = (JOIN * CHUNK, 128)
    first = pl.BlockSpec(block, lambda i: (jnp.minimum(i, low - 1), 0))
    rest = pl.BlockSpec(block, lambda i: (jnp.maximum(i - low, 0), 0))
    return pl.pallas_call(
        join_kernel,
        grid=(DEVICES // 2 // JOIN,),
        out_shape=pltpu.HBM((DEVICES // 2 * CHUNK, 128), bf16),
        in_specs=[first, first, rest, rest],
        out_specs=pl.BlockSpec(block, lambda i: (i, 0)),
        compiler_params=pltpu.CompilerParams(vmem_limit_bytes=16 * 1024 * 1024),
        cost_estimate=pl.CostEstimate(flops=0, bytes_accessed=11_000_000, transcendentals=0),
    )(keep_first, got_first, keep_rest, got_rest)


def to_owners(total):
    groups = [list(range(0, DEVICES, 2)), list(range(1, DEVICES, 2))]
    return lax.all_to_all(
        total.reshape(DEVICES // 2, CHUNK, 128),
        "fsdp", split_axis=0, concat_axis=0, tiled=True, axis_index_groups=groups,
    )


def own_part(pieces, device):
    own = jnp.sum(pieces.astype(f32), axis=0)
    rows = jnp.concatenate([own[CHUNK - 1 :], own], axis=0)
    return lax.dynamic_slice_in_dim(rows.reshape(-1), 9 * device, SHARD, 0)


def tables(positions):
    half = HD // 2
    frequency = rope_base ** (-jnp.arange(half, dtype=f32) / half)
    angles = positions.astype(f32)[:, None] * frequency[None, :]
    return (
        jnp.concatenate([jnp.cos(angles)] * 4, axis=-1),
        jnp.concatenate([jnp.sin(angles)] * 4, axis=-1),
    )


def body(hidden_in, segment_ids, weights_flat, cotangent):
    device = lax.axis_index("fsdp")
    core = lax.rem(device, 2)
    first_row = device * ROWS
    layers = weights_flat.shape[0]
    sections = []
    for layer in range(layers):
        blank = jnp.zeros((SECTION * 128,), bf16)
        sections.append(lax.dynamic_update_slice(blank, weights_flat[layer], (9 * device,)))
    gathered = lax.all_gather(jnp.concatenate(sections), "fsdp", axis=0, tiled=True)
    gathered = gathered.reshape(DEVICES, layers, SECTION, 128)

    x_same, x_sibling = window_of(hidden_in, core)
    window = jnp.concatenate([x_same, x_sibling], axis=0)
    s_same, s_sibling = window_of(segment_ids, core)
    segments = jnp.concatenate([s_same, s_sibling], axis=0)
    order = jnp.arange(ROWS, dtype=jnp.int32)
    same_first = first_row - ROWS * jnp.array([8, 6, 4, 2, 0], jnp.int32)
    sibling_first = first_row - ROWS * jnp.array([7, 5, 3, 1], jnp.int32)
    key_row = jnp.concatenate([same_first, sibling_first])[:, None] + order[None, :]
    key_row = key_row.reshape(-1)
    cosine_all, sine_all = tables(key_row - segments)
    own = SAME_CORE * ROWS
    cosine, sine = cosine_all[own : own + ROWS], sine_all[own : own + ROWS]
    key_row = key_row[None, :]
    segment = segment_ids[:, None]
    first = first_row[None]
    core_in = core[None]

    x = hidden_in
    held = []
    for layer in range(layers):
        w_qkv, gain_one = unpack_first(gathered, layer)
        w_out, w_in, w_down, gain_two = unpack_rest(gathered, layer)
        if layer == 0:
            q, kv_s, kv_t, normed = call(
                heads_zero_kernel,
                [((ROWS, QW), bf16), ((WIN_S, 2 * KW), bf16), ((WIN_T, 2 * KW), bf16),
                 ((ROWS, D), bf16)],
                [window, cosine_all, sine_all, gain_one, w_qkv],
                flops=800_000_000, nbytes=6_000_000,
            )
        else:
            q, kv, normed = call(
                heads_kernel,
                [((ROWS, QW), bf16), ((ROWS, 2 * KW), bf16), ((ROWS, D), bf16)],
                [x, cosine, sine, gain_one, w_qkv],
                flops=150_000_000, nbytes=3_000_000,
            )
            kv_s, kv_t = window_of(kv, core, (w_out,))
        x_next, mixed, lse, middle, normed_two, gate_up, hidden = call(
            attend_kernel,
            [((ROWS, D), f32), ((ROWS, QW), bf16), ((GROUP * ROWS, KVH), f32), ((ROWS, D), f32),
             ((ROWS, D), bf16), ((ROWS, 2 * FF), f32), ((ROWS, FF), bf16)],
            [first, x, q, kv_s, kv_t, segment, key_row, gain_two, w_out, w_in, w_down],
            scratch=WEIGHT_SCRATCH, smem=1, apart=3, flops=2_000_000_000, nbytes=12_000_000,
        )
        held.append((x, q, kv_s, kv_t, normed, mixed, lse, middle, normed_two, gate_up, hidden,
                     w_qkv, w_out, w_in, w_down, gain_one, gain_two))
        x = x_next
    layer_out = x.astype(bf16)

    g = cotangent
    grads = [None] * layers
    for layer in reversed(range(layers)):
        (x, q, kv_s, kv_t, normed, mixed, lse, middle, normed_two, gate_up, hidden,
         w_qkv, w_out, w_in, w_down, gain_one, gain_two) = held[layer]
        branch, grad_gu, attn, middle_grad, dq, dkv_s, dkv_t, grad_two = call(
            back_kernel,
            [((ROWS, D), bf16), ((ROWS, 2 * FF), bf16), ((ROWS, D), bf16), ((ROWS, D), f32),
             ((ROWS, QW), bf16), ((WIN_S, 2 * KW), f32), ((WIN_T, 2 * KW), bf16), ((1, D), f32)],
            [first, g, q, kv_s, kv_t, segment, key_row, cosine, sine, gain_two, lse, middle,
             gate_up, w_out, w_in, w_down],
            scratch=WEIGHT_SCRATCH
            + (pltpu.VMEM((ROWS, 2 * FF), f32), pltpu.SemaphoreType.DMA),
            smem=1, apart=4, flops=3_000_000_000, nbytes=15_000_000,
        )
        rest_shape = (((DEVICES // 2 - LOW_PLANES) * CHUNK, 128), bf16)
        keep, send, edge = call(
            pack_rest_kernel,
            [rest_shape, rest_shape, ((EDGE, 128), f32)],
            [core_in, mixed, attn, normed_two, grad_gu, hidden, branch, grad_two],
            scratch=[
                pltpu.VMEM((216 * (DEVICES - SPLIT) + 40, 128), f32), pltpu.VMEM((5, FF, 128), f32)
            ],
            smem=1, flops=1_000_000_000, nbytes=25_000_000,
        )
        own_kv, pieces = give_back(dkv_s, dkv_t, core)
        send, pieces = lax.optimization_barrier((send, pieces))
        keep_rest, got_rest = keep, swap(send)
        if layer + 1 < layers:
            own_kv, grads[layer + 1] = lax.optimization_barrier((own_kv, grads[layer + 1]))
        low_shape = ((LOW_PLANES * CHUNK, 128), bf16)
        g, keep, send = call(
            back_heads_kernel,
            [((ROWS, D), f32), low_shape, low_shape],
            [core_in, x, dq, own_kv, *pieces, cosine, sine, gain_one, w_qkv, middle_grad, normed,
             edge],
            scratch=[
                pltpu.VMEM((216 * SPLIT + EDGE + 8, 128), f32), pltpu.VMEM((8, D, 128), f32),
                pltpu.VMEM((ROWS, PW), bf16), pltpu.VMEM((1, D), f32),
            ],
            smem=1, flops=350_000_000, nbytes=10_000_000,
        )
        total = join(keep, swap(send), keep_rest, got_rest)
        if layer > 0:
            g, total = lax.optimization_barrier((g, total))
        grads[layer] = to_owners(total)
    return (layer_out, g, jnp.stack([own_part(pieces, device) for pieces in grads]))


def solution(mesh):
    in_specs = (P("fsdp", None), P("fsdp"), P(None, "fsdp"), P("fsdp", None))
    out_specs = (P("fsdp", None), P("fsdp", None), P(None, "fsdp"))
    return jax.shard_map(body, mesh=mesh, in_specs=in_specs, out_specs=out_specs, check_vma=False)
```

```python
import functools

import jax
import jax.numpy as jnp
from jax import lax
from jax.experimental import pallas as pl
from jax.experimental.pallas import tpu as pltpu
from jax.sharding import PartitionSpec as P

D = 576
FF = 1536
QH = 9
KVH = 3
HD = 64
MAXLEN = 1024
QW = QH * HD
KW = KVH * HD
PW = QW + 2 * KW
GROUP = QH // KVH
DEVICES = 128
ROWS = 128
PARAMS = 3540096
SHARD = PARAMS // DEVICES
CHUNK = 224
SECTION = 240
SPLIT = 20
LOW_PLANES = 16
JOIN = 8
EDGE = 2616
SAME_CORE = 4
WIN_S = (SAME_CORE + 1) * ROWS
WIN_T = SAME_CORE * ROWS
WIN = WIN_S + WIN_T

bf16 = jnp.bfloat16
f32 = jnp.float32
epsilon = 1e-05
rope_base = 10000.0
FACTOR = HD ** (-0.5)
VMEM_LIMIT = 60 * 1024 * 1024

HALF_GAIN_ONE = 0
HALF_QKV = D // 64
HALF_OUT = HALF_QKV + D * PW // 64
HALF_GAIN_TWO = HALF_OUT + QW * D // 64
HALF_IN = HALF_GAIN_TWO + D // 64
HALF_DOWN = HALF_IN + D * 2 * FF // 64


def mm(a, b):
    return lax.dot_general(a, b, (((1,), (0,)), ((), ())), preferred_element_type=f32)


def mm_t(a, b):
    return lax.dot_general(a, b, (((1,), (1,)), ((), ())), preferred_element_type=f32)


def t_mm(a, b):
    return lax.dot_general(a, b, (((0,), (0,)), ((), ())), preferred_element_type=f32)


def call(kernel, out_shape, args, scratch=(), smem=0, apart=0, flops=0, nbytes=0):
    in_specs = [
        pl.BlockSpec(
            memory_space=pltpu.SMEM if at < smem
            else pl.ANY if at >= len(args) - apart else pltpu.VMEM
        )
        for at in range(len(args))
    ]
    return pl.pallas_call(
        kernel,
        out_shape=[jax.ShapeDtypeStruct(s, d) for s, d in out_shape],
        in_specs=in_specs,
        out_specs=[pl.BlockSpec(memory_space=pltpu.VMEM) for _ in out_shape],
        scratch_shapes=list(scratch),
        compiler_params=pltpu.CompilerParams(vmem_limit_bytes=VMEM_LIMIT),
        cost_estimate=pl.CostEstimate(flops=flops, bytes_accessed=nbytes, transcendentals=0),
    )(*args)


def low_half(shape):
    return lax.broadcasted_iota(jnp.int32, shape, 1) < 64


def take_rows(flat, start_half, pairs, width_half, store):
    tiles = (width_half + 1) // 2
    if start_half % 2 == 0:
        for t in range(tiles):
            store(t, flat[pl.ds(start_half // 2 + t, pairs, stride=width_half), :])
    else:
        before = None
        for t in range(tiles + 1):
            if t == tiles and width_half % 2 == 1:
                store(t - 1, before)
                break
            now = pltpu.roll(flat[pl.ds(start_half // 2 + t, pairs, stride=width_half), :], 64, 1)
            if before is not None:
                store(t - 1, jnp.where(low_half(now.shape), before, now))
            before = now


def put_rows(flat, start_half, pairs, width_half, load):
    tiles = (width_half + 1) // 2
    if start_half % 2 == 0:
        for t in range(tiles):
            place = pl.ds(start_half // 2 + t, pairs, stride=width_half)
            value = load(t)
            if 2 * t + 1 == width_half:
                value = jnp.where(low_half(value.shape), value, flat[place, :])
            flat[place, :] = value
    else:
        before = None
        for t in range(tiles + 1):
            if t == tiles and width_half % 2 == 1:
                break
            place = pl.ds(start_half // 2 + t, pairs, stride=width_half)
            now = pltpu.roll(load(t), 64, 1) if t < tiles else None
            if before is None:
                value = jnp.where(low_half(now.shape), flat[place, :], now)
            else:
                value = jnp.where(low_half(before.shape), before, now)
            flat[place, :] = value
            before = now


WEIGHT_SCRATCH = (
    pltpu.VMEM((QW, D), bf16),
    pltpu.VMEM((D, 2 * FF), bf16),
    pltpu.VMEM((FF, D), bf16),
    pltpu.SemaphoreType.DMA((3,)),
)


def fetch(sources, places, sems):
    copies = [
        pltpu.make_async_copy(source, place, sems.at[n])
        for n, (source, place) in enumerate(zip(sources, places))
    ]
    return copies


def gather_flat(gathered, layer, first, count, groups, flat, landing, sems):
    size = count // groups
    copies = []
    for n in range(groups):
        copies.append(
            pltpu.make_async_copy(
                gathered.at[pl.ds(first + n * size, size), layer],
                landing.at[pl.ds(n * size, size)],
                sems.at[n],
            )
        )
        copies[-1].start()
    tail = jnp.zeros((SECTION - 216, 128), f32)
    for n in range(groups):
        copies[n].wait()

        def one_shard(d, tail):
            rows = landing[d].astype(f32)
            base = pl.multiple_of(d * 216, 8)
            flat[pl.ds(base, 24), :] = tail + rows[0:24, :]
            flat[pl.ds(base + 24, 192), :] = rows[24:216, :]
            return rows[216:SECTION, :]

        tail = lax.fori_loop(n * size, (n + 1) * size, one_shard, tail)
    flat[count * 216 : count * 216 + 24, :] = tail


def take_matrix(flat, tile, out, start_half, width_half):
    rows, columns = out.shape

    def store(parity, at, value):
        tile[at, pl.ds(parity, rows // 2, stride=2), :] = value

    for parity in range(2):
        take_rows(
            flat, start_half + parity * width_half, rows // 2, width_half,
            functools.partial(store, parity),
        )
    for t in range((width_half + 1) // 2):
        wide = min(128, columns - 128 * t)
        out[:, 128 * t : 128 * t + wide] = tile[t, 0:rows, 0:wide].astype(bf16)


def take_gain(flat, gain, start):
    first = start // 2
    for t in range(5):
        if start % 2 == 0:
            value = flat[first + t : first + t + 1, :]
        else:
            here = pltpu.roll(flat[first + t : first + t + 1, :], 64, 1)
            after = pltpu.roll(flat[first + t + 1 : first + t + 2, :], 64, 1)
            value = jnp.where(low_half((1, 128)), here, after)
        gain[0:1, 128 * t : 128 * t + 128] = value


def unpack_first_kernel(layer, gathered, w_qkv, gain, landing, flat, tile, sems):
    gather_flat(gathered, layer, 0, SPLIT + 1, 3, flat, landing, sems)
    take_gain(flat, gain, HALF_GAIN_ONE)
    take_matrix(flat, tile, w_qkv, HALF_QKV, PW // 64)


def unpack_rest_kernel(
    layer, gathered, w_out_at, w_in_at, w_down_at, gain, landing, flat, tile, sems,
    w_out, w_in, w_down, out_sems,
):
    gather_flat(gathered, layer, SPLIT, DEVICES - SPLIT, 4, flat, landing, sems)
    skip = 2 * 216 * SPLIT

    def in_tile(c, carry):
        w_in[:, pl.ds(pl.multiple_of(c * 128, 128), 128)] = flat[
            pl.ds((HALF_IN - skip) // 2 + c, D, stride=24), :
        ].astype(bf16)
        return carry

    lax.fori_loop(0, 24, in_tile, 0)
    copies = fetch((w_out, w_in, w_down), (w_out_at, w_in_at, w_down_at), out_sems)
    copies[1].start()
    take_matrix(flat, tile, w_down, HALF_DOWN - skip, D // 64)
    copies[2].start()
    take_matrix(flat, tile, w_out, HALF_OUT - skip, D // 64)
    copies[0].start()
    take_gain(flat, gain, HALF_GAIN_TWO - skip)
    for copy in copies:
        copy.wait()


def unpack_call(
    kernel, layer, out_shape, gathered, count, groups, tiles, nbytes, apart=0, scratch=()
):
    return pl.pallas_call(
        functools.partial(kernel, layer),
        out_shape=[jax.ShapeDtypeStruct(s, d) for s, d in out_shape],
        in_specs=[pl.BlockSpec(memory_space=pl.ANY)],
        out_specs=[
            pl.BlockSpec(memory_space=pl.ANY if at < apart else pltpu.VMEM)
            for at in range(len(out_shape))
        ],
        scratch_shapes=[
            pltpu.VMEM((count, SECTION, 128), bf16),
            pltpu.VMEM((count * 216 + 32, 128), f32),
            pltpu.VMEM(tiles, f32),
            pltpu.SemaphoreType.DMA((groups,)),
            *scratch,
        ],
        compiler_params=pltpu.CompilerParams(vmem_limit_bytes=VMEM_LIMIT),
        cost_estimate=pl.CostEstimate(flops=2_000_000_000, bytes_accessed=nbytes, transcendentals=0),
    )(gathered)


def unpack_first(gathered, layer):
    return unpack_call(
        unpack_first_kernel, layer, [((D, PW), bf16), ((1, 640), f32)], gathered,
        SPLIT + 1, 3, (8, D, 128), 9_000_000,
    )


def unpack_rest(gathered, layer):
    return unpack_call(
        unpack_rest_kernel, layer,
        [((QW, D), bf16), ((D, 2 * FF), bf16), ((FF, D), bf16), ((1, 640), f32)], gathered,
        DEVICES - SPLIT, 4, (5, FF, 128), 30_000_000, apart=3, scratch=WEIGHT_SCRATCH,
    )


def turn(value, cosine, sine):
    lane = lax.broadcasted_iota(jnp.int32, (value.shape[0], 128), 1)
    first = lax.rem(lane, 64) < 32
    pieces = []
    for t in range(value.shape[1] // 128):
        part = value[:, 128 * t : 128 * t + 128]
        swapped = jnp.where(first, -pltpu.roll(part, 96, 1), pltpu.roll(part, 32, 1))
        pieces.append(part * cosine + swapped * sine)
    return jnp.concatenate(pieces, axis=1)


def inverse_norm(values):
    return lax.rsqrt(jnp.mean(values * values, axis=-1, keepdims=True) + epsilon)


def heads_zero_kernel(window, cosine, sine, gain_row, w_qkv, q_out, kv_s, kv_t, normed_out):
    gain = gain_row[:, 0:D]
    for begin, rows in ((0, 384), (384, 384), (768, 384)):
        x = window[begin : begin + rows, :].astype(f32)
        normed = (x * inverse_norm(x) * gain).astype(bf16)
        project = mm(normed, w_qkv[:, 512:PW])
        both = turn(project[:, 0:256], cosine[begin : begin + rows, :], sine[begin : begin + rows, :])
        kv = jnp.concatenate([both[:, 64:256], project[:, 256:448]], axis=1).astype(bf16)
        for r in range(0, rows, 128):
            at = begin + r
            if at < WIN_S:
                kv_s[at : at + 128, :] = kv[r : r + 128, :]
            else:
                kv_t[at - WIN_S : at - WIN_S + 128, :] = kv[r : r + 128, :]
    own = SAME_CORE * ROWS
    x = window[own : own + ROWS, :].astype(f32)
    normed = (x * inverse_norm(x) * gain).astype(bf16)
    normed_out[...] = normed
    project = mm(normed, w_qkv[:, 0:640])
    q_out[...] = turn(project, cosine[own : own + ROWS, :], sine[own : own + ROWS, :])[
        :, 0:QW
    ].astype(bf16)


def heads_kernel(x_in, cosine, sine, gain_row, w_qkv, q_out, kv_out, normed_out):
    x = x_in[...]
    normed = (x * inverse_norm(x) * gain_row[:, 0:D]).astype(bf16)
    normed_out[...] = normed
    project = mm(normed, w_qkv[...])
    both = turn(project[:, 0:768], cosine[...], sine[...])
    q_out[...] = both[:, 0:QW].astype(bf16)
    kv_out[...] = jnp.concatenate([both[:, QW:768], project[:, 768:PW]], axis=1).astype(bf16)


def allowed_of(segment, key_row, first_row):
    query = first_row + lax.broadcasted_iota(jnp.int32, (ROWS, 1), 0)
    return (key_row >= segment) & (key_row <= query)


def group_rows(value, group):
    return jnp.concatenate(
        [value[:, (GROUP * group + n) * HD : (GROUP * group + n + 1) * HD] for n in range(GROUP)],
        axis=0,
    )


def window_rows(kv_s, kv_t, begin):
    return jnp.concatenate(
        [kv_s[:, begin : begin + HD], kv_t[:, begin : begin + HD]], axis=0
    )


def bias_of(first, segment, key_row):
    bias = jnp.where(allowed_of(segment[...], key_row[...], first[0]), 0.0, -1e30).astype(f32)
    return jnp.concatenate([bias] * GROUP, axis=0)


def attend(q, kv_s, kv_t, bias, lse_out=None):
    pieces, held = [], []
    for group in range(KVH):
        keys = window_rows(kv_s, kv_t, group * HD)
        values = window_rows(kv_s, kv_t, KW + group * HD)
        scores = mm_t(group_rows(q, group), keys) + bias
        peak = jnp.max(scores, axis=-1, keepdims=True)
        powers = jnp.exp(scores - peak)
        total = jnp.sum(powers, axis=-1, keepdims=True)
        if lse_out is not None:
            lse_out[:, group : group + 1] = peak + jnp.log(total)
        held.append(powers * (1.0 / total))
        mixed = mm(held[-1].astype(bf16), values)
        for n in range(GROUP):
            pieces.append(mixed[n * ROWS : (n + 1) * ROWS, :])
    return jnp.concatenate(pieces, axis=1).astype(bf16), held


def feed_forward(
    x, mixed, gain_row, w_out, w_in, w_down, copies, middle_out, normed_out, gate_up_out, hidden_out
):
    copies[0].wait()
    middle = x + mm(mixed, w_out[...])
    middle_out[...] = middle
    normed = (middle * inverse_norm(middle) * gain_row[:, 0:D]).astype(bf16)
    normed_out[...] = normed
    copies[1].wait()
    gate_up = mm(normed, w_in[...])
    gate_up_out[...] = gate_up
    gate = gate_up[:, 0:FF]
    hidden = (gate * jax.nn.sigmoid(gate) * gate_up[:, FF:]).astype(bf16)
    hidden_out[...] = hidden
    copies[2].wait()
    return middle + mm(hidden, w_down[...])


def attend_kernel(
    first, x_in, q_in, kv_s, kv_t, segment, key_row, gain_row, w_out_at, w_in_at, w_down_at,
    x_out, mixed_out, lse_out, middle_out, normed_out, gate_up_out, hidden_out,
    w_out, w_in, w_down, sems,
):
    copies = fetch((w_out_at, w_in_at, w_down_at), (w_out, w_in, w_down), sems)
    for copy in copies:
        copy.start()
    q = q_in[...] * FACTOR
    mixed, _ = attend(q, kv_s, kv_t, bias_of(first, segment, key_row), lse_out)
    mixed_out[...] = mixed
    x_out[...] = feed_forward(
        x_in[...].astype(f32), mixed, gain_row, w_out, w_in, w_down, copies,
        middle_out, normed_out, gate_up_out, hidden_out,
    )


def norm_back(values, inverse, gain, grad):
    weighted = grad * gain
    return inverse * weighted - values * inverse**3 * jnp.mean(
        weighted * values, axis=-1, keepdims=True
    )


def feed_back(
    g, middle_in, gate_up, gain_row, w_out, w_in, w_down, waits,
    branch_out, grad_gu_out, attn_out, middle_grad_out, gain_out,
):
    branch = g.astype(bf16)
    branch_out[...] = branch
    for wait in waits[0]:
        wait.wait()
    grad_hidden = mm_t(branch, w_down[...])
    gate = gate_up[:, 0:FF]
    up = gate_up[:, FF:]
    sigma = jax.nn.sigmoid(gate)
    grad_gu_out[:, 0:FF] = (
        grad_hidden * up * sigma * (1.0 + gate * (1.0 - sigma))
    ).astype(bf16)
    grad_gu_out[:, FF:] = (grad_hidden * gate * sigma).astype(bf16)
    for wait in waits[1]:
        wait.wait()
    grad_two = mm_t(grad_gu_out[...], w_in[...])
    middle = middle_in[...]
    inverse = inverse_norm(middle)
    gain_out[...] = jnp.sum(grad_two * middle * inverse, axis=0, keepdims=True)
    grad_middle = g + norm_back(middle, inverse, gain_row[:, 0:D], grad_two)
    middle_grad_out[...] = grad_middle
    attn = grad_middle.astype(bf16)
    attn_out[...] = attn
    for wait in waits[2]:
        wait.wait()
    return mm_t(attn, w_out[...]).astype(bf16)


def attend_back(q, kv_s, kv_t, held, grad_mixed, cosine, sine, dq_out, dkv_s, dkv_t):
    dq, dk, dv = [], [], []
    for group in range(KVH):
        keys = window_rows(kv_s, kv_t, group * HD)
        values = window_rows(kv_s, kv_t, KW + group * HD)
        query = group_rows(q, group)
        grad = group_rows(grad_mixed, group)
        probs = held[group]
        grad_w = mm_t(grad, values)
        delta = jnp.sum(probs * grad_w, axis=-1, keepdims=True)
        grad_scores = (probs * (grad_w - delta)).astype(bf16)
        part = mm(grad_scores, keys) * FACTOR
        for n in range(GROUP):
            dq.append(part[n * ROWS : (n + 1) * ROWS, :])
        dk.append(mm(query.T, grad_scores))
        dv.append(mm(grad.T, probs.astype(bf16)))
    dkv = jnp.concatenate(dk + dv, axis=0).T
    dkv_s[...] = dkv[0:WIN_S, :]
    dkv_t[...] = dkv[WIN_S:, :].astype(bf16)
    wide = jnp.concatenate(dq + [jnp.zeros((ROWS, HD), f32)], axis=1)
    dq_out[...] = turn(wide, cosine[...], -sine[...])[:, 0:QW].astype(bf16)


def back_kernel(
    first, g_in, q_in, kv_s, kv_t, segment, key_row, cosine, sine, gain_row, lse, middle_in,
    gate_up_at, w_out_at, w_in_at, w_down_at,
    branch_out, grad_gu_out, attn_out, middle_grad_out, dq_out, dkv_s, dkv_t, gain_out,
    w_out, w_in, w_down, sems, gate_up, gate_sem,
):
    copies = fetch((w_out_at, w_in_at, w_down_at), (w_out, w_in, w_down), sems)
    gate_copy = pltpu.make_async_copy(gate_up_at, gate_up, gate_sem)
    copies[2].start()
    gate_copy.start()
    copies[1].start()
    copies[0].start()
    bias = bias_of(first, segment, key_row)
    q = q_in[...] * FACTOR
    held = []
    for group in range(KVH):
        keys = window_rows(kv_s, kv_t, group * HD)
        scores = mm_t(group_rows(q, group), keys) + bias
        held.append(jnp.exp(scores - lse[:, group : group + 1]))
    grad_mixed = feed_back(
        g_in[...].astype(f32), middle_in, gate_up, gain_row, w_out, w_in, w_down,
        ((copies[2], gate_copy), (copies[1],), (copies[0],)),
        branch_out, grad_gu_out, attn_out, middle_grad_out, gain_out,
    )
    attend_back(q, kv_s, kv_t, held, grad_mixed, cosine, sine, dq_out, dkv_s, dkv_t)


def last_kernel(
    first, x_in, g_in, q_in, kv_s, kv_t, segment, key_row, cosine, sine, gain_row,
    w_out_at, w_in_at, w_down_at,
    x_out, mixed_out, normed_out, hidden_out,
    branch_out, grad_gu_out, attn_out, middle_grad_out, dq_out, dkv_s, dkv_t, gain_out,
    w_out, w_in, w_down, sems, gate_up, middle,
):
    copies = fetch((w_out_at, w_in_at, w_down_at), (w_out, w_in, w_down), sems)
    for copy in copies:
        copy.start()
    q = q_in[...] * FACTOR
    mixed, held = attend(q, kv_s, kv_t, bias_of(first, segment, key_row))
    mixed_out[...] = mixed
    x_out[...] = feed_forward(
        x_in[...].astype(f32), mixed, gain_row, w_out, w_in, w_down, copies,
        middle, normed_out, gate_up, hidden_out,
    ).astype(bf16)
    grad_mixed = feed_back(
        g_in[...].astype(f32), middle, gate_up, gain_row, w_out, w_in, w_down, ((), (), ()),
        branch_out, grad_gu_out, attn_out, middle_grad_out, gain_out,
    )
    attend_back(q, kv_s, kv_t, held, grad_mixed, cosine, sine, dq_out, dkv_s, dkv_t)


def back_heads_kernel(
    core, x_in, dq, own, r8, r6, r4, r2, cosine, sine, gain_row, w_qkv, middle_grad, normed, edge,
    g_out, keep, send, flat, tile, project_out, gain_out,
):
    total = own[...]
    for piece in (r8, r6, r4, r2):
        total = total + piece[...].astype(f32)
    keys = jnp.concatenate([total[:, 0:KW], jnp.zeros((ROWS, HD), f32)], axis=1)
    keys = turn(keys, cosine[...], -sine[...])[:, 0:KW]
    project = jnp.concatenate(
        [dq[...].astype(f32), keys, total[:, KW:]], axis=1
    ).astype(bf16)
    project_out[...] = project
    grad = mm_t(project, w_qkv[...])
    x = x_in[...].astype(f32)
    inverse = inverse_norm(x)
    gain_out[...] = jnp.sum(grad * x * inverse, axis=0, keepdims=True)
    g_out[...] = middle_grad[...] + norm_back(x, inverse, gain_row[:, 0:D], grad)
    pack_first(core, normed, project_out, gain_out, edge, keep, send, flat, tile)


def put_gain(flat, gain, start):
    row = jnp.concatenate([gain[...], jnp.zeros((1, 64), f32)], axis=1)
    first = start // 2
    before = None
    for t in range(5):
        part = row[:, 128 * t : 128 * t + 128]
        place = slice(first + t, first + t + 1)
        if start % 2 == 0:
            flat[place, :] = part
        else:
            now = pltpu.roll(part, 64, 1)
            if before is None:
                flat[place, :] = now
            else:
                flat[place, :] = jnp.where(low_half((1, 128)), before, now)
            before = now


def put_matrix(flat, tile, left, right, start_half, width_half):
    rows, columns = left.shape[1], right.shape[1]
    turned = left[...].T
    for t in range((width_half + 1) // 2):
        wide = min(128, columns - 128 * t)
        tile[t, 0:rows, 0:wide] = mm(turned, right[:, 128 * t : 128 * t + wide])
    for parity in range(2):
        put_rows(
            flat, start_half + parity * width_half, rows // 2, width_half,
            lambda t, parity=parity: tile[t, pl.ds(parity, rows // 2, stride=2), :],
        )


def cut(flat, core, first_plane, planes, skip, keep, send):
    last = lax.broadcasted_iota(jnp.int32, (CHUNK, 128), 0) == CHUNK - 1
    for out, flip in ((keep, 0), (send, 1)):
        def one_owner(k, carry, out=out, flip=flip):
            d = 2 * (first_plane + k) + lax.rem(core[0] + flip, 2)
            base = pl.multiple_of(d * 216 - skip + 8, 8)
            odd = jnp.where(d < DEVICES // 2, base - 1, base + CHUNK - 1)
            value = jnp.where(last, flat[pl.ds(odd, 1), :], flat[pl.ds(base, CHUNK), :])
            out[pl.ds(pl.multiple_of(k * CHUNK, CHUNK), CHUNK), :] = value.astype(bf16)
            return carry

        lax.fori_loop(0, planes, one_owner, 0)


def pack_rest_kernel(
    core, mixed, attn, normed_two, grad_gu, hidden, branch, gain_two, keep, send, edge, flat, tile
):
    skip = 216 * SPLIT
    half = 2 * (7 - skip)
    put_gain(flat, gain_two, HALF_GAIN_TWO + half)
    put_matrix(flat, tile, mixed, attn, HALF_OUT + half, D // 64)
    put_matrix(flat, tile, hidden, branch, HALF_DOWN + half, D // 64)

    turned = normed_two[...].T

    def in_tile(c, carry):
        flat[pl.ds((HALF_IN + half) // 2 + c, D, stride=24), :] = mm(
            turned, grad_gu[:, pl.ds(pl.multiple_of(c * 128, 128), 128)]
        )
        return carry

    lax.fori_loop(0, 24, in_tile, 0)
    cut(flat, core, LOW_PLANES, DEVICES // 2 - LOW_PLANES, skip, keep, send)
    edge[...] = flat[0:EDGE, :]


def pack_first(core, normed, project, gain_one, edge, keep, send, flat, tile):
    skip = 216 * SPLIT
    flat[skip : skip + EDGE, :] = edge[...]
    put_gain(flat, gain_one, HALF_GAIN_ONE + 14)
    put_matrix(flat, tile, normed, project, HALF_QKV + 14, PW // 64)
    cut(flat, core, 0, LOW_PLANES, 0, keep, send)


def hop(value, by):
    pairs = [(i, i + by) for i in range(DEVICES) if 0 <= i + by < DEVICES]
    return lax.ppermute(value, "fsdp", pairs)


def swap(value):
    return lax.ppermute(value, "fsdp", [(i, i ^ 1) for i in range(DEVICES)])


def window_of(value, core, beside=()):
    blocks = [hop(value, by) for by in (8, 6, 4, 2)] + [value]
    same = jnp.concatenate(blocks, axis=0)
    rows = value.shape[0]
    gift = lax.dynamic_slice_in_dim(same, (1 - core) * rows, SAME_CORE * rows, 0)
    if beside:
        gift, _ = lax.optimization_barrier((gift, beside))
    return same, swap(gift)


def give_back(dkv_s, dkv_t, core):
    got = swap(dkv_t).astype(f32)
    blank = jnp.zeros((ROWS, 2 * KW), f32)
    early = jnp.concatenate([got, blank], axis=0)
    late = jnp.concatenate([blank, got], axis=0)
    total = dkv_s + jnp.where(core == 0, late, early)
    pieces = [
        hop(total[at * ROWS : (at + 1) * ROWS].astype(bf16), -by)
        for at, by in enumerate((8, 6, 4, 2))
    ]
    return total[SAME_CORE * ROWS :], pieces


def join_kernel(keep_first, got_first, keep_rest, got_rest, out):
    low = LOW_PLANES // JOIN

    @pl.when(pl.program_id(0) < low)
    def _():
        out[...] = keep_first[...] + got_first[...]

    @pl.when(pl.program_id(0) >= low)
    def _():
        out[...] = keep_rest[...] + got_rest[...]


def join(keep_first, got_first, keep_rest, got_rest):
    low = LOW_PLANES // JOIN
    block = (JOIN * CHUNK, 128)
    first = pl.BlockSpec(block, lambda i: (jnp.minimum(i, low - 1), 0))
    rest = pl.BlockSpec(block, lambda i: (jnp.maximum(i - low, 0), 0))
    return pl.pallas_call(
        join_kernel,
        grid=(DEVICES // 2 // JOIN,),
        out_shape=pltpu.HBM((DEVICES // 2 * CHUNK, 128), bf16),
        in_specs=[first, first, rest, rest],
        out_specs=pl.BlockSpec(block, lambda i: (i, 0)),
        compiler_params=pltpu.CompilerParams(vmem_limit_bytes=16 * 1024 * 1024),
        cost_estimate=pl.CostEstimate(flops=0, bytes_accessed=11_000_000, transcendentals=0),
    )(keep_first, got_first, keep_rest, got_rest)


def to_owners(total):
    groups = [list(range(0, DEVICES, 2)), list(range(1, DEVICES, 2))]
    return lax.all_to_all(
        total.reshape(DEVICES // 2, CHUNK, 128),
        "fsdp", split_axis=0, concat_axis=0, tiled=True, axis_index_groups=groups,
    )


def own_part(pieces, device):
    own = jnp.sum(pieces.astype(f32), axis=0)
    rows = jnp.concatenate([own[CHUNK - 1 :], own], axis=0)
    return lax.dynamic_slice_in_dim(rows.reshape(-1), 9 * device, SHARD, 0)


def tables(positions):
    half = HD // 2
    frequency = rope_base ** (-jnp.arange(half, dtype=f32) / half)
    angles = positions.astype(f32)[:, None] * frequency[None, :]
    return (
        jnp.concatenate([jnp.cos(angles)] * 4, axis=-1),
        jnp.concatenate([jnp.sin(angles)] * 4, axis=-1),
    )


def body(hidden_in, segment_ids, weights_flat, cotangent):
    device = lax.axis_index("fsdp")
    core = lax.rem(device, 2)
    first_row = device * ROWS
    layers = weights_flat.shape[0]
    sections = []
    for layer in range(layers):
        blank = jnp.zeros((SECTION * 128,), bf16)
        sections.append(lax.dynamic_update_slice(blank, weights_flat[layer], (9 * device,)))
    gathered = lax.all_gather(jnp.concatenate(sections), "fsdp", axis=0, tiled=True)
    gathered = gathered.reshape(DEVICES, layers, SECTION, 128)

    x_same, x_sibling = window_of(hidden_in, core)
    window = jnp.concatenate([x_same, x_sibling], axis=0)
    s_same, s_sibling = window_of(segment_ids, core)
    segments = jnp.concatenate([s_same, s_sibling], axis=0)
    order = jnp.arange(ROWS, dtype=jnp.int32)
    same_first = first_row - ROWS * jnp.array([8, 6, 4, 2, 0], jnp.int32)
    sibling_first = first_row - ROWS * jnp.array([7, 5, 3, 1], jnp.int32)
    key_row = jnp.concatenate([same_first, sibling_first])[:, None] + order[None, :]
    key_row = key_row.reshape(-1)
    cosine_all, sine_all = tables(key_row - segments)
    own = SAME_CORE * ROWS
    cosine, sine = cosine_all[own : own + ROWS], sine_all[own : own + ROWS]
    key_row = key_row[None, :]
    segment = segment_ids[:, None]
    first = first_row[None]
    core_in = core[None]

    x = hidden_in
    held = []
    for layer in range(layers):
        w_qkv, gain_one = unpack_first(gathered, layer)
        w_out, w_in, w_down, gain_two = unpack_rest(gathered, layer)
        if layer == 0:
            q, kv_s, kv_t, normed = call(
                heads_zero_kernel,
                [((ROWS, QW), bf16), ((WIN_S, 2 * KW), bf16), ((WIN_T, 2 * KW), bf16),
                 ((ROWS, D), bf16)],
                [window, cosine_all, sine_all, gain_one, w_qkv],
                flops=800_000_000, nbytes=6_000_000,
            )
        else:
            q, kv, normed = call(
                heads_kernel,
                [((ROWS, QW), bf16), ((ROWS, 2 * KW), bf16), ((ROWS, D), bf16)],
                [x, cosine, sine, gain_one, w_qkv],
                flops=150_000_000, nbytes=3_000_000,
            )
            kv_s, kv_t = window_of(kv, core, (w_out,))
        if layer == layers - 1:
            (layer_out, mixed, normed_two, hidden, *last_back) = call(
                last_kernel,
                [((ROWS, D), bf16), ((ROWS, QW), bf16), ((ROWS, D), bf16), ((ROWS, FF), bf16)]
                + [((ROWS, D), bf16), ((ROWS, 2 * FF), bf16), ((ROWS, D), bf16), ((ROWS, D), f32),
                 ((ROWS, QW), bf16), ((WIN_S, 2 * KW), f32), ((WIN_T, 2 * KW), bf16), ((1, D), f32)],
                [first, x, cotangent, q, kv_s, kv_t, segment, key_row, cosine, sine, gain_two,
                 w_out, w_in, w_down],
                scratch=WEIGHT_SCRATCH
                + (pltpu.VMEM((ROWS, 2 * FF), f32), pltpu.VMEM((ROWS, D), f32)),
                smem=1, apart=3, flops=5_000_000_000, nbytes=20_000_000,
            )
            held.append((x, q, kv_s, kv_t, normed, mixed, None, None, normed_two, None, hidden,
                         w_qkv, w_out, w_in, w_down, gain_one, gain_two))
            break
        x_next, mixed, lse, middle, normed_two, gate_up, hidden = call(
            attend_kernel,
            [((ROWS, D), f32), ((ROWS, QW), bf16), ((GROUP * ROWS, KVH), f32), ((ROWS, D), f32),
             ((ROWS, D), bf16), ((ROWS, 2 * FF), f32), ((ROWS, FF), bf16)],
            [first, x, q, kv_s, kv_t, segment, key_row, gain_two, w_out, w_in, w_down],
            scratch=WEIGHT_SCRATCH, smem=1, apart=3, flops=2_000_000_000, nbytes=12_000_000,
        )
        held.append((x, q, kv_s, kv_t, normed, mixed, lse, middle, normed_two, gate_up, hidden,
                     w_qkv, w_out, w_in, w_down, gain_one, gain_two))
        x = x_next

    g = cotangent
    grads = [None] * layers
    for layer in reversed(range(layers)):
        (x, q, kv_s, kv_t, normed, mixed, lse, middle, normed_two, gate_up, hidden,
         w_qkv, w_out, w_in, w_down, gain_one, gain_two) = held[layer]
        if layer == layers - 1:
            branch, grad_gu, attn, middle_grad, dq, dkv_s, dkv_t, grad_two = last_back
        else:
            branch, grad_gu, attn, middle_grad, dq, dkv_s, dkv_t, grad_two = call(
                back_kernel,
                [((ROWS, D), bf16), ((ROWS, 2 * FF), bf16), ((ROWS, D), bf16), ((ROWS, D), f32),
                 ((ROWS, QW), bf16), ((WIN_S, 2 * KW), f32), ((WIN_T, 2 * KW), bf16), ((1, D), f32)],
                [first, g, q, kv_s, kv_t, segment, key_row, cosine, sine, gain_two, lse, middle,
                 gate_up, w_out, w_in, w_down],
                scratch=WEIGHT_SCRATCH
                + (pltpu.VMEM((ROWS, 2 * FF), f32), pltpu.SemaphoreType.DMA),
                smem=1, apart=4, flops=3_000_000_000, nbytes=15_000_000,
            )
        rest_shape = (((DEVICES // 2 - LOW_PLANES) * CHUNK, 128), bf16)
        keep, send, edge = call(
            pack_rest_kernel,
            [rest_shape, rest_shape, ((EDGE, 128), f32)],
            [core_in, mixed, attn, normed_two, grad_gu, hidden, branch, grad_two],
            scratch=[
                pltpu.VMEM((216 * (DEVICES - SPLIT) + 40, 128), f32), pltpu.VMEM((5, FF, 128), f32)
            ],
            smem=1, flops=1_000_000_000, nbytes=25_000_000,
        )
        own_kv, pieces = give_back(dkv_s, dkv_t, core)
        send, pieces = lax.optimization_barrier((send, pieces))
        keep_rest, got_rest = keep, swap(send)
        if layer + 1 < layers:
            own_kv, grads[layer + 1] = lax.optimization_barrier((own_kv, grads[layer + 1]))
        low_shape = ((LOW_PLANES * CHUNK, 128), bf16)
        g, keep, send = call(
            back_heads_kernel,
            [((ROWS, D), f32), low_shape, low_shape],
            [core_in, x, dq, own_kv, *pieces, cosine, sine, gain_one, w_qkv, middle_grad, normed,
             edge],
            scratch=[
                pltpu.VMEM((216 * SPLIT + EDGE + 8, 128), f32), pltpu.VMEM((8, D, 128), f32),
                pltpu.VMEM((ROWS, PW), bf16), pltpu.VMEM((1, D), f32),
            ],
            smem=1, flops=350_000_000, nbytes=10_000_000,
        )
        total = join(keep, swap(send), keep_rest, got_rest)
        if layer > 0:
            g, total = lax.optimization_barrier((g, total))
        grads[layer] = to_owners(total)
    return (layer_out, g, jnp.stack([own_part(pieces, device) for pieces in grads]))


def solution(mesh):
    in_specs = (P("fsdp", None), P("fsdp"), P(None, "fsdp"), P("fsdp", None))
    out_specs = (P("fsdp", None), P("fsdp", None), P(None, "fsdp"))
    return jax.shard_map(body, mesh=mesh, in_specs=in_specs, out_specs=out_specs, check_vma=False)
```

```python
import functools

import jax
import jax.numpy as jnp
from jax import lax
from jax.experimental import pallas as pl
from jax.experimental.pallas import tpu as pltpu
from jax.sharding import PartitionSpec as P

D = 576
FF = 1536
QH = 9
KVH = 3
HD = 64
MAXLEN = 1024
QW = QH * HD
KW = KVH * HD
PW = QW + 2 * KW
GROUP = QH // KVH
DEVICES = 128
ROWS = 128
PARAMS = 3540096
SHARD = PARAMS // DEVICES
CHUNK = 224
SECTION = 240
SPLIT = 20
LOW_PLANES = 16
JOIN = 8
EDGE = 2616
SAME_CORE = 4
WIN_S = (SAME_CORE + 1) * ROWS
WIN_T = SAME_CORE * ROWS
WIN = WIN_S + WIN_T

bf16 = jnp.bfloat16
f32 = jnp.float32
epsilon = 1e-05
rope_base = 10000.0
FACTOR = HD ** (-0.5)
VMEM_LIMIT = 60 * 1024 * 1024

HALF_GAIN_ONE = 0
HALF_QKV = D // 64
HALF_OUT = HALF_QKV + D * PW // 64
HALF_GAIN_TWO = HALF_OUT + QW * D // 64
HALF_IN = HALF_GAIN_TWO + D // 64
HALF_DOWN = HALF_IN + D * 2 * FF // 64


def mm(a, b):
    return lax.dot_general(a, b, (((1,), (0,)), ((), ())), preferred_element_type=f32)


def mm_t(a, b):
    return lax.dot_general(a, b, (((1,), (1,)), ((), ())), preferred_element_type=f32)


def t_mm(a, b):
    return lax.dot_general(a, b, (((0,), (0,)), ((), ())), preferred_element_type=f32)


def call(kernel, out_shape, args, scratch=(), smem=0, apart=0, flops=0, nbytes=0):
    in_specs = [
        pl.BlockSpec(
            memory_space=pltpu.SMEM if at < smem
            else pl.ANY if at >= len(args) - apart else pltpu.VMEM
        )
        for at in range(len(args))
    ]
    return pl.pallas_call(
        kernel,
        out_shape=[jax.ShapeDtypeStruct(s, d) for s, d in out_shape],
        in_specs=in_specs,
        out_specs=[pl.BlockSpec(memory_space=pltpu.VMEM) for _ in out_shape],
        scratch_shapes=list(scratch),
        compiler_params=pltpu.CompilerParams(vmem_limit_bytes=VMEM_LIMIT),
        cost_estimate=pl.CostEstimate(flops=flops, bytes_accessed=nbytes, transcendentals=0),
    )(*args)


def low_half(shape):
    return lax.broadcasted_iota(jnp.int32, shape, 1) < 64


def take_rows(flat, start_half, pairs, width_half, store):
    tiles = (width_half + 1) // 2
    if start_half % 2 == 0:
        for t in range(tiles):
            store(t, flat[pl.ds(start_half // 2 + t, pairs, stride=width_half), :])
    else:
        before = None
        for t in range(tiles + 1):
            if t == tiles and width_half % 2 == 1:
                store(t - 1, before)
                break
            now = pltpu.roll(flat[pl.ds(start_half // 2 + t, pairs, stride=width_half), :], 64, 1)
            if before is not None:
                store(t - 1, jnp.where(low_half(now.shape), before, now))
            before = now


def put_rows(flat, start_half, pairs, width_half, load):
    tiles = (width_half + 1) // 2
    if start_half % 2 == 0:
        for t in range(tiles):
            place = pl.ds(start_half // 2 + t, pairs, stride=width_half)
            value = load(t)
            if 2 * t + 1 == width_half:
                value = jnp.where(low_half(value.shape), value, flat[place, :])
            flat[place, :] = value
    else:
        before = None
        for t in range(tiles + 1):
            if t == tiles and width_half % 2 == 1:
                break
            place = pl.ds(start_half // 2 + t, pairs, stride=width_half)
            now = pltpu.roll(load(t), 64, 1) if t < tiles else None
            if before is None:
                value = jnp.where(low_half(now.shape), flat[place, :], now)
            else:
                value = jnp.where(low_half(before.shape), before, now)
            flat[place, :] = value
            before = now


WEIGHT_SCRATCH = (
    pltpu.VMEM((QW, D), bf16),
    pltpu.VMEM((D, 2 * FF), bf16),
    pltpu.VMEM((FF, D), bf16),
    pltpu.SemaphoreType.DMA((3,)),
)


def fetch(sources, places, sems):
    copies = [
        pltpu.make_async_copy(source, place, sems.at[n])
        for n, (source, place) in enumerate(zip(sources, places))
    ]
    return copies


def gather_flat(gathered, layer, first, count, groups, flat, landing, sems):
    size = count // groups
    copies = []
    for n in range(groups):
        copies.append(
            pltpu.make_async_copy(
                gathered.at[pl.ds(first + n * size, size), layer],
                landing.at[pl.ds(n * size, size)],
                sems.at[n],
            )
        )
        copies[-1].start()
    tail = jnp.zeros((SECTION - 216, 128), f32)
    for n in range(groups):
        copies[n].wait()

        def one_shard(d, tail):
            rows = landing[d].astype(f32)
            base = pl.multiple_of(d * 216, 8)
            flat[pl.ds(base, 24), :] = tail + rows[0:24, :]
            flat[pl.ds(base + 24, 192), :] = rows[24:216, :]
            return rows[216:SECTION, :]

        tail = lax.fori_loop(n * size, (n + 1) * size, one_shard, tail)
    flat[count * 216 : count * 216 + 24, :] = tail


def take_matrix(flat, tile, out, start_half, width_half):
    rows, columns = out.shape

    def store(parity, at, value):
        tile[at, pl.ds(parity, rows // 2, stride=2), :] = value

    for parity in range(2):
        take_rows(
            flat, start_half + parity * width_half, rows // 2, width_half,
            functools.partial(store, parity),
        )
    for t in range((width_half + 1) // 2):
        wide = min(128, columns - 128 * t)
        out[:, 128 * t : 128 * t + wide] = tile[t, 0:rows, 0:wide].astype(bf16)


def take_gain(flat, gain, start):
    first = start // 2
    for t in range(5):
        if start % 2 == 0:
            value = flat[first + t : first + t + 1, :]
        else:
            here = pltpu.roll(flat[first + t : first + t + 1, :], 64, 1)
            after = pltpu.roll(flat[first + t + 1 : first + t + 2, :], 64, 1)
            value = jnp.where(low_half((1, 128)), here, after)
        gain[0:1, 128 * t : 128 * t + 128] = value


def unpack_first(layer, gathered, w_qkv, gain, landing, flat, tile, sems):
    gather_flat(gathered, layer, 0, SPLIT + 1, 3, flat, landing, sems)
    take_gain(flat, gain, HALF_GAIN_ONE)
    take_matrix(flat, tile, w_qkv, HALF_QKV, PW // 64)


def unpack_rest_kernel(
    layer, gathered, w_out_at, w_in_at, w_down_at, gain, landing, flat, tile, sems,
    w_out, w_in, w_down, out_sems,
):
    gather_flat(gathered, layer, SPLIT, DEVICES - SPLIT, 4, flat, landing, sems)
    skip = 2 * 216 * SPLIT

    def in_tile(c, carry):
        w_in[:, pl.ds(pl.multiple_of(c * 128, 128), 128)] = flat[
            pl.ds((HALF_IN - skip) // 2 + c, D, stride=24), :
        ].astype(bf16)
        return carry

    lax.fori_loop(0, 24, in_tile, 0)
    copies = fetch((w_out, w_in, w_down), (w_out_at, w_in_at, w_down_at), out_sems)
    copies[1].start()
    take_matrix(flat, tile, w_down, HALF_DOWN - skip, D // 64)
    copies[2].start()
    take_matrix(flat, tile, w_out, HALF_OUT - skip, D // 64)
    copies[0].start()
    take_gain(flat, gain, HALF_GAIN_TWO - skip)
    for copy in copies:
        copy.wait()


def unpack_call(
    kernel, layer, out_shape, gathered, count, groups, tiles, nbytes, apart=0, scratch=()
):
    return pl.pallas_call(
        functools.partial(kernel, layer),
        out_shape=[jax.ShapeDtypeStruct(s, d) for s, d in out_shape],
        in_specs=[pl.BlockSpec(memory_space=pl.ANY)],
        out_specs=[
            pl.BlockSpec(memory_space=pl.ANY if at < apart else pltpu.VMEM)
            for at in range(len(out_shape))
        ],
        scratch_shapes=[
            pltpu.VMEM((count, SECTION, 128), bf16),
            pltpu.VMEM((count * 216 + 32, 128), f32),
            pltpu.VMEM(tiles, f32),
            pltpu.SemaphoreType.DMA((groups,)),
            *scratch,
        ],
        compiler_params=pltpu.CompilerParams(vmem_limit_bytes=VMEM_LIMIT),
        cost_estimate=pl.CostEstimate(flops=2_000_000_000, bytes_accessed=nbytes, transcendentals=0),
    )(gathered)


FIRST_SCRATCH = (
    pltpu.VMEM((SPLIT + 1, SECTION, 128), bf16),
    pltpu.VMEM(((SPLIT + 1) * 216 + 32, 128), f32),
    pltpu.VMEM((8, D, 128), f32),
    pltpu.SemaphoreType.DMA((3,)),
)


def unpack_rest(gathered, layer):
    return unpack_call(
        unpack_rest_kernel, layer,
        [((QW, D), bf16), ((D, 2 * FF), bf16), ((FF, D), bf16), ((1, 640), f32)], gathered,
        DEVICES - SPLIT, 4, (5, FF, 128), 30_000_000, apart=3, scratch=WEIGHT_SCRATCH,
    )


def turn(value, cosine, sine):
    lane = lax.broadcasted_iota(jnp.int32, (value.shape[0], 128), 1)
    first = lax.rem(lane, 64) < 32
    pieces = []
    for t in range(value.shape[1] // 128):
        part = value[:, 128 * t : 128 * t + 128]
        swapped = jnp.where(first, -pltpu.roll(part, 96, 1), pltpu.roll(part, 32, 1))
        pieces.append(part * cosine + swapped * sine)
    return jnp.concatenate(pieces, axis=1)


def inverse_norm(values):
    return lax.rsqrt(jnp.mean(values * values, axis=-1, keepdims=True) + epsilon)


def heads_zero_kernel(
    window, cosine, sine, gathered, w_qkv, gain_row, q_out, kv_s, kv_t, normed_out, *scratch
):
    unpack_first(0, gathered, w_qkv, gain_row, *scratch)
    gain = gain_row[:, 0:D]
    for begin, rows in ((0, 384), (384, 384), (768, 384)):
        x = window[begin : begin + rows, :].astype(f32)
        normed = (x * inverse_norm(x) * gain).astype(bf16)
        project = mm(normed, w_qkv[:, 512:PW])
        both = turn(project[:, 0:256], cosine[begin : begin + rows, :], sine[begin : begin + rows, :])
        kv = jnp.concatenate([both[:, 64:256], project[:, 256:448]], axis=1).astype(bf16)
        for r in range(0, rows, 128):
            at = begin + r
            if at < WIN_S:
                kv_s[at : at + 128, :] = kv[r : r + 128, :]
            else:
                kv_t[at - WIN_S : at - WIN_S + 128, :] = kv[r : r + 128, :]
    own = SAME_CORE * ROWS
    x = window[own : own + ROWS, :].astype(f32)
    normed = (x * inverse_norm(x) * gain).astype(bf16)
    normed_out[...] = normed
    project = mm(normed, w_qkv[:, 0:640])
    q_out[...] = turn(project, cosine[own : own + ROWS, :], sine[own : own + ROWS, :])[
        :, 0:QW
    ].astype(bf16)


def heads_kernel(
    layer, x_in, cosine, sine, gathered, w_qkv, gain_row, q_out, kv_out, normed_out, *scratch
):
    unpack_first(layer, gathered, w_qkv, gain_row, *scratch)
    x = x_in[...]
    normed = (x * inverse_norm(x) * gain_row[:, 0:D]).astype(bf16)
    normed_out[...] = normed
    project = mm(normed, w_qkv[...])
    both = turn(project[:, 0:768], cosine[...], sine[...])
    q_out[...] = both[:, 0:QW].astype(bf16)
    kv_out[...] = jnp.concatenate([both[:, QW:768], project[:, 768:PW]], axis=1).astype(bf16)


def allowed_of(segment, key_row, first_row):
    query = first_row + lax.broadcasted_iota(jnp.int32, (ROWS, 1), 0)
    return (key_row >= segment) & (key_row <= query)


def group_rows(value, group):
    return jnp.concatenate(
        [value[:, (GROUP * group + n) * HD : (GROUP * group + n + 1) * HD] for n in range(GROUP)],
        axis=0,
    )


def window_rows(kv_s, kv_t, begin):
    return jnp.concatenate(
        [kv_s[:, begin : begin + HD], kv_t[:, begin : begin + HD]], axis=0
    )


def bias_of(first, segment, key_row):
    bias = jnp.where(allowed_of(segment[...], key_row[...], first[0]), 0.0, -1e30).astype(f32)
    return jnp.concatenate([bias] * GROUP, axis=0)


def attend(q, kv_s, kv_t, bias, lse_out=None):
    pieces, held = [], []
    for group in range(KVH):
        keys = window_rows(kv_s, kv_t, group * HD)
        values = window_rows(kv_s, kv_t, KW + group * HD)
        scores = mm_t(group_rows(q, group), keys) + bias
        peak = jnp.max(scores, axis=-1, keepdims=True)
        powers = jnp.exp(scores - peak)
        total = jnp.sum(powers, axis=-1, keepdims=True)
        if lse_out is not None:
            lse_out[:, group : group + 1] = peak + jnp.log(total)
        held.append(powers * (1.0 / total))
        mixed = mm(held[-1].astype(bf16), values)
        for n in range(GROUP):
            pieces.append(mixed[n * ROWS : (n + 1) * ROWS, :])
    return jnp.concatenate(pieces, axis=1).astype(bf16), held


def feed_forward(
    x, mixed, gain_row, w_out, w_in, w_down, copies, middle_out, normed_out, gate_up_out, hidden_out
):
    copies[0].wait()
    middle = x + mm(mixed, w_out[...])
    middle_out[...] = middle
    normed = (middle * inverse_norm(middle) * gain_row[:, 0:D]).astype(bf16)
    normed_out[...] = normed
    copies[1].wait()
    gate_up = mm(normed, w_in[...])
    gate_up_out[...] = gate_up
    gate = gate_up[:, 0:FF]
    hidden = (gate * jax.nn.sigmoid(gate) * gate_up[:, FF:]).astype(bf16)
    hidden_out[...] = hidden
    copies[2].wait()
    return middle + mm(hidden, w_down[...])


def attend_kernel(
    first, x_in, q_in, kv_s, kv_t, segment, key_row, gain_row, w_out_at, w_in_at, w_down_at,
    x_out, mixed_out, lse_out, middle_out, normed_out, gate_up_out, hidden_out,
    w_out, w_in, w_down, sems,
):
    copies = fetch((w_out_at, w_in_at, w_down_at), (w_out, w_in, w_down), sems)
    for copy in copies:
        copy.start()
    q = q_in[...] * FACTOR
    mixed, _ = attend(q, kv_s, kv_t, bias_of(first, segment, key_row), lse_out)
    mixed_out[...] = mixed
    x_out[...] = feed_forward(
        x_in[...].astype(f32), mixed, gain_row, w_out, w_in, w_down, copies,
        middle_out, normed_out, gate_up_out, hidden_out,
    )


def norm_back(values, inverse, gain, grad):
    weighted = grad * gain
    return inverse * weighted - values * inverse**3 * jnp.mean(
        weighted * values, axis=-1, keepdims=True
    )


def feed_back(
    g, middle_in, gate_up, gain_row, w_out, w_in, w_down, waits,
    branch_out, grad_gu_out, attn_out, middle_grad_out, gain_out,
):
    branch = g.astype(bf16)
    branch_out[...] = branch
    for wait in waits[0]:
        wait.wait()
    grad_hidden = mm_t(branch, w_down[...])
    gate = gate_up[:, 0:FF]
    up = gate_up[:, FF:]
    sigma = jax.nn.sigmoid(gate)
    grad_gu_out[:, 0:FF] = (
        grad_hidden * up * sigma * (1.0 + gate * (1.0 - sigma))
    ).astype(bf16)
    grad_gu_out[:, FF:] = (grad_hidden * gate * sigma).astype(bf16)
    for wait in waits[1]:
        wait.wait()
    grad_two = mm_t(grad_gu_out[...], w_in[...])
    middle = middle_in[...]
    inverse = inverse_norm(middle)
    gain_out[...] = jnp.sum(grad_two * middle * inverse, axis=0, keepdims=True)
    grad_middle = g + norm_back(middle, inverse, gain_row[:, 0:D], grad_two)
    middle_grad_out[...] = grad_middle
    attn = grad_middle.astype(bf16)
    attn_out[...] = attn
    for wait in waits[2]:
        wait.wait()
    return mm_t(attn, w_out[...]).astype(bf16)


def attend_back(q, kv_s, kv_t, held, grad_mixed, cosine, sine, dq_out, dkv_s, dkv_t):
    dq, dk, dv = [], [], []
    for group in range(KVH):
        keys = window_rows(kv_s, kv_t, group * HD)
        values = window_rows(kv_s, kv_t, KW + group * HD)
        query = group_rows(q, group)
        grad = group_rows(grad_mixed, group)
        probs = held[group]
        grad_w = mm_t(grad, values)
        delta = jnp.sum(probs * grad_w, axis=-1, keepdims=True)
        grad_scores = (probs * (grad_w - delta)).astype(bf16)
        part = mm(grad_scores, keys) * FACTOR
        for n in range(GROUP):
            dq.append(part[n * ROWS : (n + 1) * ROWS, :])
        dk.append(mm(query.T, grad_scores))
        dv.append(mm(grad.T, probs.astype(bf16)))
    dkv = jnp.concatenate(dk + dv, axis=0).T
    dkv_s[...] = dkv[0:WIN_S, :]
    dkv_t[...] = dkv[WIN_S:, :].astype(bf16)
    wide = jnp.concatenate(dq + [jnp.zeros((ROWS, HD), f32)], axis=1)
    dq_out[...] = turn(wide, cosine[...], -sine[...])[:, 0:QW].astype(bf16)


def back_kernel(
    first, g_in, q_in, kv_s, kv_t, segment, key_row, cosine, sine, gain_row, lse, middle_in,
    gate_up_at, w_out_at, w_in_at, w_down_at,
    branch_out, grad_gu_out, attn_out, middle_grad_out, dq_out, dkv_s, dkv_t, gain_out,
    w_out, w_in, w_down, sems, gate_up, gate_sem,
):
    copies = fetch((w_out_at, w_in_at, w_down_at), (w_out, w_in, w_down), sems)
    gate_copy = pltpu.make_async_copy(gate_up_at, gate_up, gate_sem)
    copies[2].start()
    gate_copy.start()
    copies[1].start()
    copies[0].start()
    bias = bias_of(first, segment, key_row)
    q = q_in[...] * FACTOR
    held = []
    for group in range(KVH):
        keys = window_rows(kv_s, kv_t, group * HD)
        scores = mm_t(group_rows(q, group), keys) + bias
        held.append(jnp.exp(scores - lse[:, group : group + 1]))
    grad_mixed = feed_back(
        g_in[...].astype(f32), middle_in, gate_up, gain_row, w_out, w_in, w_down,
        ((copies[2], gate_copy), (copies[1],), (copies[0],)),
        branch_out, grad_gu_out, attn_out, middle_grad_out, gain_out,
    )
    attend_back(q, kv_s, kv_t, held, grad_mixed, cosine, sine, dq_out, dkv_s, dkv_t)


def last_kernel(
    first, x_in, g_in, q_in, kv_s, kv_t, segment, key_row, cosine, sine, gain_row,
    w_out_at, w_in_at, w_down_at,
    x_out, mixed_out, normed_out, hidden_out,
    branch_out, grad_gu_out, attn_out, middle_grad_out, dq_out, dkv_s, dkv_t, gain_out,
    w_out, w_in, w_down, sems, gate_up, middle,
):
    copies = fetch((w_out_at, w_in_at, w_down_at), (w_out, w_in, w_down), sems)
    for copy in copies:
        copy.start()
    q = q_in[...] * FACTOR
    mixed, held = attend(q, kv_s, kv_t, bias_of(first, segment, key_row))
    mixed_out[...] = mixed
    x_out[...] = feed_forward(
        x_in[...].astype(f32), mixed, gain_row, w_out, w_in, w_down, copies,
        middle, normed_out, gate_up, hidden_out,
    ).astype(bf16)
    grad_mixed = feed_back(
        g_in[...].astype(f32), middle, gate_up, gain_row, w_out, w_in, w_down, ((), (), ()),
        branch_out, grad_gu_out, attn_out, middle_grad_out, gain_out,
    )
    attend_back(q, kv_s, kv_t, held, grad_mixed, cosine, sine, dq_out, dkv_s, dkv_t)


def back_heads_kernel(
    core, x_in, dq, own, r8, r6, r4, r2, cosine, sine, gain_row, w_qkv, middle_grad, normed, edge,
    g_out, keep, send, flat, tile, project_out, gain_out,
):
    total = own[...]
    for piece in (r8, r6, r4, r2):
        total = total + piece[...].astype(f32)
    keys = jnp.concatenate([total[:, 0:KW], jnp.zeros((ROWS, HD), f32)], axis=1)
    keys = turn(keys, cosine[...], -sine[...])[:, 0:KW]
    project = jnp.concatenate(
        [dq[...].astype(f32), keys, total[:, KW:]], axis=1
    ).astype(bf16)
    project_out[...] = project
    grad = mm_t(project, w_qkv[...])
    x = x_in[...].astype(f32)
    inverse = inverse_norm(x)
    gain_out[...] = jnp.sum(grad * x * inverse, axis=0, keepdims=True)
    g_out[...] = middle_grad[...] + norm_back(x, inverse, gain_row[:, 0:D], grad)
    pack_first(core, normed, project_out, gain_out, edge, keep, send, flat, tile)


def put_gain(flat, gain, start):
    row = jnp.concatenate([gain[...], jnp.zeros((1, 64), f32)], axis=1)
    first = start // 2
    before = None
    for t in range(5):
        part = row[:, 128 * t : 128 * t + 128]
        place = slice(first + t, first + t + 1)
        if start % 2 == 0:
            flat[place, :] = part
        else:
            now = pltpu.roll(part, 64, 1)
            if before is None:
                flat[place, :] = now
            else:
                flat[place, :] = jnp.where(low_half((1, 128)), before, now)
            before = now


def put_matrix(flat, tile, left, right, start_half, width_half):
    rows, columns = left.shape[1], right.shape[1]
    turned = left[...].T
    for t in range((width_half + 1) // 2):
        wide = min(128, columns - 128 * t)
        tile[t, 0:rows, 0:wide] = mm(turned, right[:, 128 * t : 128 * t + wide])
    for parity in range(2):
        put_rows(
            flat, start_half + parity * width_half, rows // 2, width_half,
            lambda t, parity=parity: tile[t, pl.ds(parity, rows // 2, stride=2), :],
        )


def cut(flat, core, first_plane, planes, skip, keep, send):
    last = lax.broadcasted_iota(jnp.int32, (CHUNK, 128), 0) == CHUNK - 1
    for out, flip in ((keep, 0), (send, 1)):
        def one_owner(k, carry, out=out, flip=flip):
            d = 2 * (first_plane + k) + lax.rem(core[0] + flip, 2)
            base = pl.multiple_of(d * 216 - skip + 8, 8)
            odd = jnp.where(d < DEVICES // 2, base - 1, base + CHUNK - 1)
            value = jnp.where(last, flat[pl.ds(odd, 1), :], flat[pl.ds(base, CHUNK), :])
            out[pl.ds(pl.multiple_of(k * CHUNK, CHUNK), CHUNK), :] = value.astype(bf16)
            return carry

        lax.fori_loop(0, planes, one_owner, 0)


def pack_rest_kernel(
    core, mixed, attn, normed_two, grad_gu, hidden, branch, gain_two, keep, send, edge, flat, tile
):
    skip = 216 * SPLIT
    half = 2 * (7 - skip)
    put_gain(flat, gain_two, HALF_GAIN_TWO + half)
    put_matrix(flat, tile, mixed, attn, HALF_OUT + half, D // 64)
    put_matrix(flat, tile, hidden, branch, HALF_DOWN + half, D // 64)

    turned = normed_two[...].T

    def in_tile(c, carry):
        flat[pl.ds((HALF_IN + half) // 2 + c, D, stride=24), :] = mm(
            turned, grad_gu[:, pl.ds(pl.multiple_of(c * 128, 128), 128)]
        )
        return carry

    lax.fori_loop(0, 24, in_tile, 0)
    cut(flat, core, LOW_PLANES, DEVICES // 2 - LOW_PLANES, skip, keep, send)
    edge[...] = flat[0:EDGE, :]


def pack_first(core, normed, project, gain_one, edge, keep, send, flat, tile):
    skip = 216 * SPLIT
    flat[skip : skip + EDGE, :] = edge[...]
    put_gain(flat, gain_one, HALF_GAIN_ONE + 14)
    put_matrix(flat, tile, normed, project, HALF_QKV + 14, PW // 64)
    cut(flat, core, 0, LOW_PLANES, 0, keep, send)


def hop(value, by):
    pairs = [(i, i + by) for i in range(DEVICES) if 0 <= i + by < DEVICES]
    return lax.ppermute(value, "fsdp", pairs)


def swap(value):
    return lax.ppermute(value, "fsdp", [(i, i ^ 1) for i in range(DEVICES)])


def window_of(value, core, beside=()):
    blocks = [hop(value, by) for by in (8, 6, 4, 2)] + [value]
    same = jnp.concatenate(blocks, axis=0)
    rows = value.shape[0]
    gift = lax.dynamic_slice_in_dim(same, (1 - core) * rows, SAME_CORE * rows, 0)
    if beside:
        gift, _ = lax.optimization_barrier((gift, beside))
    return same, swap(gift)


def give_back(dkv_s, dkv_t, core):
    got = swap(dkv_t).astype(f32)
    blank = jnp.zeros((ROWS, 2 * KW), f32)
    early = jnp.concatenate([got, blank], axis=0)
    late = jnp.concatenate([blank, got], axis=0)
    total = dkv_s + jnp.where(core == 0, late, early)
    pieces = [
        hop(total[at * ROWS : (at + 1) * ROWS].astype(bf16), -by)
        for at, by in enumerate((8, 6, 4, 2))
    ]
    return total[SAME_CORE * ROWS :], pieces


def add_kernel(keep, got, *refs):
    refs[-1][...] = keep[...] + got[...]


def join(keep, got, first_plane, total=None):
    block = (JOIN * CHUNK, 128)
    part = pl.BlockSpec(block, lambda i: (i, 0))
    given = () if total is None else (total,)
    return pl.pallas_call(
        add_kernel,
        grid=(keep.shape[0] // block[0],),
        out_shape=pltpu.HBM((DEVICES // 2 * CHUNK, 128), bf16),
        in_specs=[part, part] + [pl.BlockSpec(memory_space=pl.ANY) for _ in given],
        out_specs=pl.BlockSpec(block, lambda i: (i + first_plane // JOIN, 0)),
        input_output_aliases={2: 0} if given else {},
        compiler_params=pltpu.CompilerParams(vmem_limit_bytes=16 * 1024 * 1024),
        cost_estimate=pl.CostEstimate(
            flops=0, bytes_accessed=6 * keep.size, transcendentals=0
        ),
    )(keep, got, *given)


def to_owners(total):
    groups = [list(range(0, DEVICES, 2)), list(range(1, DEVICES, 2))]
    return lax.all_to_all(
        total.reshape(DEVICES // 2, CHUNK, 128),
        "fsdp", split_axis=0, concat_axis=0, tiled=True, axis_index_groups=groups,
    )


def own_part(pieces, device):
    own = jnp.sum(pieces.astype(f32), axis=0)
    rows = jnp.concatenate([own[CHUNK - 1 :], own], axis=0)
    return lax.dynamic_slice_in_dim(rows.reshape(-1), 9 * device, SHARD, 0)


def tables(positions):
    half = HD // 2
    frequency = rope_base ** (-jnp.arange(half, dtype=f32) / half)
    angles = positions.astype(f32)[:, None] * frequency[None, :]
    return (
        jnp.concatenate([jnp.cos(angles)] * 4, axis=-1),
        jnp.concatenate([jnp.sin(angles)] * 4, axis=-1),
    )


def body(hidden_in, segment_ids, weights_flat, cotangent):
    device = lax.axis_index("fsdp")
    core = lax.rem(device, 2)
    first_row = device * ROWS
    layers = weights_flat.shape[0]
    sections = []
    for layer in range(layers):
        blank = jnp.zeros((SECTION * 128,), bf16)
        sections.append(lax.dynamic_update_slice(blank, weights_flat[layer], (9 * device,)))
    gathered = lax.all_gather(jnp.concatenate(sections), "fsdp", axis=0, tiled=True)
    gathered = gathered.reshape(DEVICES, layers, SECTION, 128)

    x_same, x_sibling = window_of(hidden_in, core)
    window = jnp.concatenate([x_same, x_sibling], axis=0)
    s_same, s_sibling = window_of(segment_ids, core)
    segments = jnp.concatenate([s_same, s_sibling], axis=0)
    order = jnp.arange(ROWS, dtype=jnp.int32)
    same_first = first_row - ROWS * jnp.array([8, 6, 4, 2, 0], jnp.int32)
    sibling_first = first_row - ROWS * jnp.array([7, 5, 3, 1], jnp.int32)
    key_row = jnp.concatenate([same_first, sibling_first])[:, None] + order[None, :]
    key_row = key_row.reshape(-1)
    cosine_all, sine_all = tables(key_row - segments)
    own = SAME_CORE * ROWS
    cosine, sine = cosine_all[own : own + ROWS], sine_all[own : own + ROWS]
    key_row = key_row[None, :]
    segment = segment_ids[:, None]
    first = first_row[None]
    core_in = core[None]

    x = hidden_in
    held = []
    for layer in range(layers):
        w_out, w_in, w_down, gain_two = unpack_rest(gathered, layer)
        if layer == 0:
            w_qkv, gain_one, q, kv_s, kv_t, normed = call(
                heads_zero_kernel,
                [((D, PW), bf16), ((1, 640), f32), ((ROWS, QW), bf16), ((WIN_S, 2 * KW), bf16), ((WIN_T, 2 * KW), bf16),
                 ((ROWS, D), bf16)],
                [window, cosine_all, sine_all, gathered],
                scratch=FIRST_SCRATCH, apart=1, flops=800_000_000, nbytes=6_000_000,
            )
        else:
            w_qkv, gain_one, q, kv, normed = call(
                functools.partial(heads_kernel, layer),
                [((D, PW), bf16), ((1, 640), f32), ((ROWS, QW), bf16), ((ROWS, 2 * KW), bf16), ((ROWS, D), bf16)],
                [x, cosine, sine, gathered],
                scratch=FIRST_SCRATCH, apart=1, flops=150_000_000, nbytes=3_000_000,
            )
            kv_s, kv_t = window_of(kv, core, (w_out,))
        if layer == layers - 1:
            (layer_out, mixed, normed_two, hidden, *last_back) = call(
                last_kernel,
                [((ROWS, D), bf16), ((ROWS, QW), bf16), ((ROWS, D), bf16), ((ROWS, FF), bf16)]
                + [((ROWS, D), bf16), ((ROWS, 2 * FF), bf16), ((ROWS, D), bf16), ((ROWS, D), f32),
                 ((ROWS, QW), bf16), ((WIN_S, 2 * KW), f32), ((WIN_T, 2 * KW), bf16), ((1, D), f32)],
                [first, x, cotangent, q, kv_s, kv_t, segment, key_row, cosine, sine, gain_two,
                 w_out, w_in, w_down],
                scratch=WEIGHT_SCRATCH
                + (pltpu.VMEM((ROWS, 2 * FF), f32), pltpu.VMEM((ROWS, D), f32)),
                smem=1, apart=3, flops=5_000_000_000, nbytes=20_000_000,
            )
            held.append((x, q, kv_s, kv_t, normed, mixed, None, None, normed_two, None, hidden,
                         w_qkv, w_out, w_in, w_down, gain_one, gain_two))
            break
        x_next, mixed, lse, middle, normed_two, gate_up, hidden = call(
            attend_kernel,
            [((ROWS, D), f32), ((ROWS, QW), bf16), ((GROUP * ROWS, KVH), f32), ((ROWS, D), f32),
             ((ROWS, D), bf16), ((ROWS, 2 * FF), f32), ((ROWS, FF), bf16)],
            [first, x, q, kv_s, kv_t, segment, key_row, gain_two, w_out, w_in, w_down],
            scratch=WEIGHT_SCRATCH, smem=1, apart=3, flops=2_000_000_000, nbytes=12_000_000,
        )
        held.append((x, q, kv_s, kv_t, normed, mixed, lse, middle, normed_two, gate_up, hidden,
                     w_qkv, w_out, w_in, w_down, gain_one, gain_two))
        x = x_next

    g = cotangent
    grads = [None] * layers
    for layer in reversed(range(layers)):
        (x, q, kv_s, kv_t, normed, mixed, lse, middle, normed_two, gate_up, hidden,
         w_qkv, w_out, w_in, w_down, gain_one, gain_two) = held[layer]
        if layer == layers - 1:
            branch, grad_gu, attn, middle_grad, dq, dkv_s, dkv_t, grad_two = last_back
        else:
            branch, grad_gu, attn, middle_grad, dq, dkv_s, dkv_t, grad_two = call(
                back_kernel,
                [((ROWS, D), bf16), ((ROWS, 2 * FF), bf16), ((ROWS, D), bf16), ((ROWS, D), f32),
                 ((ROWS, QW), bf16), ((WIN_S, 2 * KW), f32), ((WIN_T, 2 * KW), bf16), ((1, D), f32)],
                [first, g, q, kv_s, kv_t, segment, key_row, cosine, sine, gain_two, lse, middle,
                 gate_up, w_out, w_in, w_down],
                scratch=WEIGHT_SCRATCH
                + (pltpu.VMEM((ROWS, 2 * FF), f32), pltpu.SemaphoreType.DMA),
                smem=1, apart=4, flops=3_000_000_000, nbytes=15_000_000,
            )
        rest_shape = (((DEVICES // 2 - LOW_PLANES) * CHUNK, 128), bf16)
        keep, send, edge = call(
            pack_rest_kernel,
            [rest_shape, rest_shape, ((EDGE, 128), f32)],
            [core_in, mixed, attn, normed_two, grad_gu, hidden, branch, grad_two],
            scratch=[
                pltpu.VMEM((216 * (DEVICES - SPLIT) + 40, 128), f32), pltpu.VMEM((5, FF, 128), f32)
            ],
            smem=1, flops=1_000_000_000, nbytes=25_000_000,
        )
        own_kv, pieces = give_back(dkv_s, dkv_t, core)
        send, pieces = lax.optimization_barrier((send, pieces))
        keep_rest, got_rest = keep, swap(send)
        if layer + 1 < layers:
            own_kv, grads[layer + 1] = lax.optimization_barrier((own_kv, grads[layer + 1]))
        low_shape = ((LOW_PLANES * CHUNK, 128), bf16)
        g, keep, send = call(
            back_heads_kernel,
            [((ROWS, D), f32), low_shape, low_shape],
            [core_in, x, dq, own_kv, *pieces, cosine, sine, gain_one, w_qkv, middle_grad, normed,
             edge],
            scratch=[
                pltpu.VMEM((216 * SPLIT + EDGE + 8, 128), f32), pltpu.VMEM((8, D, 128), f32),
                pltpu.VMEM((ROWS, PW), bf16), pltpu.VMEM((1, D), f32),
            ],
            smem=1, flops=350_000_000, nbytes=10_000_000,
        )
        total = join(keep, swap(send), 0, join(keep_rest, got_rest, LOW_PLANES))
        if layer > 0:
            g, total = lax.optimization_barrier((g, total))
        grads[layer] = to_owners(total)
    return (layer_out, g, jnp.stack([own_part(pieces, device) for pieces in grads]))


def solution(mesh):
    in_specs = (P("fsdp", None), P("fsdp"), P(None, "fsdp"), P("fsdp", None))
    out_specs = (P("fsdp", None), P("fsdp", None), P(None, "fsdp"))
    return jax.shard_map(body, mesh=mesh, in_specs=in_specs, out_specs=out_specs, check_vma=False)
```

```python
import functools

import jax
import jax.numpy as jnp
from jax import lax
from jax.experimental import pallas as pl
from jax.experimental.pallas import tpu as pltpu
from jax.sharding import PartitionSpec as P

D = 576
FF = 1536
QH = 9
KVH = 3
HD = 64
MAXLEN = 1024
QW = QH * HD
KW = KVH * HD
PW = QW + 2 * KW
GROUP = QH // KVH
DEVICES = 128
ROWS = 128
PARAMS = 3540096
SHARD = PARAMS // DEVICES
CHUNK = 224
SECTION = 240
SPLIT = 20
LOW_PLANES = 16
JOIN = 8
EDGE = 2616
SAME_CORE = 4
WIN_S = (SAME_CORE + 1) * ROWS
WIN_T = SAME_CORE * ROWS
WIN = WIN_S + WIN_T

bf16 = jnp.bfloat16
f32 = jnp.float32
epsilon = 1e-05
rope_base = 10000.0
FACTOR = HD ** (-0.5)
VMEM_LIMIT = 60 * 1024 * 1024

HALF_GAIN_ONE = 0
HALF_QKV = D // 64
HALF_OUT = HALF_QKV + D * PW // 64
HALF_GAIN_TWO = HALF_OUT + QW * D // 64
HALF_IN = HALF_GAIN_TWO + D // 64
HALF_DOWN = HALF_IN + D * 2 * FF // 64


def mm(a, b):
    return lax.dot_general(a, b, (((1,), (0,)), ((), ())), preferred_element_type=f32)


def mm_t(a, b):
    return lax.dot_general(a, b, (((1,), (1,)), ((), ())), preferred_element_type=f32)


def t_mm(a, b):
    return lax.dot_general(a, b, (((0,), (0,)), ((), ())), preferred_element_type=f32)


def call(kernel, out_shape, args, scratch=(), smem=0, apart=0, flops=0, nbytes=0):
    in_specs = [
        pl.BlockSpec(
            memory_space=pltpu.SMEM if at < smem
            else pl.ANY if at >= len(args) - apart else pltpu.VMEM
        )
        for at in range(len(args))
    ]
    return pl.pallas_call(
        kernel,
        out_shape=[jax.ShapeDtypeStruct(s, d) for s, d in out_shape],
        in_specs=in_specs,
        out_specs=[pl.BlockSpec(memory_space=pltpu.VMEM) for _ in out_shape],
        scratch_shapes=list(scratch),
        compiler_params=pltpu.CompilerParams(vmem_limit_bytes=VMEM_LIMIT),
        cost_estimate=pl.CostEstimate(flops=flops, bytes_accessed=nbytes, transcendentals=0),
    )(*args)


def low_half(shape):
    return lax.broadcasted_iota(jnp.int32, shape, 1) < 64


def take_rows(flat, start_half, pairs, width_half, store):
    tiles = (width_half + 1) // 2
    if start_half % 2 == 0:
        for t in range(tiles):
            store(t, flat[pl.ds(start_half // 2 + t, pairs, stride=width_half), :])
    else:
        before = None
        for t in range(tiles + 1):
            if t == tiles and width_half % 2 == 1:
                store(t - 1, before)
                break
            now = pltpu.roll(flat[pl.ds(start_half // 2 + t, pairs, stride=width_half), :], 64, 1)
            if before is not None:
                store(t - 1, jnp.where(low_half(now.shape), before, now))
            before = now


def put_rows(flat, start_half, pairs, width_half, load):
    tiles = (width_half + 1) // 2
    if start_half % 2 == 0:
        for t in range(tiles):
            place = pl.ds(start_half // 2 + t, pairs, stride=width_half)
            value = load(t)
            if 2 * t + 1 == width_half:
                value = jnp.where(low_half(value.shape), value, flat[place, :])
            flat[place, :] = value
    else:
        before = None
        for t in range(tiles + 1):
            if t == tiles and width_half % 2 == 1:
                break
            place = pl.ds(start_half // 2 + t, pairs, stride=width_half)
            now = pltpu.roll(load(t), 64, 1) if t < tiles else None
            if before is None:
                value = jnp.where(low_half(now.shape), flat[place, :], now)
            else:
                value = jnp.where(low_half(before.shape), before, now)
            flat[place, :] = value
            before = now


WEIGHT_SCRATCH = (
    pltpu.VMEM((QW, D), bf16),
    pltpu.VMEM((D, 2 * FF), bf16),
    pltpu.VMEM((FF, D), bf16),
    pltpu.SemaphoreType.DMA((3,)),
)


def fetch(sources, places, sems):
    copies = [
        pltpu.make_async_copy(source, place, sems.at[n])
        for n, (source, place) in enumerate(zip(sources, places))
    ]
    return copies


def gather_flat(gathered, layer, first, count, groups, flat, landing, sems):
    size = count // groups
    copies = []
    for n in range(groups):
        copies.append(
            pltpu.make_async_copy(
                gathered.at[pl.ds(first + n * size, size), layer],
                landing.at[pl.ds(n * size, size)],
                sems.at[n],
            )
        )
        copies[-1].start()
    tail = jnp.zeros((SECTION - 216, 128), f32)
    for n in range(groups):
        copies[n].wait()

        def one_shard(d, tail):
            rows = landing[d].astype(f32)
            base = pl.multiple_of(d * 216, 8)
            flat[pl.ds(base, 24), :] = tail + rows[0:24, :]
            flat[pl.ds(base + 24, 192), :] = rows[24:216, :]
            return rows[216:SECTION, :]

        tail = lax.fori_loop(n * size, (n + 1) * size, one_shard, tail)
    flat[count * 216 : count * 216 + 24, :] = tail


def take_matrix(flat, tile, out, start_half, width_half):
    rows, columns = out.shape

    def store(parity, at, value):
        tile[at, pl.ds(parity, rows // 2, stride=2), :] = value

    for parity in range(2):
        take_rows(
            flat, start_half + parity * width_half, rows // 2, width_half,
            functools.partial(store, parity),
        )
    for t in range((width_half + 1) // 2):
        wide = min(128, columns - 128 * t)
        out[:, 128 * t : 128 * t + wide] = tile[t, 0:rows, 0:wide].astype(bf16)


def take_gain(flat, gain, start):
    first = start // 2
    for t in range(5):
        if start % 2 == 0:
            value = flat[first + t : first + t + 1, :]
        else:
            here = pltpu.roll(flat[first + t : first + t + 1, :], 64, 1)
            after = pltpu.roll(flat[first + t + 1 : first + t + 2, :], 64, 1)
            value = jnp.where(low_half((1, 128)), here, after)
        gain[0:1, 128 * t : 128 * t + 128] = value


def unpack_first(layer, gathered, w_qkv, gain, landing, flat, tile, sems):
    gather_flat(gathered, layer, 0, SPLIT + 1, 3, flat, landing, sems)
    take_gain(flat, gain, HALF_GAIN_ONE)
    take_matrix(flat, tile, w_qkv, HALF_QKV, PW // 64)


def unpack_rest_kernel(
    layer, gathered, w_out_at, w_in_at, w_down_at, gain, landing, flat, tile, sems,
    w_out, w_in, w_down, out_sems,
):
    gather_flat(gathered, layer, SPLIT, DEVICES - SPLIT, 4, flat, landing, sems)
    skip = 2 * 216 * SPLIT

    def in_tile(c, carry):
        w_in[:, pl.ds(pl.multiple_of(c * 128, 128), 128)] = flat[
            pl.ds((HALF_IN - skip) // 2 + c, D, stride=24), :
        ].astype(bf16)
        return carry

    lax.fori_loop(0, 24, in_tile, 0)
    copies = fetch((w_out, w_in, w_down), (w_out_at, w_in_at, w_down_at), out_sems)
    copies[1].start()
    take_matrix(flat, tile, w_down, HALF_DOWN - skip, D // 64)
    copies[2].start()
    take_matrix(flat, tile, w_out, HALF_OUT - skip, D // 64)
    copies[0].start()
    take_gain(flat, gain, HALF_GAIN_TWO - skip)
    for copy in copies:
        copy.wait()


def unpack_call(
    kernel, layer, out_shape, gathered, count, groups, tiles, nbytes, apart=0, scratch=()
):
    return pl.pallas_call(
        functools.partial(kernel, layer),
        out_shape=[jax.ShapeDtypeStruct(s, d) for s, d in out_shape],
        in_specs=[pl.BlockSpec(memory_space=pl.ANY)],
        out_specs=[
            pl.BlockSpec(memory_space=pl.ANY if at < apart else pltpu.VMEM)
            for at in range(len(out_shape))
        ],
        scratch_shapes=[
            pltpu.VMEM((count, SECTION, 128), bf16),
            pltpu.VMEM((count * 216 + 32, 128), f32),
            pltpu.VMEM(tiles, f32),
            pltpu.SemaphoreType.DMA((groups,)),
            *scratch,
        ],
        compiler_params=pltpu.CompilerParams(vmem_limit_bytes=VMEM_LIMIT),
        cost_estimate=pl.CostEstimate(flops=2_000_000_000, bytes_accessed=nbytes, transcendentals=0),
    )(gathered)


FIRST_SCRATCH = (
    pltpu.VMEM((SPLIT + 1, SECTION, 128), bf16),
    pltpu.VMEM(((SPLIT + 1) * 216 + 32, 128), f32),
    pltpu.VMEM((8, D, 128), f32),
    pltpu.SemaphoreType.DMA((3,)),
)


def unpack_rest(gathered, layer):
    return unpack_call(
        unpack_rest_kernel, layer,
        [((QW, D), bf16), ((D, 2 * FF), bf16), ((FF, D), bf16), ((1, 640), f32)], gathered,
        DEVICES - SPLIT, 4, (5, FF, 128), 30_000_000, apart=3, scratch=WEIGHT_SCRATCH,
    )


def turn(value, cosine, sine):
    lane = lax.broadcasted_iota(jnp.int32, (value.shape[0], 128), 1)
    first = lax.rem(lane, 64) < 32
    pieces = []
    for t in range(value.shape[1] // 128):
        part = value[:, 128 * t : 128 * t + 128]
        swapped = jnp.where(first, -pltpu.roll(part, 96, 1), pltpu.roll(part, 32, 1))
        pieces.append(part * cosine + swapped * sine)
    return jnp.concatenate(pieces, axis=1)


def inverse_norm(values):
    return lax.rsqrt(jnp.mean(values * values, axis=-1, keepdims=True) + epsilon)


def heads_zero_kernel(
    window, cosine, sine, gathered, w_qkv, gain_row, q_out, kv_s, kv_t, normed_out, *scratch
):
    unpack_first(0, gathered, w_qkv, gain_row, *scratch)
    gain = gain_row[:, 0:D]
    for begin, rows in ((0, 384), (384, 384), (768, 384)):
        x = window[begin : begin + rows, :].astype(f32)
        normed = (x * inverse_norm(x) * gain).astype(bf16)
        project = mm(normed, w_qkv[:, 512:PW])
        both = turn(project[:, 0:256], cosine[begin : begin + rows, :], sine[begin : begin + rows, :])
        kv = jnp.concatenate([both[:, 64:256], project[:, 256:448]], axis=1).astype(bf16)
        for r in range(0, rows, 128):
            at = begin + r
            if at < WIN_S:
                kv_s[at : at + 128, :] = kv[r : r + 128, :]
            else:
                kv_t[at - WIN_S : at - WIN_S + 128, :] = kv[r : r + 128, :]
    own = SAME_CORE * ROWS
    x = window[own : own + ROWS, :].astype(f32)
    normed = (x * inverse_norm(x) * gain).astype(bf16)
    normed_out[...] = normed
    project = mm(normed, w_qkv[:, 0:640])
    q_out[...] = turn(project, cosine[own : own + ROWS, :], sine[own : own + ROWS, :])[
        :, 0:QW
    ].astype(bf16)


def heads_kernel(
    layer, x_in, cosine, sine, gathered, w_qkv, gain_row, q_out, kv_out, normed_out, *scratch
):
    unpack_first(layer, gathered, w_qkv, gain_row, *scratch)
    x = x_in[...]
    normed = (x * inverse_norm(x) * gain_row[:, 0:D]).astype(bf16)
    normed_out[...] = normed
    project = mm(normed, w_qkv[...])
    both = turn(project[:, 0:768], cosine[...], sine[...])
    q_out[...] = both[:, 0:QW].astype(bf16)
    kv_out[...] = jnp.concatenate([both[:, QW:768], project[:, 768:PW]], axis=1).astype(bf16)


def allowed_of(segment, key_row, first_row):
    query = first_row + lax.broadcasted_iota(jnp.int32, (ROWS, 1), 0)
    return (key_row >= segment) & (key_row <= query)


def group_rows(value, group):
    return jnp.concatenate(
        [value[:, (GROUP * group + n) * HD : (GROUP * group + n + 1) * HD] for n in range(GROUP)],
        axis=0,
    )


def window_rows(kv_s, kv_t, begin):
    return jnp.concatenate(
        [kv_s[:, begin : begin + HD], kv_t[:, begin : begin + HD]], axis=0
    )


def bias_of(first, segment, key_row):
    bias = jnp.where(allowed_of(segment[...], key_row[...], first[0]), 0.0, -1e30).astype(f32)
    return jnp.concatenate([bias] * GROUP, axis=0)


def attend(q, kv_s, kv_t, bias, lse_out=None):
    pieces, held = [], []
    for group in range(KVH):
        keys = window_rows(kv_s, kv_t, group * HD)
        values = window_rows(kv_s, kv_t, KW + group * HD)
        scores = mm_t(group_rows(q, group), keys) + bias
        peak = jnp.max(scores, axis=-1, keepdims=True)
        powers = jnp.exp(scores - peak)
        total = jnp.sum(powers, axis=-1, keepdims=True)
        if lse_out is not None:
            lse_out[:, group : group + 1] = peak + jnp.log(total)
        held.append(powers * (1.0 / total))
        mixed = mm(held[-1].astype(bf16), values)
        for n in range(GROUP):
            pieces.append(mixed[n * ROWS : (n + 1) * ROWS, :])
    return jnp.concatenate(pieces, axis=1).astype(bf16), held


def feed_forward(
    x, mixed, gain_row, w_out, w_in, w_down, copies, middle_out, normed_out, gate_up_out, hidden_out
):
    copies[0].wait()
    middle = x + mm(mixed, w_out[...])
    middle_out[...] = middle
    normed = (middle * inverse_norm(middle) * gain_row[:, 0:D]).astype(bf16)
    normed_out[...] = normed
    copies[1].wait()
    gate_up = mm(normed, w_in[...])
    gate_up_out[...] = gate_up
    gate = gate_up[:, 0:FF]
    hidden = (gate * jax.nn.sigmoid(gate) * gate_up[:, FF:]).astype(bf16)
    hidden_out[...] = hidden
    copies[2].wait()
    return middle + mm(hidden, w_down[...])


def attend_kernel(
    first, x_in, q_in, kv_s, kv_t, segment, key_row, gain_row, w_out_at, w_in_at, w_down_at,
    x_out, mixed_out, lse_out, middle_out, normed_out, gate_up_out, hidden_out,
    w_out, w_in, w_down, sems,
):
    copies = fetch((w_out_at, w_in_at, w_down_at), (w_out, w_in, w_down), sems)
    for copy in copies:
        copy.start()
    q = q_in[...] * FACTOR
    mixed, _ = attend(q, kv_s, kv_t, bias_of(first, segment, key_row), lse_out)
    mixed_out[...] = mixed
    x_out[...] = feed_forward(
        x_in[...].astype(f32), mixed, gain_row, w_out, w_in, w_down, copies,
        middle_out, normed_out, gate_up_out, hidden_out,
    )


def norm_back(values, inverse, gain, grad):
    weighted = grad * gain
    return inverse * weighted - values * inverse**3 * jnp.mean(
        weighted * values, axis=-1, keepdims=True
    )


def feed_back(
    g, middle_in, gate_up, gain_row, w_out, w_in, w_down, waits,
    branch_out, grad_gu_out, attn_out, middle_grad_out, gain_out,
):
    branch = g.astype(bf16)
    branch_out[...] = branch
    for wait in waits[0]:
        wait.wait()
    grad_hidden = mm_t(branch, w_down[...])
    gate = gate_up[:, 0:FF]
    up = gate_up[:, FF:]
    sigma = jax.nn.sigmoid(gate)
    grad_gu_out[:, 0:FF] = (
        grad_hidden * up * sigma * (1.0 + gate * (1.0 - sigma))
    ).astype(bf16)
    grad_gu_out[:, FF:] = (grad_hidden * gate * sigma).astype(bf16)
    for wait in waits[1]:
        wait.wait()
    grad_two = mm_t(grad_gu_out[...], w_in[...])
    middle = middle_in[...]
    inverse = inverse_norm(middle)
    gain_out[...] = jnp.sum(grad_two * middle * inverse, axis=0, keepdims=True)
    grad_middle = g + norm_back(middle, inverse, gain_row[:, 0:D], grad_two)
    middle_grad_out[...] = grad_middle
    attn = grad_middle.astype(bf16)
    attn_out[...] = attn
    for wait in waits[2]:
        wait.wait()
    return mm_t(attn, w_out[...]).astype(bf16)


def attend_back(
    q, kv_s, kv_t, held, grad_mixed, cosine, sine, dq_out, dkv_s, dkv_t, factor=1.0
):
    dq, dk, dv = [], [], []
    for group in range(KVH):
        keys = window_rows(kv_s, kv_t, group * HD)
        values = window_rows(kv_s, kv_t, KW + group * HD)
        query = group_rows(q, group)
        grad = group_rows(grad_mixed, group)
        probs = held[group]
        grad_w = mm_t(grad, values)
        delta = jnp.sum(probs * grad_w, axis=-1, keepdims=True)
        grad_scores = (probs * (grad_w - delta)).astype(bf16)
        part = mm(grad_scores, keys) * FACTOR
        for n in range(GROUP):
            dq.append(part[n * ROWS : (n + 1) * ROWS, :])
        dk.append(mm(query.T, grad_scores) * factor)
        dv.append(mm(grad.T, probs.astype(bf16)))
    dkv = jnp.concatenate(dk + dv, axis=0).T
    dkv_s[...] = dkv[0:WIN_S, :]
    dkv_t[...] = dkv[WIN_S:, :].astype(bf16)
    wide = jnp.concatenate(dq + [jnp.zeros((ROWS, HD), f32)], axis=1)
    dq_out[...] = turn(wide, cosine[...], -sine[...])[:, 0:QW].astype(bf16)


def back_kernel(
    first, g_in, q_in, kv_s, kv_t, segment, key_row, cosine, sine, gain_row, lse, middle_in,
    gate_up_at, w_out_at, w_in_at, w_down_at,
    branch_out, grad_gu_out, attn_out, middle_grad_out, dq_out, dkv_s, dkv_t, gain_out,
    w_out, w_in, w_down, sems, gate_up, gate_sem,
):
    copies = fetch((w_out_at, w_in_at, w_down_at), (w_out, w_in, w_down), sems)
    gate_copy = pltpu.make_async_copy(gate_up_at, gate_up, gate_sem)
    copies[2].start()
    gate_copy.start()
    copies[1].start()
    copies[0].start()
    bias = bias_of(first, segment, key_row)
    q = q_in[...]
    held = []
    for group in range(KVH):
        keys = window_rows(kv_s, kv_t, group * HD)
        scores = mm_t(group_rows(q, group), keys) * FACTOR + bias
        held.append(jnp.exp(scores - lse[:, group : group + 1]))
    grad_mixed = feed_back(
        g_in[...].astype(f32), middle_in, gate_up, gain_row, w_out, w_in, w_down,
        ((copies[2], gate_copy), (copies[1],), (copies[0],)),
        branch_out, grad_gu_out, attn_out, middle_grad_out, gain_out,
    )
    attend_back(q, kv_s, kv_t, held, grad_mixed, cosine, sine, dq_out, dkv_s, dkv_t, FACTOR)


def last_kernel(
    first, x_in, g_in, q_in, kv_s, kv_t, segment, key_row, cosine, sine, gain_row,
    w_out_at, w_in_at, w_down_at,
    x_out, mixed_out, normed_out, hidden_out,
    branch_out, grad_gu_out, attn_out, middle_grad_out, dq_out, dkv_s, dkv_t, gain_out,
    w_out, w_in, w_down, sems, gate_up, middle,
):
    copies = fetch((w_out_at, w_in_at, w_down_at), (w_out, w_in, w_down), sems)
    for copy in copies:
        copy.start()
    q = q_in[...] * FACTOR
    mixed, held = attend(q, kv_s, kv_t, bias_of(first, segment, key_row))
    mixed_out[...] = mixed
    x_out[...] = feed_forward(
        x_in[...].astype(f32), mixed, gain_row, w_out, w_in, w_down, copies,
        middle, normed_out, gate_up, hidden_out,
    ).astype(bf16)
    grad_mixed = feed_back(
        g_in[...].astype(f32), middle, gate_up, gain_row, w_out, w_in, w_down, ((), (), ()),
        branch_out, grad_gu_out, attn_out, middle_grad_out, gain_out,
    )
    attend_back(q, kv_s, kv_t, held, grad_mixed, cosine, sine, dq_out, dkv_s, dkv_t)


def back_heads_kernel(
    core, x_in, dq, own, r8, r6, r4, r2, cosine, sine, gain_row, w_qkv, middle_grad, normed, edge,
    g_out, keep, send, flat, tile, project_out, gain_out,
):
    total = own[...]
    for piece in (r8, r6, r4, r2):
        total = total + piece[...].astype(f32)
    keys = jnp.concatenate([total[:, 0:KW], jnp.zeros((ROWS, HD), f32)], axis=1)
    keys = turn(keys, cosine[...], -sine[...])[:, 0:KW]
    project = jnp.concatenate(
        [dq[...].astype(f32), keys, total[:, KW:]], axis=1
    ).astype(bf16)
    project_out[...] = project
    grad = mm_t(project, w_qkv[...])
    x = x_in[...].astype(f32)
    inverse = inverse_norm(x)
    gain_out[...] = jnp.sum(grad * x * inverse, axis=0, keepdims=True)
    g_out[...] = middle_grad[...] + norm_back(x, inverse, gain_row[:, 0:D], grad)
    pack_first(core, normed, project_out, gain_out, edge, keep, send, flat, tile)


def put_gain(flat, gain, start):
    row = jnp.concatenate([gain[...], jnp.zeros((1, 64), f32)], axis=1)
    first = start // 2
    before = None
    for t in range(5):
        part = row[:, 128 * t : 128 * t + 128]
        place = slice(first + t, first + t + 1)
        if start % 2 == 0:
            flat[place, :] = part
        else:
            now = pltpu.roll(part, 64, 1)
            if before is None:
                flat[place, :] = now
            else:
                flat[place, :] = jnp.where(low_half((1, 128)), before, now)
            before = now


def put_matrix(flat, tile, left, right, start_half, width_half):
    rows, columns = left.shape[1], right.shape[1]
    turned = left[...].T
    for t in range((width_half + 1) // 2):
        wide = min(128, columns - 128 * t)
        tile[t, 0:rows, 0:wide] = mm(turned, right[:, 128 * t : 128 * t + wide])
    for parity in range(2):
        put_rows(
            flat, start_half + parity * width_half, rows // 2, width_half,
            lambda t, parity=parity: tile[t, pl.ds(parity, rows // 2, stride=2), :],
        )


def cut(flat, core, first_plane, planes, skip, keep, send):
    last = lax.broadcasted_iota(jnp.int32, (CHUNK, 128), 0) == CHUNK - 1
    for out, flip in ((keep, 0), (send, 1)):
        def one_owner(k, carry, out=out, flip=flip):
            d = 2 * (first_plane + k) + lax.rem(core[0] + flip, 2)
            base = pl.multiple_of(d * 216 - skip + 8, 8)
            odd = jnp.where(d < DEVICES // 2, base - 1, base + CHUNK - 1)
            value = jnp.where(last, flat[pl.ds(odd, 1), :], flat[pl.ds(base, CHUNK), :])
            out[pl.ds(pl.multiple_of(k * CHUNK, CHUNK), CHUNK), :] = value.astype(bf16)
            return carry

        lax.fori_loop(0, planes, one_owner, 0)


def pack_rest_kernel(
    core, mixed, attn, normed_two, grad_gu, hidden, branch, gain_two, keep, send, edge, flat, tile
):
    skip = 216 * SPLIT
    half = 2 * (7 - skip)
    put_gain(flat, gain_two, HALF_GAIN_TWO + half)
    put_matrix(flat, tile, mixed, attn, HALF_OUT + half, D // 64)
    put_matrix(flat, tile, hidden, branch, HALF_DOWN + half, D // 64)

    turned = normed_two[...].T

    def in_tile(c, carry):
        flat[pl.ds((HALF_IN + half) // 2 + c, D, stride=24), :] = mm(
            turned, grad_gu[:, pl.ds(pl.multiple_of(c * 128, 128), 128)]
        )
        return carry

    lax.fori_loop(0, 24, in_tile, 0)
    cut(flat, core, LOW_PLANES, DEVICES // 2 - LOW_PLANES, skip, keep, send)
    edge[...] = flat[0:EDGE, :]


def pack_first(core, normed, project, gain_one, edge, keep, send, flat, tile):
    skip = 216 * SPLIT
    flat[skip : skip + EDGE, :] = edge[...]
    put_gain(flat, gain_one, HALF_GAIN_ONE + 14)
    put_matrix(flat, tile, normed, project, HALF_QKV + 14, PW // 64)
    cut(flat, core, 0, LOW_PLANES, 0, keep, send)


def hop(value, by):
    pairs = [(i, i + by) for i in range(DEVICES) if 0 <= i + by < DEVICES]
    return lax.ppermute(value, "fsdp", pairs)


def swap(value):
    return lax.ppermute(value, "fsdp", [(i, i ^ 1) for i in range(DEVICES)])


def window_of(value, core, beside=()):
    blocks = [hop(value, by) for by in (8, 6, 4, 2)] + [value]
    same = jnp.concatenate(blocks, axis=0)
    rows = value.shape[0]
    gift = lax.dynamic_slice_in_dim(same, (1 - core) * rows, SAME_CORE * rows, 0)
    if beside:
        gift, _ = lax.optimization_barrier((gift, beside))
    return same, swap(gift)


def give_back(dkv_s, dkv_t, core):
    got = swap(dkv_t).astype(f32)
    blank = jnp.zeros((ROWS, 2 * KW), f32)
    early = jnp.concatenate([got, blank], axis=0)
    late = jnp.concatenate([blank, got], axis=0)
    total = dkv_s + jnp.where(core == 0, late, early)
    pieces = [
        hop(total[at * ROWS : (at + 1) * ROWS].astype(bf16), -by)
        for at, by in enumerate((8, 6, 4, 2))
    ]
    return total[SAME_CORE * ROWS :], pieces


def add_kernel(keep, got, *refs):
    refs[-1][...] = keep[...] + got[...]


def join(keep, got, first_plane, total=None):
    block = (JOIN * CHUNK, 128)
    part = pl.BlockSpec(block, lambda i: (i, 0))
    given = () if total is None else (total,)
    return pl.pallas_call(
        add_kernel,
        grid=(keep.shape[0] // block[0],),
        out_shape=pltpu.HBM((DEVICES // 2 * CHUNK, 128), bf16),
        in_specs=[part, part] + [pl.BlockSpec(memory_space=pl.ANY) for _ in given],
        out_specs=pl.BlockSpec(block, lambda i: (i + first_plane // JOIN, 0)),
        input_output_aliases={2: 0} if given else {},
        compiler_params=pltpu.CompilerParams(vmem_limit_bytes=16 * 1024 * 1024),
        cost_estimate=pl.CostEstimate(
            flops=0, bytes_accessed=6 * keep.size, transcendentals=0
        ),
    )(keep, got, *given)


def to_owners(total):
    groups = [list(range(0, DEVICES, 2)), list(range(1, DEVICES, 2))]
    return lax.all_to_all(
        total.reshape(DEVICES // 2, CHUNK, 128),
        "fsdp", split_axis=0, concat_axis=0, tiled=True, axis_index_groups=groups,
    )


def own_part(pieces, device):
    own = jnp.sum(pieces.astype(f32), axis=0)
    rows = jnp.concatenate([own[CHUNK - 1 :], own], axis=0)
    return lax.dynamic_slice_in_dim(rows.reshape(-1), 9 * device, SHARD, 0)


def tables(positions):
    half = HD // 2
    frequency = rope_base ** (-jnp.arange(half, dtype=f32) / half)
    angles = positions.astype(f32)[:, None] * frequency[None, :]
    return (
        jnp.concatenate([jnp.cos(angles)] * 4, axis=-1),
        jnp.concatenate([jnp.sin(angles)] * 4, axis=-1),
    )


def body(hidden_in, segment_ids, weights_flat, cotangent):
    device = lax.axis_index("fsdp")
    core = lax.rem(device, 2)
    first_row = device * ROWS
    layers = weights_flat.shape[0]
    room = SECTION * 128 - SHARD
    padded = jnp.pad(weights_flat, ((0, 0), (9 * DEVICES, room)))
    sections = lax.dynamic_slice(padded, (0, 9 * (DEVICES - device)), (layers, SECTION * 128))
    gathered = lax.all_gather(sections.reshape(-1), "fsdp", axis=0, tiled=True)
    gathered = gathered.reshape(DEVICES, layers, SECTION, 128)

    x_same, x_sibling = window_of(hidden_in, core)
    window = jnp.concatenate([x_same, x_sibling], axis=0)
    s_same, s_sibling = window_of(segment_ids, core)
    segments = jnp.concatenate([s_same, s_sibling], axis=0)
    order = jnp.arange(ROWS, dtype=jnp.int32)
    same_first = first_row - ROWS * jnp.array([8, 6, 4, 2, 0], jnp.int32)
    sibling_first = first_row - ROWS * jnp.array([7, 5, 3, 1], jnp.int32)
    key_row = jnp.concatenate([same_first, sibling_first])[:, None] + order[None, :]
    key_row = key_row.reshape(-1)
    cosine_all, sine_all = tables(key_row - segments)
    own = SAME_CORE * ROWS
    cosine, sine = cosine_all[own : own + ROWS], sine_all[own : own + ROWS]
    key_row = key_row[None, :]
    segment = segment_ids[:, None]
    first = first_row[None]
    core_in = core[None]

    x = hidden_in
    held = []
    for layer in range(layers):
        w_out, w_in, w_down, gain_two = unpack_rest(gathered, layer)
        if layer == 0:
            w_qkv, gain_one, q, kv_s, kv_t, normed = call(
                heads_zero_kernel,
                [((D, PW), bf16), ((1, 640), f32), ((ROWS, QW), bf16), ((WIN_S, 2 * KW), bf16), ((WIN_T, 2 * KW), bf16),
                 ((ROWS, D), bf16)],
                [window, cosine_all, sine_all, gathered],
                scratch=FIRST_SCRATCH, apart=1, flops=800_000_000, nbytes=6_000_000,
            )
        else:
            w_qkv, gain_one, q, kv, normed = call(
                functools.partial(heads_kernel, layer),
                [((D, PW), bf16), ((1, 640), f32), ((ROWS, QW), bf16), ((ROWS, 2 * KW), bf16), ((ROWS, D), bf16)],
                [x, cosine, sine, gathered],
                scratch=FIRST_SCRATCH, apart=1, flops=150_000_000, nbytes=3_000_000,
            )
            kv_s, kv_t = window_of(kv, core, (w_out,))
        if layer == layers - 1:
            (layer_out, mixed, normed_two, hidden, *last_back) = call(
                last_kernel,
                [((ROWS, D), bf16), ((ROWS, QW), bf16), ((ROWS, D), bf16), ((ROWS, FF), bf16)]
                + [((ROWS, D), bf16), ((ROWS, 2 * FF), bf16), ((ROWS, D), bf16), ((ROWS, D), f32),
                 ((ROWS, QW), bf16), ((WIN_S, 2 * KW), f32), ((WIN_T, 2 * KW), bf16), ((1, D), f32)],
                [first, x, cotangent, q, kv_s, kv_t, segment, key_row, cosine, sine, gain_two,
                 w_out, w_in, w_down],
                scratch=WEIGHT_SCRATCH
                + (pltpu.VMEM((ROWS, 2 * FF), f32), pltpu.VMEM((ROWS, D), f32)),
                smem=1, apart=3, flops=5_000_000_000, nbytes=20_000_000,
            )
            held.append((x, q, kv_s, kv_t, normed, mixed, None, None, normed_two, None, hidden,
                         w_qkv, w_out, w_in, w_down, gain_one, gain_two))
            break
        x_next, mixed, lse, middle, normed_two, gate_up, hidden = call(
            attend_kernel,
            [((ROWS, D), f32), ((ROWS, QW), bf16), ((GROUP * ROWS, KVH), f32), ((ROWS, D), f32),
             ((ROWS, D), bf16), ((ROWS, 2 * FF), f32), ((ROWS, FF), bf16)],
            [first, x, q, kv_s, kv_t, segment, key_row, gain_two, w_out, w_in, w_down],
            scratch=WEIGHT_SCRATCH, smem=1, apart=3, flops=2_000_000_000, nbytes=12_000_000,
        )
        held.append((x, q, kv_s, kv_t, normed, mixed, lse, middle, normed_two, gate_up, hidden,
                     w_qkv, w_out, w_in, w_down, gain_one, gain_two))
        x = x_next

    g = cotangent
    grads = [None] * layers
    for layer in reversed(range(layers)):
        (x, q, kv_s, kv_t, normed, mixed, lse, middle, normed_two, gate_up, hidden,
         w_qkv, w_out, w_in, w_down, gain_one, gain_two) = held[layer]
        if layer == layers - 1:
            branch, grad_gu, attn, middle_grad, dq, dkv_s, dkv_t, grad_two = last_back
        else:
            branch, grad_gu, attn, middle_grad, dq, dkv_s, dkv_t, grad_two = call(
                back_kernel,
                [((ROWS, D), bf16), ((ROWS, 2 * FF), bf16), ((ROWS, D), bf16), ((ROWS, D), f32),
                 ((ROWS, QW), bf16), ((WIN_S, 2 * KW), f32), ((WIN_T, 2 * KW), bf16), ((1, D), f32)],
                [first, g, q, kv_s, kv_t, segment, key_row, cosine, sine, gain_two, lse, middle,
                 gate_up, w_out, w_in, w_down],
                scratch=WEIGHT_SCRATCH
                + (pltpu.VMEM((ROWS, 2 * FF), f32), pltpu.SemaphoreType.DMA),
                smem=1, apart=4, flops=3_000_000_000, nbytes=15_000_000,
            )
        rest_shape = (((DEVICES // 2 - LOW_PLANES) * CHUNK, 128), bf16)
        keep, send, edge = call(
            pack_rest_kernel,
            [rest_shape, rest_shape, ((EDGE, 128), f32)],
            [core_in, mixed, attn, normed_two, grad_gu, hidden, branch, grad_two],
            scratch=[
                pltpu.VMEM((216 * (DEVICES - SPLIT) + 40, 128), f32), pltpu.VMEM((5, FF, 128), f32)
            ],
            smem=1, flops=1_000_000_000, nbytes=25_000_000,
        )
        own_kv, pieces = give_back(dkv_s, dkv_t, core)
        send, pieces = lax.optimization_barrier((send, pieces))
        keep_rest, got_rest = keep, swap(send)
        if layer + 1 < layers:
            own_kv, grads[layer + 1] = lax.optimization_barrier((own_kv, grads[layer + 1]))
        low_shape = ((LOW_PLANES * CHUNK, 128), bf16)
        g, keep, send = call(
            back_heads_kernel,
            [((ROWS, D), f32), low_shape, low_shape],
            [core_in, x, dq, own_kv, *pieces, cosine, sine, gain_one, w_qkv, middle_grad, normed,
             edge],
            scratch=[
                pltpu.VMEM((216 * SPLIT + EDGE + 8, 128), f32), pltpu.VMEM((8, D, 128), f32),
                pltpu.VMEM((ROWS, PW), bf16), pltpu.VMEM((1, D), f32),
            ],
            smem=1, flops=350_000_000, nbytes=10_000_000,
        )
        total = join(keep, swap(send), 0, join(keep_rest, got_rest, LOW_PLANES))
        if layer > 0:
            g, total = lax.optimization_barrier((g, total))
        grads[layer] = to_owners(total)
    return (layer_out, g, jnp.stack([own_part(pieces, device) for pieces in grads]))


def solution(mesh):
    in_specs = (P("fsdp", None), P("fsdp"), P(None, "fsdp"), P("fsdp", None))
    out_specs = (P("fsdp", None), P("fsdp", None), P(None, "fsdp"))
    return jax.shard_map(body, mesh=mesh, in_specs=in_specs, out_specs=out_specs, check_vma=False)
```
